128 devices in a mesh: row: 16 (over z, x_hi, core), col: 8 (over x_lo, y).
Axes of the slice: x: 4 (x_hi: 2, x_lo: 2; x = x_hi * 2 + x_lo), y: 4, z: 4, core: 2. Of those that a mesh axis runs over, the one named last changes fastest.
Arguments:
- layer_input: bfloat16 [4096, 1024], P('row', 'col'), may hold values from -6 to 6
- query_weight: bfloat16 [2, 1024, 1024], P(None, 'row', 'col'), may hold values from -0.1875 to 0.1875
- key_weight: bfloat16 [2, 1024, 1024], P(None, 'row', 'col'), may hold values from -0.1875 to 0.1875
- value_weight: bfloat16 [2, 1024, 1024], P(None, 'row', 'col'), may hold values from -0.1875 to 0.1875
- proj_weight: bfloat16 [2, 1024, 1024], P(None, 'row', 'col'), may hold values from -1.5 to 1.5
- up_weight: bfloat16 [2, 1024, 4096], P(None, 'row', 'col'), may hold values from -0.1875 to 0.1875
- down_weight: bfloat16 [2, 4096, 1024], P(None, 'row', 'col'), may hold values from -0.09375 to 0.09375
- query_shift: bfloat16 [2, 1024], P(None, 'col'), may hold values from -1.75 to 1.75
- value_shift: bfloat16 [2, 1024], P(None, 'col'), may hold values from -0.125 to 0.125
- proj_shift: bfloat16 [2, 1024], P(None, 'col'), may hold values from -1.75 to 1.75
- up_shift: bfloat16 [2, 4096], P(None, 'col'), may hold values from -1.75 to 1.75
- down_shift: bfloat16 [2, 1024], P(None, 'col'), may hold values from -1.75 to 1.75
- first_gain: bfloat16 [2, 1024], P(None, 'col'), may hold values from 0.5 to 1.5
- first_shift: bfloat16 [2, 1024], P(None, 'col'), may hold values from -1.75 to 1.75
- second_gain: bfloat16 [2, 1024], P(None, 'col'), may hold values from 0.5 to 1.5
- second_shift: bfloat16 [2, 1024], P(None, 'col'), may hold values from -1.75 to 1.75
- segment_ids: int32 [4096], replicated, may hold values from 0 to 5, as said below
- cotangent: bfloat16 [4096, 1024], P('row', 'col'), may hold values from -6 to 6
Outputs:
- activations: bfloat16 [4096, 1024], P('row', 'col')
- input_grad: float32 [4096, 1024], P('row', 'col')
- query_grads: float32 [2, 1024, 1024], P(None, 'row', 'col')
- key_grads: float32 [2, 1024, 1024], P(None, 'row', 'col')
- value_grads: float32 [2, 1024, 1024], P(None, 'row', 'col')
- proj_grads: float32 [2, 1024, 1024], P(None, 'row', 'col')
- up_grads: float32 [2, 1024, 4096], P(None, 'row', 'col')
- down_grads: float32 [2, 4096, 1024], P(None, 'row', 'col')
- query_shift_grads: float32 [2, 1024], P(None, 'col')
- value_shift_grads: float32 [2, 1024], P(None, 'col')
- proj_shift_grads: float32 [2, 1024], P(None, 'col')
- up_shift_grads: float32 [2, 4096], P(None, 'col')
- down_shift_grads: float32 [2, 1024], P(None, 'col')
- first_gain_grads: float32 [2, 1024], P(None, 'col')
- first_shift_grads: float32 [2, 1024], P(None, 'col')
- second_gain_grads: float32 [2, 1024], P(None, 'col')
- second_shift_grads: float32 [2, 1024], P(None, 'col')
The draws below stay inside these ranges and needn't reach their ends.
Inputs may be any that keep to these rules, and one draw needn't show every extreme that they name: `segment_ids`: A token's document number depends only on its place within its block of 256 tokens (its index modulo 256), so every document has equally many tokens in each block; within a block the numbers never fall; document 0 holds the first 64 places of every block, and no document holds more places of a block.
All inputs are finite; a program needn't handle non-finite values.
Results may differ from the reference program's by a relative error of at most 0.035.
Values may be sent and summed in bfloat16 or wider, within the bound.
A program may use at most 128 MiB of HBM per device.

```python
from functools import partial
import jax
import jax.numpy as jnp
from jax import lax

D = 1024
HEADS = 16
FF = 4096
TOK_DEV = 256
LAYERS = 2
HEAD_DIM = 64
TOKENS = 4096


def draw_segment_ids(key, part):
    key = jax.random.fold_in(key, 7)
    longest = TOK_DEV // 4
    jitter = jax.random.randint(key, (4,), 0, max(longest // 4, 1) + 1)
    counter = jnp.arange(1, 5, dtype=jnp.int32)
    cuts = longest + counter * 3 * longest // 5 + jitter
    slots = jnp.arange(TOKENS, dtype=jnp.int32) % TOK_DEV
    segment = (slots >= longest).astype(jnp.int32)
    segment = segment + jnp.sum((slots[:, None] >= cuts[None, :]).astype(jnp.int32), axis=1)
    return segment.astype(jnp.int32)


def levels(rng, extent, cuts, low, top_value):
    gain, own = 1.0, jax.random.fold_in(rng, 6)
    for position, shards_of in cuts:
        steps = jnp.exp(jax.random.uniform(jax.random.fold_in(own, position), (shards_of,), jnp.float32, low / len(cuts), top_value / len(cuts)))
        gain = gain * jnp.repeat(steps, extent[position] // shards_of).reshape([-1 if axis == position else 1 for axis in range(len(extent))])
    return gain


def gaussian(own_key, shape, spread, reach, cuts=(), held_as=jnp.bfloat16):
    entries = spread * jax.random.normal(own_key, shape, jnp.float32)
    if cuts:
        entries = entries * levels(own_key, shape, cuts, -0.22, 0.18)
    return jnp.clip(entries, -reach, reach).astype(held_as)


def setup_inputs(seed: int = 0) -> dict:
    keys = jax.random.split(jax.random.key(seed), 19)
    return {
        "layer_input": gaussian(keys[0], (TOKENS, D), 1.0, 6.0, ((0, 16), (1, 8))),
        "query_weight": gaussian(keys[1], (LAYERS, D, D), D ** -0.5, 0.1875, ((1, 16), (2, 8))),
        "key_weight": gaussian(keys[2], (LAYERS, D, D), D ** -0.5, 0.1875, ((1, 16), (2, 8))),
        "value_weight": gaussian(keys[3], (LAYERS, D, D), D ** -0.5, 0.1875, ((1, 16), (2, 8))),
        "proj_weight": gaussian(keys[4], (LAYERS, D, D), (max(D * 64 // TOKENS, 1)) ** -0.5, 1.5, ((1, 16), (2, 8))),
        "up_weight": gaussian(keys[5], (LAYERS, D, FF), D ** -0.5, 0.1875, ((1, 16), (2, 8))),
        "down_weight": gaussian(keys[6], (LAYERS, FF, D), FF ** -0.5, 0.09375, ((1, 16), (2, 8))),
        "query_shift": gaussian(keys[7], (LAYERS, D), 0.3, 1.75, ((1, 8),)),
        "value_shift": gaussian(keys[8], (LAYERS, D), 0.02, 0.125, ((1, 8),)),
        "proj_shift": gaussian(keys[9], (LAYERS, D), 0.3, 1.75, ((1, 8),)),
        "up_shift": gaussian(keys[10], (LAYERS, FF), 0.3, 1.75, ((1, 8),)),
        "down_shift": gaussian(keys[11], (LAYERS, D), 0.3, 1.75, ((1, 8),)),
        "first_gain": jnp.clip(1.0 + 0.1 * jax.random.normal(keys[12], (LAYERS, D), jnp.float32), 0.5, 1.5).astype(jnp.bfloat16),
        "first_shift": gaussian(keys[13], (LAYERS, D), 0.3, 1.75, ((1, 8),)),
        "second_gain": jnp.clip(1.0 + 0.1 * jax.random.normal(keys[14], (LAYERS, D), jnp.float32), 0.5, 1.5).astype(jnp.bfloat16),
        "second_shift": gaussian(keys[15], (LAYERS, D), 0.3, 1.75, ((1, 8),)),
        "segment_ids": draw_segment_ids(jax.random.fold_in(keys[18], 71), 0),
        "cotangent": gaussian(keys[17], (TOKENS, D), 1.0, 6.0, ((0, 16), (1, 8))),
    }


@jax.custom_vjp
def low(v):
    return lax.optimization_barrier(v.astype(jnp.bfloat16)).astype(jnp.float32)

@jax.custom_vjp
def low_back(v):
    return v

def low_keep(v):
    return (low(v), None)

def low_pass(kept, grad):
    return (grad,)

def back_keep(v):
    return (v, None)

def back_low(kept, grad):
    return (low(grad),)
low.defvjp(low_keep, low_pass)
low_back.defvjp(back_keep, back_low)

def product(left_op, right_op):
    return jnp.dot(left_op, right_op, precision=lax.Precision.HIGHEST, preferred_element_type=jnp.float32)

def normalize(summed, gain_vec, shift_vec):
    average = lax.optimization_barrier(jnp.mean(summed, axis=-1, keepdims=True))
    variance = lax.optimization_barrier(jnp.mean(summed * summed, axis=-1, keepdims=True)) - average * average
    return (summed - average) * lax.rsqrt(variance + 1e-12) * gain_vec + shift_vec

def one_head(same_doc, operands):
    queries, key_rows, value_rows = operands
    scores = low_back(product(queries, key_rows.T) * HEAD_DIM ** (-0.5))
    masked = jnp.where(same_doc, scores, -1000000000.0)
    highest = lax.optimization_barrier(jnp.max(masked, axis=-1, keepdims=True))
    log_total = highest + jnp.log(lax.optimization_barrier(jnp.sum(jnp.exp(masked - highest), axis=-1, keepdims=True)))
    attn_probs = low(jnp.exp(masked - log_total))
    return product(attn_probs, value_rows)

def split_heads(matrix):
    return matrix.reshape(TOKENS, HEADS, HEAD_DIM).transpose(1, 0, 2)

def one_layer(hidden, params, same_doc):
    query_w, key_w, value_w, proj_w, up_w, down_w, query_b, value_b, proj_b, up_b, down_b, gain_one, shift_one, gain_two, shift_two = params
    inputs = low(hidden)
    queries = low(low_back(product(inputs, query_w) + query_b))
    key_rows = low(low_back(product(inputs, key_w)))
    value_rows = low(low_back(product(inputs, value_w) + value_b))
    heads_out = lax.map(jax.checkpoint(partial(one_head, same_doc)), (split_heads(queries), split_heads(key_rows), split_heads(value_rows)))
    attended = low(low_back(heads_out.transpose(1, 0, 2).reshape(TOKENS, D)))
    projected = low_back(product(attended, proj_w) + proj_b)
    first_out = normalize(hidden + projected, gain_one, shift_one)
    up_pre = low_back(product(low(first_out), up_w) + up_b)
    gated_act = low(jax.nn.gelu(up_pre, approximate=False))
    down_out = low_back(product(gated_act, down_w) + down_b)
    return normalize(first_out + down_out, gain_two, shift_two)

def reference(layer_input, query_weight, key_weight, value_weight, proj_weight, up_weight, down_weight, query_shift, value_shift, proj_shift, up_shift, down_shift, first_gain, first_shift, second_gain, second_shift, segment_ids, cotangent):
    same_doc = segment_ids[:, None] == segment_ids[None, :]
    floats = tuple((array.astype(jnp.float32) for array in (query_weight, key_weight, value_weight, proj_weight, up_weight, down_weight, query_shift, value_shift, proj_shift, up_shift, down_shift, first_gain, first_shift, second_gain, second_shift)))

    def forward(start_act, *params):
        hidden = start_act
        for layer_index in range(LAYERS):
            hidden = one_layer(hidden, tuple((param[layer_index] for param in params)), same_doc)
        return hidden
    result, pullback = jax.vjp(forward, layer_input.astype(jnp.float32), *floats)
    gradients = pullback(cotangent.astype(jnp.float32))
    return (result.astype(jnp.bfloat16), gradients[0], gradients[1], gradients[2], gradients[3], gradients[4], gradients[5], gradients[6], gradients[7], gradients[8], gradients[9], gradients[10], gradients[11], gradients[12], gradients[13], gradients[14], gradients[15])
```

```python
import functools
from types import SimpleNamespace

import jax
import jax.numpy as jnp
from jax import lax
from jax.experimental import pallas as pl
from jax.experimental.pallas import tpu as pltpu
from jax.sharding import PartitionSpec as P

MESH = pl.DeviceIdType.MESH
LAYERS = 2
HEAD_DIM = 64
LANES = 128
F32 = jnp.float32
BF16 = jnp.bfloat16
PAIRS = ((0, 0), (1, 1), (1, 2), (2, 1), (2, 2), (2, 3), (3, 2), (3, 3))
KEYS_OF = {i: [(n, j) for n, (a, j) in enumerate(PAIRS) if a == i] for i in range(4)}
QUERIES_OF = {j: [(n, i) for n, (i, b) in enumerate(PAIRS) if b == j] for j in range(4)}

PROJ_B, DOWN_B, GAIN1, SHIFT1, GAIN2, SHIFT2 = range(6)
VEC_ROWS = 8


def dot(a, b):
    return jnp.dot(a, b, preferred_element_type=F32)


def dot_nt(a, b):
    return lax.dot_general(a, b, (((1,), (1,)), ((), ())), preferred_element_type=F32)


def dot_tn(a, b):
    return lax.dot_general(a, b, (((0,), (0,)), ((), ())), preferred_element_type=F32)


class Sizes:
    def __init__(self, nr, nc, tok, d, ff):
        self.nr, self.nc, self.tok, self.d, self.ff = nr, nc, tok, d, ff
        self.t = tok // nc
        self.dc, self.fc = d // nc, ff // nc
        self.dr, self.fr = d // nr, ff // nr
        self.hr = nr // nc
        self.qc = tok // 4


def scratch_of(s):
    L = LAYERS
    v = {}
    v["xf"] = ((L, s.tok, s.d), BF16)
    v["x1"] = ((L, s.tok, s.d), BF16)
    v["dff"] = ((L, s.tok, s.d), BF16)
    v["drf"] = ((L, s.tok, s.d), BF16)
    v["part"] = ((s.tok, s.d), BF16)
    v["got"] = ((s.nc, s.t, s.d), BF16)
    v["got_in"] = ((s.nc, s.tok, s.dc), BF16)
    v["act_out"] = ((s.t, s.d), BF16)
    v["act_in"] = ((s.tok, s.dc), BF16)
    v["cot"] = ((s.t, s.d), BF16)
    v["pv"] = ((L * VEC_ROWS, s.d), BF16)
    v["kv"] = ((L, s.nr, s.tok, 2 * s.dc), BF16)
    v["dkv"] = ((s.nr, s.tok, 2 * s.dc), BF16)
    v["dkv_in"] = ((L, s.nr, s.tok, 2 * s.dc), BF16)
    v["probs"] = ((L, len(PAIRS), 2 * s.qc, s.nr * s.qc), BF16)
    v["q2"] = ((L, 4, 2 * s.qc, s.dc), BF16)
    v["do2"] = ((4, 2 * s.qc, s.dc), BF16)
    v["delta"] = ((4, 2 * s.qc, 1), F32)
    v["dq2"] = ((4, 2 * s.qc, s.dc), F32)
    v["att"] = ((L, s.tok, s.dc), F32)
    v["gate"] = ((L, s.tok, s.fc), BF16)
    v["slope"] = ((L, s.tok, s.fc), F32)
    v["de"] = ((s.tok, s.fc), BF16)
    v["n1"] = ((L, s.t, s.d), F32)
    v["n2"] = ((L, s.t, s.d), F32)
    v["r1"] = ((L, s.t, 1), F32)
    v["r2"] = ((L, s.t, 1), F32)
    v["carry"] = ((s.t, s.d), F32)
    v["dqkv"] = ((s.tok, 3 * s.dc), BF16)
    v["wqkv"] = ((L, s.d, 3 * s.dc), BF16)
    v["wproj"] = ((L, s.dc, s.d), BF16)
    v["wup"] = ((L, s.d, s.fc), BF16)
    v["wdown"] = ((L, s.fc, s.d), BF16)
    v["gqkv"] = ((s.d, 3 * s.dc), BF16)
    v["gproj"] = ((s.dc, s.d), BF16)
    v["gup"] = ((s.d, s.fc), BF16)
    v["gdown"] = ((s.fc, s.d), BF16)
    v["gqkv_in"] = ((L, s.nr, s.dr, 3 * s.dc), BF16)
    v["gproj_in"] = ((L, s.nr, s.dr, s.dc), BF16)
    v["gup_in"] = ((L, s.nr, s.dr, s.fc), BF16)
    v["gdown_in"] = ((L, s.nr, s.fr, s.dc), BF16)
    v["vec"] = ((L * VEC_ROWS, s.d), F32)
    v["vec_in"] = ((s.nc, L * VEC_ROWS, s.dc), F32)
    v["own"] = ((L * 2 * VEC_ROWS, s.dc), F32)
    v["own_in"] = ((s.nr, L * 2 * VEC_ROWS, s.dc), F32)
    return v


INPUTS = ("x", "cotan", "wq", "wp", "wu", "wd", "pvec", "qkvb", "upb", "segq", "segk")
OUTPUTS = ("o_act", "o_in", "o_qkv", "o_proj", "o_up", "o_down", "o_vec")
PHASES = (
    ["x", "cotan", "pvec", "act", "gin", "vec", "own"]
    + [f"{n}{l}" for l in range(LAYERS) for n in
       ("wq", "wp", "wu", "wd", "kv", "pr", "n1", "fr", "h", "df", "dn", "dr", "dkv", "dx", "gq", "gp", "gu", "gd")]
)
PHASE = {name: index for index, name in enumerate(PHASES)}


def kernel(s, *refs):
    names = INPUTS + OUTPUTS + tuple(scratch_of(s)) + ("send", "recv")
    m = SimpleNamespace(**dict(zip(names, refs)))
    L = LAYERS
    r, c = lax.axis_index("row"), lax.axis_index("col")
    home = lax.div(r, s.hr)
    part_of_home = lax.rem(r, s.hr)
    at_home = home == c

    def remote(src, dst, phase, row, col):
        return pltpu.make_async_remote_copy(
            src_ref=src, dst_ref=dst, send_sem=m.send.at[PHASE[phase]], recv_sem=m.recv.at[PHASE[phase]],
            device_id=(row, col), device_id_type=MESH)

    def wait(sems, phase, ref):
        pltpu.make_async_copy(ref, ref, sems.at[PHASE[phase]]).wait()

    def each_col(fn):
        def step(k, carry):
            fn(lax.rem(c + k, s.nc))
            return carry
        lax.fori_loop(1, s.nc, step, 0)

    def each_row(fn):
        def step(k, carry):
            fn(lax.rem(r + k, s.nr))
            return carry
        lax.fori_loop(1, s.nr, step, 0)

    def each_row_of_home(fn):
        def step(k, carry):
            row = lax.rem(r + k, s.nr)

            @pl.when(jnp.logical_or(k > 0, jnp.logical_not(at_home)))
            def _():
                fn(row)
            return carry
        lax.fori_loop(0, s.nr, step, 0)

    def each_owner(fn):
        def step(k, carry):
            rr, cc = lax.div(k, s.nc), lax.rem(k, s.nc)
            row = c * s.hr + rr

            @pl.when(jnp.logical_or(row != r, cc != c))
            def _():
                fn(rr, row, cc)
            return carry
        lax.fori_loop(0, s.nr, step, 0)

    def wait_home(sems, phase, ref):
        @pl.when(at_home)
        def _():
            wait(sems, phase, ref.at[pl.ds(0, s.nr - 1)])

        @pl.when(jnp.logical_not(at_home))
        def _():
            wait(sems, phase, ref)

    def rows(i, n):
        return pl.ds(pl.multiple_of(i * n, n), n)

    barrier = pltpu.get_barrier_semaphore()

    def greet(row, col):
        pl.semaphore_signal(barrier, inc=1, device_id=(row, col), device_id_type=MESH)

    each_col(lambda cc: greet(r, cc))
    each_row(lambda rr: greet(rr, c))
    each_row_of_home(lambda rr: greet(rr, home))
    each_owner(lambda rr, row, cc: greet(row, cc))

    m.xf[0, :, rows(c, s.dc)] = m.x[...]
    m.cot[:, rows(c, s.dc)] = m.cotan[rows(c, s.t), :]
    m.pv[:, rows(c, s.dc)] = m.pvec[...]
    for l in range(L):
        m.wqkv[l, rows(r, s.dr), :] = m.wq[l]
        m.wup[l, rows(r, s.dr), :] = m.wu[l]

        @pl.when(at_home)
        def _():
            m.wproj[l, rows(part_of_home, s.dr), rows(c, s.dc)] = m.wp[l]
            m.wdown[l, rows(part_of_home, s.fr), rows(c, s.dc)] = m.wd[l]
    m.vec[...] = jnp.zeros(m.vec.shape, F32)
    m.own[...] = jnp.zeros(m.own.shape, F32)

    pl.semaphore_wait(barrier, s.nc - 1 + s.nr - 1 + 2 * s.nr - 2 * at_home.astype(jnp.int32))

    each_row(lambda rr: remote(m.wq.at[0], m.wqkv.at[0, rows(r, s.dr)], "wq0", rr, c).start())
    each_col(lambda cc: remote(m.x, m.xf.at[0, :, rows(c, s.dc)], "x", r, cc).start())
    each_col(lambda cc: remote(m.pvec, m.pv.at[:, rows(c, s.dc)], "pvec", r, cc).start())
    each_col(lambda cc: remote(m.cotan.at[rows(cc, s.t)], m.cot.at[:, rows(c, s.dc)], "cotan", r, cc).start())
    for l in range(L):
        if l:
            each_row(lambda rr: remote(m.wq.at[l], m.wqkv.at[l, rows(r, s.dr)], f"wq{l}", rr, c).start())
        each_row_of_home(lambda rr: remote(
            m.wp.at[l], m.wproj.at[l, rows(part_of_home, s.dr), rows(c, s.dc)], f"wp{l}", rr, home).start())
        each_row(lambda rr: remote(m.wu.at[l], m.wup.at[l, rows(r, s.dr)], f"wu{l}", rr, c).start())
        each_row_of_home(lambda rr: remote(
            m.wd.at[l], m.wdown.at[l, rows(part_of_home, s.fr), rows(c, s.dc)], f"wd{l}", rr, home).start())

    few = s.nc - 1
    wait(m.recv, "x", m.xf.at[0, :, pl.ds(0, few * s.dc)])
    wait(m.recv, "pvec", m.pv.at[:, pl.ds(0, few * s.dc)])

    def vector(l, which):
        return m.pv[l * VEC_ROWS + which : l * VEC_ROWS + which + 1, :].astype(F32)

    def share(buf, value, phase):
        buf[rows(c, s.t), :] = value
        each_col(lambda cc: remote(buf.at[rows(c, s.t)], buf.at[rows(c, s.t)], phase, r, cc).start())

    def shared(buf, phase):
        for sems in (m.recv, m.send):
            wait(sems, phase, buf.at[pl.ds(0, few * s.t)])

    def scatter(value, phase):
        m.part[...] = value.astype(BF16)
        each_col(lambda cc: remote(m.part.at[rows(cc, s.t)], m.got.at[c], phase, r, cc).start())
        m.got[c] = m.part[rows(c, s.t), :]

    def scattered(phase):
        for sems in (m.recv, m.send):
            wait(sems, phase, m.got.at[pl.ds(0, few)])
        total = m.got[0].astype(F32)
        for k in range(1, s.nc):
            total = total + m.got[k].astype(F32)
        return total

    def norm(u, l, gain, shift, n_ref, r_ref):
        mean = jnp.sum(u, axis=1, keepdims=True) / s.d
        var = jnp.sum(u * u, axis=1, keepdims=True) / s.d - mean * mean
        inv = lax.rsqrt(var + 1e-12)
        n = (u - mean) * inv
        n_ref[l] = n
        r_ref[l] = inv
        return n * vector(l, gain) + vector(l, shift)

    def norm_back(g, l, gain, shift, n_ref, r_ref):
        n = n_ref[l]
        w = g * vector(l, gain)
        first = jnp.sum(w, axis=1, keepdims=True) / s.d
        second = jnp.sum(w * n, axis=1, keepdims=True) / s.d
        at = l * VEC_ROWS
        m.vec[at + gain : at + gain + 1, :] = jnp.sum(g * n, axis=0, keepdims=True)
        m.vec[at + shift : at + shift + 1, :] = jnp.sum(g, axis=0, keepdims=True)
        return r_ref[l] * (w - first - n * second)

    low_lanes = lax.broadcasted_iota(jnp.int32, (s.qc, s.dc), 1) < HEAD_DIM

    def two_heads(block):
        block = block.astype(F32)
        return jnp.concatenate([jnp.where(low_lanes, block, 0.0), jnp.where(low_lanes, 0.0, block)], axis=0)

    def one_block(pair):
        return jnp.where(low_lanes, pair[: s.qc], pair[s.qc :])

    def keys(l, j, value):
        lanes = pl.ds(s.dc if value else 0, s.dc)
        return m.kv[l, :, pl.ds(j * s.qc, s.qc), lanes].reshape(s.nr * s.qc, s.dc)

    hidden = m.xf[0, rows(c, s.t), :].astype(F32)
    for l in range(L):
        wait(m.recv, f"wq{l}", m.wqkv.at[l, pl.ds(0, (s.nr - 1) * s.dr)])
        qkv = dot(m.xf[l], m.wqkv[l]) + m.qkvb[l : l + 1, :]
        m.kv[l, r] = qkv[:, s.dc :].astype(BF16)
        each_row(lambda rr: remote(m.kv.at[l, r], m.kv.at[l, r], f"kv{l}", rr, c).start())
        for i in range(4):
            block = qkv[i * s.qc : (i + 1) * s.qc, : s.dc].astype(BF16)
            m.q2[l, i] = (two_heads(block) * HEAD_DIM ** (-0.5)).astype(BF16)
        m.carry[...] = hidden
        wait(m.recv, f"kv{l}", m.kv.at[l, pl.ds(0, s.nr - 1)])
        wait(m.send, f"kv{l}", m.kv.at[l, pl.ds(0, s.nr - 1)])
        for i in range(4):
            queries = m.q2[l, i]
            ids = m.segq[i]
            scores = []
            for _, j in KEYS_OF[i]:
                raw = dot_nt(queries, keys(l, j, False))
                scores.append(jnp.where(ids == m.segk[j : j + 1, :], raw, -1e9))
            top = functools.reduce(jnp.maximum, [jnp.max(x, axis=1, keepdims=True) for x in scores])
            raised = [jnp.exp(x - top) for x in scores]
            inverse = 1.0 / sum(jnp.sum(x, axis=1, keepdims=True) for x in raised)
            out = jnp.zeros((2 * s.qc, s.dc), F32)
            for (n, j), x in zip(KEYS_OF[i], raised):
                prob = (x * inverse).astype(BF16)
                m.probs[l, n] = prob
                out = out + dot(prob, keys(l, j, True))
            m.att[l, i * s.qc : (i + 1) * s.qc, :] = one_block(out)
        wait_home(m.recv, f"wp{l}", m.gproj_in.at[l])
        scatter(dot(m.att[l].astype(BF16), m.wproj[l]), f"pr{l}")
        u = scattered(f"pr{l}") + vector(l, PROJ_B) + m.carry[...]
        first_out = norm(u, l, GAIN1, SHIFT1, m.n1, m.r1)
        share(m.x1.at[l], first_out.astype(BF16), f"n1{l}")
        m.carry[...] = first_out
        wait(m.recv, f"wu{l}", m.wup.at[l, pl.ds(0, (s.nr - 1) * s.dr)])
        shared(m.x1.at[l], f"n1{l}")
        pre = dot(m.x1[l], m.wup[l]) + m.upb[l : l + 1, :]
        cdf = 0.5 * (1.0 + lax.erf(pre * 0.5**0.5))
        m.gate[l] = (pre * cdf).astype(BF16)
        m.slope[l] = cdf + pre * (jnp.exp(-0.5 * pre * pre) * 0.3989422804014327)
        wait_home(m.recv, f"wd{l}", m.gdown_in.at[l])
        scatter(dot(m.gate[l], m.wdown[l]), f"fr{l}")
        u = scattered(f"fr{l}") + vector(l, DOWN_B) + m.carry[...]
        hidden = norm(u, l, GAIN2, SHIFT2, m.n2, m.r2)
        if l + 1 < L:
            share(m.xf.at[l + 1], hidden.astype(BF16), f"h{l}")
            shared(m.xf.at[l + 1], f"h{l}")

    m.act_out[...] = hidden.astype(BF16)
    each_col(lambda cc: remote(m.act_out.at[:, rows(cc, s.dc)], m.act_in.at[rows(c, s.t)], "act", r, cc).start())
    m.act_in[rows(c, s.t), :] = m.act_out[:, rows(c, s.dc)]

    wait(m.recv, "cotan", m.cot.at[:, pl.ds(0, few * s.dc)])
    grad = m.cot[...].astype(F32)
    for l in reversed(range(L)):
        at = l * VEC_ROWS
        own = l * 2 * VEC_ROWS
        dz = norm_back(grad, l, GAIN2, SHIFT2, m.n2, m.r2)
        m.carry[...] = dz
        low = dz.astype(BF16)
        share(m.dff.at[l], low, f"df{l}")
        m.vec[at + DOWN_B : at + DOWN_B + 1, :] = jnp.sum(low.astype(F32), axis=0, keepdims=True)
        shared(m.dff.at[l], f"df{l}")
        de = (dot_nt(m.dff[l], m.wdown[l]) * m.slope[l]).astype(BF16)
        m.de[...] = de
        scatter(dot_nt(de, m.wup[l]), f"dn{l}")
        sums = jnp.sum(de.astype(F32), axis=0, keepdims=True)
        for k in range(s.fc // LANES):
            m.own[own + k : own + k + 1, :] = sums[:, k * LANES : (k + 1) * LANES]
        if l + 1 < L:
            wait_home(m.send, f"gd{l + 1}", m.gdown_in.at[l])
            wait(m.send, f"gu{l + 1}", m.gup_in.at[l, pl.ds(0, s.nr - 1)])
        m.gdown[...] = dot_tn(m.gate[l], m.dff[l]).astype(BF16)
        each_owner(lambda rr, row, cc: remote(
            m.gdown.at[rows(rr, s.fr), rows(cc, s.dc)], m.gdown_in.at[l, r], f"gd{l}", row, cc).start())

        @pl.when(at_home)
        def _():
            m.gdown_in[l, r] = m.gdown[rows(part_of_home, s.fr), rows(c, s.dc)]
        m.gup[...] = dot_tn(m.x1[l], m.de[...]).astype(BF16)
        each_row(lambda rr: remote(m.gup.at[rows(rr, s.dr)], m.gup_in.at[l, r], f"gu{l}", rr, c).start())
        m.gup_in[l, r] = m.gup[rows(r, s.dr), :]
        grad = scattered(f"dn{l}") + m.carry[...]
        du = norm_back(grad, l, GAIN1, SHIFT1, m.n1, m.r1)
        m.carry[...] = du
        low = du.astype(BF16)
        share(m.drf.at[l], low, f"dr{l}")
        m.vec[at + PROJ_B : at + PROJ_B + 1, :] = jnp.sum(low.astype(F32), axis=0, keepdims=True)
        shared(m.drf.at[l], f"dr{l}")
        dout = dot_nt(m.drf[l], m.wproj[l]).astype(BF16)
        for i in range(4):
            block = two_heads(dout[i * s.qc : (i + 1) * s.qc, :])
            kept = m.att[l, i * s.qc : (i + 1) * s.qc, :]
            m.do2[i] = block.astype(BF16)
            m.delta[i] = jnp.sum(block * jnp.concatenate([kept, kept], axis=0), axis=1, keepdims=True)
            m.dq2[i] = jnp.zeros((2 * s.qc, s.dc), F32)
        if l + 1 < L:
            wait(m.send, f"dkv{l + 1}", m.dkv.at[pl.ds(0, s.nr - 1)])
        for j in range(4):
            key_grad = jnp.zeros((s.nr * s.qc, s.dc), F32)
            value_grad = jnp.zeros((s.nr * s.qc, s.dc), F32)
            for n, i in QUERIES_OF[j]:
                prob = m.probs[l, n]
                prob_grad = dot_nt(m.do2[i], keys(l, j, True))
                score_grad = (prob.astype(F32) * (prob_grad - m.delta[i])).astype(BF16)
                m.dq2[i] += dot(score_grad, keys(l, j, False))
                key_grad = key_grad + dot_tn(score_grad, m.q2[l, i])
                value_grad = value_grad + dot_tn(prob, m.do2[i])
            shape = (s.nr, s.qc, s.dc)
            m.dkv[:, pl.ds(j * s.qc, s.qc), pl.ds(0, s.dc)] = key_grad.astype(BF16).reshape(shape)
            m.dkv[:, pl.ds(j * s.qc, s.qc), pl.ds(s.dc, s.dc)] = value_grad.astype(BF16).reshape(shape)
        each_row(lambda rr: remote(m.dkv.at[rr], m.dkv_in.at[l, r], f"dkv{l}", rr, c).start())
        m.dkv_in[l, r] = m.dkv[r]
        for i in range(4):
            m.dqkv[i * s.qc : (i + 1) * s.qc, : s.dc] = (one_block(m.dq2[i]) * HEAD_DIM ** (-0.5)).astype(BF16)
        if l + 1 < L:
            wait_home(m.send, f"gp{l + 1}", m.gproj_in.at[l])
            wait(m.send, f"gq{l + 1}", m.gqkv_in.at[l, pl.ds(0, s.nr - 1)])
        m.gproj[...] = dot_tn(m.att[l].astype(BF16), m.drf[l]).astype(BF16)
        each_owner(lambda rr, row, cc: remote(
            m.gproj.at[rows(rr, s.dr), rows(cc, s.dc)], m.gproj_in.at[l, r], f"gp{l}", row, cc).start())

        @pl.when(at_home)
        def _():
            m.gproj_in[l, r] = m.gproj[rows(part_of_home, s.dr), rows(c, s.dc)]
        wait(m.recv, f"dkv{l}", m.dkv_in.at[l, pl.ds(0, s.nr - 1)])
        total = m.dkv_in[l, 0].astype(F32)
        for k in range(1, s.nr):
            total = total + m.dkv_in[l, k].astype(F32)
        m.dqkv[:, s.dc :] = total.astype(BF16)
        back = dot_nt(m.dqkv[...], m.wqkv[l])
        if l:
            scatter(back, f"dx{l}")
        else:
            m.part[...] = back.astype(BF16)
            m.part[rows(c, s.t), :] = (m.part[rows(c, s.t), :].astype(F32) + m.carry[...]).astype(BF16)
            each_col(lambda cc: remote(m.part.at[:, rows(cc, s.dc)], m.got_in.at[c], "gin", r, cc).start())
            m.got_in[c] = m.part[:, rows(c, s.dc)]
        sums = jnp.sum(m.dqkv[...].astype(F32), axis=0, keepdims=True)
        m.own[own + 4 : own + 5, :] = sums[:, : s.dc]
        m.own[own + 5 : own + 6, :] = sums[:, 2 * s.dc :]
        m.gqkv[...] = dot_tn(m.xf[l], m.dqkv[...]).astype(BF16)
        each_row(lambda rr: remote(m.gqkv.at[rows(rr, s.dr)], m.gqkv_in.at[l, r], f"gq{l}", rr, c).start())
        m.gqkv_in[l, r] = m.gqkv[rows(r, s.dr), :]
        if l:
            grad = scattered(f"dx{l}") + m.carry[...]

    each_col(lambda cc: remote(m.vec.at[:, rows(cc, s.dc)], m.vec_in.at[c], "vec", r, cc).start())
    m.vec_in[c] = m.vec[:, rows(c, s.dc)]
    wait(m.recv, "vec", m.vec_in.at[pl.ds(0, few)])
    total = m.vec_in[0]
    for k in range(1, s.nc):
        total = total + m.vec_in[k]
    for l in range(L):
        own = l * 2 * VEC_ROWS + VEC_ROWS
        m.own[own : own + VEC_ROWS, :] = total[l * VEC_ROWS : (l + 1) * VEC_ROWS]
    m.own_in[r] = m.own[...]
    each_row(lambda rr: remote(m.own, m.own_in.at[r], "own", rr, c).start())

    def sum_up(buf, l, out):
        total = buf[l, 0].astype(F32)
        for k in range(1, s.nr):
            total = total + buf[l, k].astype(F32)
        out[l] = total

    for l in reversed(range(L)):
        wait_home(m.recv, f"gd{l}", m.gdown_in.at[l])
        sum_up(m.gdown_in, l, m.o_down)
        wait(m.recv, f"gu{l}", m.gup_in.at[l, pl.ds(0, s.nr - 1)])
        sum_up(m.gup_in, l, m.o_up)
        wait_home(m.recv, f"gp{l}", m.gproj_in.at[l])
        sum_up(m.gproj_in, l, m.o_proj)
        if l == 0:
            wait(m.recv, "gin", m.got_in.at[pl.ds(0, few)])
            total = m.got_in[0].astype(F32)
            for k in range(1, s.nc):
                total = total + m.got_in[k].astype(F32)
            m.o_in[...] = total
            wait(m.recv, "act", m.act_in.at[pl.ds(0, few * s.t)])
            m.o_act[...] = m.act_in[...]
        wait(m.recv, f"gq{l}", m.gqkv_in.at[l, pl.ds(0, s.nr - 1)])
        sum_up(m.gqkv_in, l, m.o_qkv)
    wait(m.recv, "own", m.own_in.at[pl.ds(0, s.nr - 1)])
    total = m.own_in[0]
    for k in range(1, s.nr):
        total = total + m.own_in[k]
    m.o_vec[...] = total

    wait(m.send, "x", m.xf.at[0, :, pl.ds(0, few * s.dc)])
    wait(m.send, "pvec", m.pv.at[:, pl.ds(0, few * s.dc)])
    wait(m.send, "cotan", m.cot.at[:, pl.ds(0, few * s.dc)])
    wait(m.send, "act", m.act_in.at[pl.ds(0, few * s.t)])
    wait(m.send, "gin", m.got_in.at[pl.ds(0, few)])
    wait(m.send, "vec", m.vec_in.at[pl.ds(0, few)])
    wait(m.send, "own", m.own_in.at[pl.ds(0, s.nr - 1)])
    for l in range(L):
        wait(m.send, f"wq{l}", m.wqkv.at[l, pl.ds(0, (s.nr - 1) * s.dr)])
        wait(m.send, f"wu{l}", m.wup.at[l, pl.ds(0, (s.nr - 1) * s.dr)])
        wait_home(m.send, f"wp{l}", m.gproj_in.at[l])
        wait_home(m.send, f"wd{l}", m.gdown_in.at[l])
    wait(m.send, "dkv0", m.dkv.at[pl.ds(0, s.nr - 1)])
    wait_home(m.send, "gd0", m.gdown_in.at[0])
    wait(m.send, "gu0", m.gup_in.at[0, pl.ds(0, s.nr - 1)])
    wait_home(m.send, "gp0", m.gproj_in.at[0])
    wait(m.send, "gq0", m.gqkv_in.at[0, pl.ds(0, s.nr - 1)])


def body(s, layer_input, query_weight, key_weight, value_weight, proj_weight, up_weight, down_weight, query_shift,
         value_shift, proj_shift, up_shift, down_shift, first_gain, first_shift, second_gain, second_shift, segment_ids,
         cotangent):
    L = LAYERS
    wq = jnp.concatenate([query_weight, key_weight, value_weight], axis=2)
    zero = jnp.zeros_like(proj_shift)
    pvec = jnp.stack([proj_shift, down_shift, first_gain, first_shift, second_gain, second_shift, zero, zero], axis=1)
    pvec = pvec.reshape(L * VEC_ROWS, s.dc)
    qkvb = jnp.concatenate([query_shift, jnp.zeros_like(query_shift), value_shift], axis=1).astype(F32)
    upb = up_shift.astype(F32)
    places = segment_ids[: s.tok].reshape(4, 1, s.qc)
    segq = jnp.tile(places, (1, 2, 1)).reshape(4, 2 * s.qc, 1)
    segk = jnp.tile(places, (1, s.nr, 1)).reshape(4, s.nr * s.qc)
    shapes = scratch_of(s)
    out_shape = (
        jax.ShapeDtypeStruct((s.tok, s.dc), BF16),
        jax.ShapeDtypeStruct((s.tok, s.dc), F32),
        jax.ShapeDtypeStruct((L, s.dr, 3 * s.dc), F32),
        jax.ShapeDtypeStruct((L, s.dr, s.dc), F32),
        jax.ShapeDtypeStruct((L, s.dr, s.fc), F32),
        jax.ShapeDtypeStruct((L, s.fr, s.dc), F32),
        jax.ShapeDtypeStruct((L * 2 * VEC_ROWS, s.dc), F32),
    )
    vmem = pl.BlockSpec(memory_space=pltpu.VMEM)
    o_act, o_in, o_qkv, o_proj, o_up, o_down, o_vec = pl.pallas_call(
        functools.partial(kernel, s),
        out_shape=out_shape,
        in_specs=[vmem] * len(INPUTS),
        out_specs=[vmem] * len(OUTPUTS),
        scratch_shapes=[pltpu.VMEM(shape, dtype) for shape, dtype in shapes.values()]
        + [pltpu.SemaphoreType.DMA((len(PHASES),))] * 2,
        compiler_params=pltpu.CompilerParams(
            collective_id=0, has_side_effects=True, vmem_limit_bytes=60 * 2**20),
        name="encoder",
    )(layer_input, cotangent, wq, proj_weight, up_weight, down_weight, pvec, qkvb, upb, segq, segk)
    own = o_vec.reshape(L, 2 * VEC_ROWS, s.dc)
    up_rows = s.fc // LANES
    vectors = own[:, VEC_ROWS:]
    return (
        o_act, o_in, o_qkv[:, :, : s.dc], o_qkv[:, :, s.dc : 2 * s.dc], o_qkv[:, :, 2 * s.dc :], o_proj, o_up, o_down,
        own[:, 4], own[:, 5], vectors[:, PROJ_B], own[:, :up_rows].reshape(L, s.fc), vectors[:, DOWN_B],
        vectors[:, GAIN1], vectors[:, SHIFT1], vectors[:, GAIN2], vectors[:, SHIFT2],
    )


def build(mesh, tok, d, ff):
    s = Sizes(mesh.shape["row"], mesh.shape["col"], tok, d, ff)
    return jax.shard_map(
        functools.partial(body, s),
        mesh=mesh,
        in_specs=(P("row", "col"),) + (P(None, "row", "col"),) * 6 + (P(None, "col"),) * 9 + (P(), P("row", "col")),
        out_specs=(P("row", "col"),) * 2 + (P(None, "row", "col"),) * 6 + (P(None, "col"),) * 9,
        check_vma=False,
    )


def solution(mesh):
    return build(mesh, 256, 1024, 4096)
```

```python
import functools
from types import SimpleNamespace

import jax
import jax.numpy as jnp
from jax import lax
from jax.experimental import pallas as pl
from jax.experimental.pallas import tpu as pltpu
from jax.sharding import PartitionSpec as P

MESH = pl.DeviceIdType.MESH
LAYERS = 2
HEAD_DIM = 64
LANES = 128
F32 = jnp.float32
BF16 = jnp.bfloat16
PAIRS = ((0, 0), (1, 1), (1, 2), (2, 1), (2, 2), (2, 3), (3, 2), (3, 3))
KEYS_OF = {i: [(n, j) for n, (a, j) in enumerate(PAIRS) if a == i] for i in range(4)}
QUERIES_OF = {j: [(n, i) for n, (i, b) in enumerate(PAIRS) if b == j] for j in range(4)}

PROJ_B, DOWN_B, GAIN1, SHIFT1, GAIN2, SHIFT2 = range(6)
VEC_ROWS = 8


def dot(a, b):
    return jnp.dot(a, b, preferred_element_type=F32)


def dot_nt(a, b):
    return lax.dot_general(a, b, (((1,), (1,)), ((), ())), preferred_element_type=F32)


def dot_tn(a, b):
    return lax.dot_general(a, b, (((0,), (0,)), ((), ())), preferred_element_type=F32)


class Sizes:
    def __init__(self, nr, nc, tok, d, ff):
        self.nr, self.nc, self.tok, self.d, self.ff = nr, nc, tok, d, ff
        self.t = tok // nc
        self.dc, self.fc = d // nc, ff // nc
        self.dr, self.fr = d // nr, ff // nr
        self.nzx = nr // 2
        self.qc = tok // 4


def scratch_of(s):
    L = LAYERS
    v = {}
    v["xf"] = ((L, s.tok, s.d), BF16)
    v["x1"] = ((L, s.tok, s.d), BF16)
    v["dff"] = ((L, s.tok, s.d), BF16)
    v["drf"] = ((L, s.tok, s.d), BF16)
    v["part"] = ((s.tok, s.d), BF16)
    v["got"] = ((s.nc, s.t, s.d), BF16)
    v["got_in"] = ((s.nc, s.tok, s.dc), BF16)
    v["act_out"] = ((s.t, s.d), BF16)
    v["act_in"] = ((s.tok, s.dc), BF16)
    v["cot"] = ((s.t, s.d), BF16)
    v["pv"] = ((L * VEC_ROWS, s.d), F32)
    v["kv"] = ((L, s.nzx, 2, s.tok, 2 * s.dc), BF16)
    v["dkv"] = ((s.nzx, 2, s.tok, 2 * s.dc), BF16)
    v["dkv_c"] = ((L, s.nzx, s.tok, 2 * s.dc), BF16)
    v["dkv_in"] = ((L, s.nzx, s.tok, 2 * s.dc), BF16)
    v["probs"] = ((L, len(PAIRS), 2 * s.qc, s.nr * s.qc), BF16)
    v["q2"] = ((L, 4, 2 * s.qc, s.dc), BF16)
    v["do2"] = ((4, 2 * s.qc, s.dc), BF16)
    v["delta"] = ((4, 2 * s.qc, 1), F32)
    v["dq2"] = ((4, 2 * s.qc, s.dc), F32)
    v["att"] = ((L, s.tok, s.dc), F32)
    v["gate"] = ((L, s.tok, s.fc), BF16)
    v["slope"] = ((L, s.tok, s.fc), F32)
    v["de"] = ((s.tok, s.fc), BF16)
    v["n1"] = ((L, s.t, s.d), F32)
    v["n2"] = ((L, s.t, s.d), F32)
    v["r1"] = ((L, s.t, 1), F32)
    v["r2"] = ((L, s.t, 1), F32)
    v["carry"] = ((s.t, s.d), F32)
    v["dqkv"] = ((s.tok, 3 * s.dc), BF16)
    v["wqkv"] = ((L, s.nzx, 2, s.dr, 3 * s.dc), BF16)
    v["wup"] = ((L, s.nzx, 2, s.dr, s.fc), BF16)
    v["wproj"] = ((L, s.dc, s.d), BF16)
    v["wdown"] = ((L, s.fc, s.d), BF16)
    v["wp_own"] = ((L, s.dr, s.dc), BF16)
    v["wd_own"] = ((L, s.fr, s.dc), BF16)
    v["gqkv"] = ((s.nzx, 2, s.dr, 3 * s.dc), BF16)
    v["gup"] = ((s.nzx, 2, s.dr, s.fc), BF16)
    v["gproj"] = ((s.dc, s.d), BF16)
    v["gdown"] = ((s.fc, s.d), BF16)
    v["gqkv_c"] = ((L, s.nzx, s.dr, 3 * s.dc), BF16)
    v["gup_c"] = ((L, s.nzx, s.dr, s.fc), BF16)
    v["gproj_c"] = ((L, s.dr, s.d), BF16)
    v["gdown_c"] = ((L, s.fr, s.d), BF16)
    v["gqkv_in"] = ((L, s.nzx, s.dr, 3 * s.dc), BF16)
    v["gup_in"] = ((L, s.nzx, s.dr, s.fc), BF16)
    v["gproj_in"] = ((L, s.nzx, s.dr, s.dc), BF16)
    v["gdown_in"] = ((L, s.nzx, s.fr, s.dc), BF16)
    v["gproj_out"] = ((L, s.dr, s.dc), BF16)
    v["gdown_out"] = ((L, s.fr, s.dc), BF16)
    v["gproj_fin"] = ((L, s.dr, s.dc), BF16)
    v["gdown_fin"] = ((L, s.fr, s.dc), BF16)
    v["vec"] = ((L * VEC_ROWS, s.d), F32)
    v["vec_in"] = ((s.nc, L * VEC_ROWS, s.dc), F32)
    v["own"] = ((L * 2 * VEC_ROWS, s.dc), F32)
    v["own_in"] = ((s.nr, L * 2 * VEC_ROWS, s.dc), F32)
    return v


INPUTS = ("x", "cotan", "wq", "wk", "wv", "wp", "wu", "wd", "qb", "vb", "pb", "upb", "db", "g1", "s1", "g2", "s2", "segq",
          "segk")
OUTPUTS = ("o_act", "o_in", "o_q", "o_k", "o_v", "o_proj", "o_up", "o_down", "o_vec")
PHASES = (
    ["x", "cotan", "pvec", "act", "gin", "vec", "own", "wpt", "wdt"]
    + [f"{n}{l}" for l in range(LAYERS) for n in ("pr", "n1", "fr", "h", "df", "dn", "dr", "dx", "gpt", "gdt")]
    + [f"{n}{l}{e}" for l in range(LAYERS) for n in ("wq", "wp", "wu", "wd", "kv", "dkv", "gq", "gp", "gu", "gd")
       for e in ("", "c")]
)
PHASE = {name: index for index, name in enumerate(PHASES)}


def kernel(s, *refs):
    names = INPUTS + OUTPUTS + tuple(scratch_of(s)) + ("send", "recv")
    m = SimpleNamespace(**dict(zip(names, refs)))
    L = LAYERS
    r, c = lax.axis_index("row"), lax.axis_index("col")
    zx, k = lax.div(r, 2), lax.rem(r, 2)
    other = zx * 2 + 1 - k
    at_home = zx == c
    chips, few = s.nzx - 1, s.nc - 1

    def remote(src, dst, phase, row, col):
        return pltpu.make_async_remote_copy(
            src_ref=src, dst_ref=dst, send_sem=m.send.at[PHASE[phase]], recv_sem=m.recv.at[PHASE[phase]],
            device_id=(row, col), device_id_type=MESH)

    def wait(sems, phase, ref):
        pltpu.make_async_copy(ref, ref, sems.at[PHASE[phase]]).wait()

    def each_col(fn):
        def step(q, carry):
            fn(lax.rem(c + q, s.nc))
            return carry
        lax.fori_loop(1, s.nc, step, 0)

    def each_row(fn):
        def step(q, carry):
            fn(lax.rem(r + q, s.nr))
            return carry
        lax.fori_loop(1, s.nr, step, 0)

    def each_chip(fn):
        def step(q, carry):
            fn(lax.rem(zx + q, s.nzx))
            return carry
        lax.fori_loop(1, s.nzx, step, 0)

    def rows(i, n):
        return pl.ds(pl.multiple_of(i * n, n), n)

    barrier = pltpu.get_barrier_semaphore()

    def greet(row, col):
        pl.semaphore_signal(barrier, inc=1, device_id=(row, col), device_id_type=MESH)

    swap_row, swap_col = c * 2 + k, zx
    each_col(lambda cc: greet(r, cc))
    each_row(lambda rr: greet(rr, c))

    @pl.when(jnp.logical_not(at_home))
    def _():
        greet(swap_row, swap_col)

    def weight(name, l):
        if name in ("wq", "wu", "kv"):
            ref = {"wq": m.wqkv, "wu": m.wup, "kv": m.kv}[name]
            return (lambda i, kk: ref.at[l, i, kk]), (lambda kk: ref.at[l, :, kk]), ref.at[l, pl.ds(0, chips), 0]
        ref, n = {"wp": (m.wproj, s.dr), "wd": (m.wdown, s.fr)}[name]
        return ((lambda i, kk: ref.at[l, rows(kk, n), rows(i, s.dc)]), (lambda kk: ref.at[l, rows(kk, n)]),
                ref.at[l, pl.ds(0, n), pl.ds(0, chips * s.dc)])

    def gather(name, l):
        piece = weight(name, l)[0](zx, k)
        each_chip(lambda i: remote(piece, piece, f"{name}{l}", i * 2 + k, c).start())

    def pass_on(name, l):
        _, half, many = weight(name, l)
        wait(m.recv, f"{name}{l}", many)
        remote(half(k), half(k), f"{name}{l}c", other, c).start()

    def gathered(name, l):
        wait(m.recv, f"{name}{l}c", weight(name, l)[1](1 - k))

    def sent_gather(name, l):
        _, half, many = weight(name, l)
        wait(m.send, f"{name}{l}", many)
        wait(m.send, f"{name}{l}c", half(k))

    def partial_sum(name, l):
        if name in ("gq", "gu", "dkv"):
            full, mid, got = {"gq": (m.gqkv, m.gqkv_c, m.gqkv_in), "gu": (m.gup, m.gup_c, m.gup_in),
                              "dkv": (m.dkv, m.dkv_c, m.dkv_in)}[name]
            return (lambda kk: full.at[:, kk]), mid, (lambda i: mid.at[l, i]), got
        full, mid, got, n = {"gp": (m.gproj, m.gproj_c, m.gproj_in, s.dr),
                             "gd": (m.gdown, m.gdown_c, m.gdown_in, s.fr)}[name]
        return (lambda kk: full.at[rows(kk, n)]), mid, (lambda i: mid.at[l, :, rows(i, s.dc)]), got

    def reduce_start(name, l):
        half, mid, _, _ = partial_sum(name, l)
        remote(half(1 - k), mid.at[l], f"{name}{l}c", other, c).start()

    def reduce_mid(name, l):
        half, mid, piece, got = partial_sum(name, l)
        wait(m.recv, f"{name}{l}c", mid.at[l])
        mid[l] = (half(k)[...].astype(F32) + mid[l].astype(F32)).astype(BF16)
        each_chip(lambda i: remote(piece(i), got.at[l, zx], f"{name}{l}", i * 2 + k, c).start())
        got[l, zx] = piece(zx)[...]

    def reduce_end(name, l):
        got = partial_sum(name, l)[3]
        wait(m.recv, f"{name}{l}", got.at[l, pl.ds(0, chips)])
        total = got[l, 0].astype(F32)
        for i in range(1, s.nzx):
            total = total + got[l, i].astype(F32)
        return total

    def sent_half(name, l):
        half, mid, _, _ = partial_sum(name, l)
        wait(m.send, f"{name}{l}c", mid.at[l])

    def sent_pieces(name, l):
        got = partial_sum(name, l)[3]
        wait(m.send, f"{name}{l}", got.at[l, pl.ds(0, chips)])

    m.xf[0, :, rows(c, s.dc)] = m.x[...]
    m.cot[:, rows(c, s.dc)] = m.cotan[rows(c, s.t), :]
    m.pv[:, rows(c, s.dc)] = jnp.zeros((L * VEC_ROWS, s.dc), F32)
    for l in range(L):
        for which, ref in enumerate((m.pb, m.db, m.g1, m.s1, m.g2, m.s2)):
            m.pv[l * VEC_ROWS + which : l * VEC_ROWS + which + 1, rows(c, s.dc)] = ref[l : l + 1, :].astype(F32)
        for which, ref in enumerate((m.wq, m.wk, m.wv)):
            m.wqkv[l, zx, k, :, which * s.dc : (which + 1) * s.dc] = ref[l]
        m.wup[l, zx, k] = m.wu[l]

    pl.semaphore_wait(barrier, s.nc - 1 + s.nr - 1 + 1 - at_home.astype(jnp.int32))

    gather("wq", 0)
    each_col(lambda cc: remote(m.x, m.xf.at[0, :, rows(c, s.dc)], "x", r, cc).start())

    @pl.when(jnp.logical_not(at_home))
    def _():
        remote(m.wp, m.wp_own, "wpt", swap_row, swap_col).start()
        remote(m.wd, m.wd_own, "wdt", swap_row, swap_col).start()
    mine = m.pv.at[:, rows(c, s.dc)]
    each_col(lambda cc: remote(mine, mine, "pvec", r, cc).start())
    each_col(lambda cc: remote(m.cotan.at[rows(cc, s.t)], m.cot.at[:, rows(c, s.dc)], "cotan", r, cc).start())
    m.vec[...] = jnp.zeros(m.vec.shape, F32)
    m.own[...] = jnp.zeros(m.own.shape, F32)

    def vector(l, which):
        return m.pv[l * VEC_ROWS + which : l * VEC_ROWS + which + 1, :]

    def share(buf, value, phase):
        buf[rows(c, s.t), :] = value
        each_col(lambda cc: remote(buf.at[rows(c, s.t)], buf.at[rows(c, s.t)], phase, r, cc).start())

    def shared(buf, phase):
        for sems in (m.recv, m.send):
            wait(sems, phase, buf.at[pl.ds(0, few * s.t)])

    def scatter(value, phase):
        m.part[...] = value.astype(BF16)
        each_col(lambda cc: remote(m.part.at[rows(cc, s.t)], m.got.at[c], phase, r, cc).start())
        m.got[c] = m.part[rows(c, s.t), :]

    def scattered(phase):
        for sems in (m.recv, m.send):
            wait(sems, phase, m.got.at[pl.ds(0, few)])
        total = m.got[0].astype(F32)
        for i in range(1, s.nc):
            total = total + m.got[i].astype(F32)
        return total

    def norm(u, l, gain, shift, n_ref, r_ref):
        mean = jnp.sum(u, axis=1, keepdims=True) / s.d
        var = jnp.sum(u * u, axis=1, keepdims=True) / s.d - mean * mean
        inv = lax.rsqrt(var + 1e-12)
        n = (u - mean) * inv
        n_ref[l] = n
        r_ref[l] = inv
        return n * vector(l, gain) + vector(l, shift)

    def norm_back(g, l, gain, shift, n_ref, r_ref):
        n = n_ref[l]
        w = g * vector(l, gain)
        first = jnp.sum(w, axis=1, keepdims=True) / s.d
        second = jnp.sum(w * n, axis=1, keepdims=True) / s.d
        at = l * VEC_ROWS
        m.vec[at + gain : at + gain + 1, :] = jnp.sum(g * n, axis=0, keepdims=True)
        m.vec[at + shift : at + shift + 1, :] = jnp.sum(g, axis=0, keepdims=True)
        return r_ref[l] * (w - first - n * second)

    low_lanes = lax.broadcasted_iota(jnp.int32, (s.qc, s.dc), 1) < HEAD_DIM

    def two_heads(block):
        block = block.astype(F32)
        return jnp.concatenate([jnp.where(low_lanes, block, 0.0), jnp.where(low_lanes, 0.0, block)], axis=0)

    def one_block(pair):
        return jnp.where(low_lanes, pair[: s.qc], pair[s.qc :])

    def keys(l, j, value):
        lanes = pl.ds(s.dc if value else 0, s.dc)
        return m.kv[l, :, :, pl.ds(j * s.qc, s.qc), lanes].reshape(s.nr * s.qc, s.dc)

    def swapped(l):
        m.wproj[l, rows(k, s.dr), rows(zx, s.dc)] = m.wp_own[l]
        m.wdown[l, rows(k, s.fr), rows(zx, s.dc)] = m.wd_own[l]

    pass_on("wq", 0)
    wait(m.recv, "x", m.xf.at[0, :, pl.ds(0, few * s.dc)])
    wait(m.recv, "pvec", m.pv.at[:, pl.ds(0, few * s.dc)])

    @pl.when(at_home)
    def _():
        m.wp_own[...] = m.wp[...]
        m.wd_own[...] = m.wd[...]

    @pl.when(jnp.logical_not(at_home))
    def _():
        wait(m.recv, "wpt", m.wp_own)
        wait(m.recv, "wdt", m.wd_own)
    swapped(0)
    hidden = m.xf[0, rows(c, s.t), :].astype(F32)
    for l in range(L):
        gathered("wq", l)
        qkv = dot(m.xf[l], m.wqkv[l].reshape(s.d, 3 * s.dc))
        keep = (qkv[:, 2 * s.dc :] + m.vb[l : l + 1, :].astype(F32)).astype(BF16)
        m.kv[l, zx, k, :, : s.dc] = qkv[:, s.dc : 2 * s.dc].astype(BF16)
        m.kv[l, zx, k, :, s.dc :] = keep
        gather("kv", l)
        if l == 0:
            gather("wp", 0)
        for i in range(4):
            block = (qkv[i * s.qc : (i + 1) * s.qc, : s.dc] + m.qb[l : l + 1, :].astype(F32)).astype(BF16)
            m.q2[l, i] = (two_heads(block) * HEAD_DIM ** (-0.5)).astype(BF16)
        m.carry[...] = hidden
        pass_on("kv", l)
        if l == 0:
            gather("wu", 0)
            gather("wd", 0)
            pass_on("wp", 0)
        else:
            pass_on("wu", 1)
            pass_on("wd", 1)
        gathered("kv", l)
        for i in range(4):
            queries = m.q2[l, i]
            ids = m.segq[i]
            scores = []
            for _, j in KEYS_OF[i]:
                raw = dot_nt(queries, keys(l, j, False))
                scores.append(jnp.where(ids == m.segk[j : j + 1, :], raw, -1e9))
            top = functools.reduce(jnp.maximum, [jnp.max(x, axis=1, keepdims=True) for x in scores])
            raised = [jnp.exp(x - top) for x in scores]
            inverse = 1.0 / sum(jnp.sum(x, axis=1, keepdims=True) for x in raised)
            out = jnp.zeros((2 * s.qc, s.dc), F32)
            for (n, j), x in zip(KEYS_OF[i], raised):
                prob = (x * inverse).astype(BF16)
                m.probs[l, n] = prob
                out = out + dot(prob, keys(l, j, True))
            m.att[l, i * s.qc : (i + 1) * s.qc, :] = one_block(out)
        gathered("wp", l)
        scatter(dot(m.att[l].astype(BF16), m.wproj[l]), f"pr{l}")
        if l == 0:
            pass_on("wu", 0)
            pass_on("wd", 0)
            swapped(1)
        u = scattered(f"pr{l}") + vector(l, PROJ_B) + m.carry[...]
        first_out = norm(u, l, GAIN1, SHIFT1, m.n1, m.r1)
        share(m.x1.at[l], first_out.astype(BF16), f"n1{l}")
        m.carry[...] = first_out
        if l == 0:
            gather("wq", 1)
            gather("wp", 1)
        gathered("wu", l)
        shared(m.x1.at[l], f"n1{l}")
        pre = dot(m.x1[l], m.wup[l].reshape(s.d, s.fc)) + m.upb[l : l + 1, :].astype(F32)
        cdf = 0.5 * (1.0 + lax.erf(pre * 0.5**0.5))
        m.gate[l] = (pre * cdf).astype(BF16)
        m.slope[l] = cdf + pre * (jnp.exp(-0.5 * pre * pre) * 0.3989422804014327)
        gathered("wd", l)
        scatter(dot(m.gate[l], m.wdown[l]), f"fr{l}")
        if l == 0:
            pass_on("wq", 1)
            pass_on("wp", 1)
        u = scattered(f"fr{l}") + vector(l, DOWN_B) + m.carry[...]
        hidden = norm(u, l, GAIN2, SHIFT2, m.n2, m.r2)
        if l == 0:
            share(m.xf.at[1], hidden.astype(BF16), "h0")
            gather("wu", 1)
            gather("wd", 1)
            shared(m.xf.at[1], "h0")

    m.act_out[...] = hidden.astype(BF16)
    each_col(lambda cc: remote(m.act_out.at[:, rows(cc, s.dc)], m.act_in.at[rows(c, s.t)], "act", r, cc).start())
    m.act_in[rows(c, s.t), :] = m.act_out[:, rows(c, s.dc)]

    def swap_back(l, name, total):
        out, fin, phase = {"gp": (m.gproj_out, m.gproj_fin, f"gpt{l}"), "gd": (m.gdown_out, m.gdown_fin, f"gdt{l}")}[name]
        out[l] = total.astype(BF16)

        @pl.when(jnp.logical_not(at_home))
        def _():
            remote(out.at[l], fin.at[l], phase, swap_row, swap_col).start()

        @pl.when(at_home)
        def _():
            fin[l] = out[l]

    def swap_end(l, name, out):
        fin, phase = {"gp": (m.gproj_fin, f"gpt{l}"), "gd": (m.gdown_fin, f"gdt{l}")}[name]

        @pl.when(jnp.logical_not(at_home))
        def _():
            wait(m.recv, phase, fin.at[l])
        out[l] = fin[l].astype(F32)

    wait(m.recv, "cotan", m.cot.at[:, pl.ds(0, few * s.dc)])
    grad = m.cot[...].astype(F32)
    for l in reversed(range(L)):
        at = l * VEC_ROWS
        own = l * 2 * VEC_ROWS
        dz = norm_back(grad, l, GAIN2, SHIFT2, m.n2, m.r2)
        m.carry[...] = dz
        low = dz.astype(BF16)
        share(m.dff.at[l], low, f"df{l}")
        m.vec[at + DOWN_B : at + DOWN_B + 1, :] = jnp.sum(low.astype(F32), axis=0, keepdims=True)
        if l + 1 < L:
            reduce_mid("gq", l + 1)
            swap_back(l + 1, "gp", reduce_end("gp", l + 1))
        shared(m.dff.at[l], f"df{l}")
        de = (dot_nt(m.dff[l], m.wdown[l]) * m.slope[l]).astype(BF16)
        m.de[...] = de
        scatter(dot_nt(de, m.wup[l].reshape(s.d, s.fc)), f"dn{l}")
        sums = jnp.sum(de.astype(F32), axis=0, keepdims=True)
        for i in range(s.fc // LANES):
            m.own[own + i : own + i + 1, :] = sums[:, i * LANES : (i + 1) * LANES]
        if l + 1 < L:
            sent_half("gd", l + 1)
            sent_half("gu", l + 1)
        m.gdown[...] = dot_tn(m.gate[l], m.dff[l]).astype(BF16)
        reduce_start("gd", l)
        m.gup[...] = dot_tn(m.x1[l], m.de[...]).astype(BF16).reshape(m.gup.shape)
        reduce_start("gu", l)
        grad = scattered(f"dn{l}") + m.carry[...]
        du = norm_back(grad, l, GAIN1, SHIFT1, m.n1, m.r1)
        m.carry[...] = du
        low = du.astype(BF16)
        share(m.drf.at[l], low, f"dr{l}")
        m.vec[at + PROJ_B : at + PROJ_B + 1, :] = jnp.sum(low.astype(F32), axis=0, keepdims=True)
        reduce_mid("gd", l)
        reduce_mid("gu", l)
        shared(m.drf.at[l], f"dr{l}")
        if l == 0:
            each_col(lambda cc: remote(m.vec.at[:, rows(cc, s.dc)], m.vec_in.at[c], "vec", r, cc).start())
            m.vec_in[c] = m.vec[:, rows(c, s.dc)]
        dout = dot_nt(m.drf[l], m.wproj[l]).astype(BF16)
        for i in range(4):
            block = two_heads(dout[i * s.qc : (i + 1) * s.qc, :])
            kept = m.att[l, i * s.qc : (i + 1) * s.qc, :]
            m.do2[i] = block.astype(BF16)
            m.delta[i] = jnp.sum(block * jnp.concatenate([kept, kept], axis=0), axis=1, keepdims=True)
            m.dq2[i] = jnp.zeros((2 * s.qc, s.dc), F32)
        if l + 1 < L:
            sent_half("dkv", l + 1)
        for j in range(4):
            key_grad = jnp.zeros((s.nr * s.qc, s.dc), F32)
            value_grad = jnp.zeros((s.nr * s.qc, s.dc), F32)
            for n, i in QUERIES_OF[j]:
                prob = m.probs[l, n]
                prob_grad = dot_nt(m.do2[i], keys(l, j, True))
                score_grad = (prob.astype(F32) * (prob_grad - m.delta[i])).astype(BF16)
                m.dq2[i] += dot(score_grad, keys(l, j, False))
                key_grad = key_grad + dot_tn(score_grad, m.q2[l, i])
                value_grad = value_grad + dot_tn(prob, m.do2[i])
            shape = (s.nzx, 2, s.qc, s.dc)
            m.dkv[:, :, pl.ds(j * s.qc, s.qc), pl.ds(0, s.dc)] = key_grad.astype(BF16).reshape(shape)
            m.dkv[:, :, pl.ds(j * s.qc, s.qc), pl.ds(s.dc, s.dc)] = value_grad.astype(BF16).reshape(shape)
        reduce_start("dkv", l)
        for i in range(4):
            m.dqkv[i * s.qc : (i + 1) * s.qc, : s.dc] = (one_block(m.dq2[i]) * HEAD_DIM ** (-0.5)).astype(BF16)
        reduce_mid("dkv", l)
        if l + 1 < L:
            sent_half("gp", l + 1)
            sent_half("gq", l + 1)
        m.gproj[...] = dot_tn(m.att[l].astype(BF16), m.drf[l]).astype(BF16)
        reduce_start("gp", l)
        swap_back(l, "gd", reduce_end("gd", l))
        m.o_up[l] = reduce_end("gu", l)
        reduce_mid("gp", l)
        if l + 1 < L:
            swap_end(l + 1, "gd", m.o_down)
            swap_end(l + 1, "gp", m.o_proj)
            total = reduce_end("gq", l + 1)
            for which, out in enumerate((m.o_q, m.o_k, m.o_v)):
                out[l + 1] = total[:, which * s.dc : (which + 1) * s.dc]
        if l == 0:
            wait(m.recv, "vec", m.vec_in.at[pl.ds(0, few)])
            total = m.vec_in[0]
            for i in range(1, s.nc):
                total = total + m.vec_in[i]
            for i in range(L):
                to = i * 2 * VEC_ROWS + VEC_ROWS
                m.own[to : to + VEC_ROWS, :] = total[i * VEC_ROWS : (i + 1) * VEC_ROWS]
        m.dqkv[:, s.dc :] = reduce_end("dkv", l).astype(BF16)
        back = dot_nt(m.dqkv[...], m.wqkv[l].reshape(s.d, 3 * s.dc))
        if l:
            scatter(back, f"dx{l}")
        else:
            m.part[...] = back.astype(BF16)
            m.part[rows(c, s.t), :] = (m.part[rows(c, s.t), :].astype(F32) + m.carry[...]).astype(BF16)
            each_col(lambda cc: remote(m.part.at[:, rows(cc, s.dc)], m.got_in.at[c], "gin", r, cc).start())
            m.got_in[c] = m.part[:, rows(c, s.dc)]
        m.gqkv[...] = dot_tn(m.xf[l], m.dqkv[...]).astype(BF16).reshape(m.gqkv.shape)
        reduce_start("gq", l)
        sums = jnp.sum(m.dqkv[...].astype(F32), axis=0, keepdims=True)
        m.own[own + 4 : own + 5, :] = sums[:, : s.dc]
        m.own[own + 5 : own + 6, :] = sums[:, 2 * s.dc :]
        if l:
            grad = scattered(f"dx{l}") + m.carry[...]

    m.own_in[r] = m.own[...]
    each_row(lambda rr: remote(m.own, m.own_in.at[r], "own", rr, c).start())
    reduce_mid("gq", 0)
    swap_back(0, "gp", reduce_end("gp", 0))
    swap_end(0, "gd", m.o_down)
    wait(m.recv, "act", m.act_in.at[pl.ds(0, few * s.t)])
    m.o_act[...] = m.act_in[...]
    wait(m.recv, "gin", m.got_in.at[pl.ds(0, few)])
    total = m.got_in[0].astype(F32)
    for i in range(1, s.nc):
        total = total + m.got_in[i].astype(F32)
    m.o_in[...] = total
    wait(m.recv, "own", m.own_in.at[pl.ds(0, s.nr - 1)])
    total = m.own_in[0]
    for i in range(1, s.nr):
        total = total + m.own_in[i]
    m.o_vec[...] = total
    total = reduce_end("gq", 0)
    for which, out in enumerate((m.o_q, m.o_k, m.o_v)):
        out[0] = total[:, which * s.dc : (which + 1) * s.dc]
    swap_end(0, "gp", m.o_proj)

    wait(m.send, "x", m.xf.at[0, :, pl.ds(0, few * s.dc)])
    wait(m.send, "pvec", m.pv.at[:, pl.ds(0, few * s.dc)])
    wait(m.send, "cotan", m.cot.at[:, pl.ds(0, few * s.dc)])
    wait(m.send, "act", m.act_in.at[pl.ds(0, few * s.t)])
    wait(m.send, "gin", m.got_in.at[pl.ds(0, few)])
    wait(m.send, "vec", m.vec_in.at[pl.ds(0, few)])
    wait(m.send, "own", m.own_in.at[pl.ds(0, s.nr - 1)])

    @pl.when(jnp.logical_not(at_home))
    def _():
        wait(m.send, "wpt", m.wp_own)
        wait(m.send, "wdt", m.wd_own)
        for l in range(L):
            wait(m.send, f"gpt{l}", m.gproj_fin.at[l])
            wait(m.send, f"gdt{l}", m.gdown_fin.at[l])
    for l in range(L):
        for name in ("wq", "wp", "wu", "wd", "kv"):
            sent_gather(name, l)
        for name in ("gq", "gp", "gu", "gd", "dkv"):
            sent_pieces(name, l)
    for name in ("gq", "gp", "gu", "gd", "dkv"):
        sent_half(name, 0)


def body(s, layer_input, query_weight, key_weight, value_weight, proj_weight, up_weight, down_weight, query_shift,
         value_shift, proj_shift, up_shift, down_shift, first_gain, first_shift, second_gain, second_shift, segment_ids,
         cotangent):
    L = LAYERS
    places = segment_ids[: s.tok].reshape(4, 1, s.qc)
    segq = jnp.tile(places, (1, 2, 1)).reshape(4, 2 * s.qc, 1)
    segk = jnp.tile(places, (1, s.nr, 1)).reshape(4, s.nr * s.qc)
    shapes = scratch_of(s)
    square = jax.ShapeDtypeStruct((L, s.dr, s.dc), F32)
    out_shape = (
        jax.ShapeDtypeStruct((s.tok, s.dc), BF16),
        jax.ShapeDtypeStruct((s.tok, s.dc), F32),
        square, square, square, square,
        jax.ShapeDtypeStruct((L, s.dr, s.fc), F32),
        jax.ShapeDtypeStruct((L, s.fr, s.dc), F32),
        jax.ShapeDtypeStruct((L * 2 * VEC_ROWS, s.dc), F32),
    )
    vmem = pl.BlockSpec(memory_space=pltpu.VMEM)
    *arrays, o_vec = pl.pallas_call(
        functools.partial(kernel, s),
        out_shape=out_shape,
        in_specs=[vmem] * len(INPUTS),
        out_specs=[vmem] * len(OUTPUTS),
        scratch_shapes=[pltpu.VMEM(shape, dtype) for shape, dtype in shapes.values()]
        + [pltpu.SemaphoreType.DMA((len(PHASES),))] * 2,
        compiler_params=pltpu.CompilerParams(
            collective_id=0, has_side_effects=True, vmem_limit_bytes=60 * 2**20),
        name="encoder",
    )(layer_input, cotangent, query_weight, key_weight, value_weight, proj_weight, up_weight, down_weight, query_shift,
      value_shift, proj_shift, up_shift, down_shift, first_gain, first_shift, second_gain, second_shift, segq, segk)
    own = o_vec.reshape(L, 2 * VEC_ROWS, s.dc)
    up_rows = s.fc // LANES
    vectors = own[:, VEC_ROWS:]
    return (
        *arrays, own[:, 4], own[:, 5], vectors[:, PROJ_B], own[:, :up_rows].reshape(L, s.fc), vectors[:, DOWN_B],
        vectors[:, GAIN1], vectors[:, SHIFT1], vectors[:, GAIN2], vectors[:, SHIFT2],
    )


def build(mesh, tok, d, ff):
    s = Sizes(mesh.shape["row"], mesh.shape["col"], tok, d, ff)
    return jax.shard_map(
        functools.partial(body, s),
        mesh=mesh,
        in_specs=(P("row", "col"),) + (P(None, "row", "col"),) * 6 + (P(None, "col"),) * 9 + (P(), P("row", "col")),
        out_specs=(P("row", "col"),) * 2 + (P(None, "row", "col"),) * 6 + (P(None, "col"),) * 9,
        check_vma=False,
    )


def solution(mesh):
    return build(mesh, 256, 1024, 4096)
```

```python
import functools
from types import SimpleNamespace

import jax
import jax.numpy as jnp
from jax import lax
from jax.experimental import pallas as pl
from jax.experimental.pallas import tpu as pltpu
from jax.sharding import PartitionSpec as P

MESH = pl.DeviceIdType.MESH
LAYERS = 2
HEAD_DIM = 64
LANES = 128
F32 = jnp.float32
BF16 = jnp.bfloat16
PAIRS = ((0, 0), (1, 1), (1, 2), (2, 1), (2, 2), (2, 3), (3, 2), (3, 3))
KEYS_OF = {i: [(n, j) for n, (a, j) in enumerate(PAIRS) if a == i] for i in range(4)}
QUERIES_OF = {j: [(n, i) for n, (i, b) in enumerate(PAIRS) if b == j] for j in range(4)}

PROJ_B, DOWN_B, GAIN1, SHIFT1, GAIN2, SHIFT2 = range(6)
VEC_ROWS = 8


def dot(a, b):
    return jnp.dot(a, b, preferred_element_type=F32)


def dot_nt(a, b):
    return lax.dot_general(a, b, (((1,), (1,)), ((), ())), preferred_element_type=F32)


def dot_tn(a, b):
    return lax.dot_general(a, b, (((0,), (0,)), ((), ())), preferred_element_type=F32)


class Sizes:
    def __init__(self, nr, nc, tok, d, ff):
        self.nr, self.nc, self.tok, self.d, self.ff = nr, nc, tok, d, ff
        self.half = tok // 2
        self.t = self.half // nc
        self.dc, self.fc = d // nc, ff // nc
        self.dr, self.fr = d // nr, ff // nr
        self.nz = nr // 4
        self.nzx = nr // 2
        self.qc = tok // 4


def scratch_of(s):
    L = LAYERS
    v = {}
    v["xf"] = ((L, 2, s.half, s.d), BF16)
    v["x1"] = ((L, 2, s.half, s.d), BF16)
    v["dff"] = ((L, 2, s.half, s.d), BF16)
    v["drf"] = ((L, 2, s.half, s.d), BF16)
    v["part"] = ((2, s.half, s.d), BF16)
    v["got"] = ((2, s.nc, s.t, s.d), BF16)
    v["got_in"] = ((2, s.nc, s.half, s.dc), BF16)
    v["act_out"] = ((2, s.t, s.d), BF16)
    v["act_in"] = ((2, s.half, s.dc), BF16)
    v["cot"] = ((2, s.t, s.d), BF16)
    v["pv"] = ((L * VEC_ROWS, s.d), F32)
    v["kv"] = ((L, s.nzx, 2, s.tok, 2 * s.dc), BF16)
    v["dkv"] = ((2, s.nzx, 2, s.half, 2 * s.dc), BF16)
    v["dkv_c"] = ((L, 2, s.nzx, s.half, 2 * s.dc), BF16)
    v["dkv_in"] = ((L, 2, s.nzx, s.half, 2 * s.dc), BF16)
    v["probs"] = ((L, len(PAIRS), 2 * s.qc, s.nr * s.qc), BF16)
    v["q2"] = ((L, 4, 2 * s.qc, s.dc), BF16)
    v["do2"] = ((4, 2 * s.qc, s.dc), BF16)
    v["delta"] = ((4, 2 * s.qc, 1), F32)
    v["dq2"] = ((4, 2 * s.qc, s.dc), F32)
    v["att"] = ((L, s.tok, s.dc), F32)
    v["gate"] = ((L, 2, s.half, s.fc), BF16)
    v["slope"] = ((L, 2, s.half, s.fc), F32)
    v["de"] = ((2, s.half, s.fc), BF16)
    v["n1"] = ((L, 2, s.t, s.d), F32)
    v["n2"] = ((L, 2, s.t, s.d), F32)
    v["r1"] = ((L, 2, s.t, 1), F32)
    v["r2"] = ((L, 2, s.t, 1), F32)
    v["carry"] = ((2, s.t, s.d), F32)
    v["dqkv"] = ((s.tok, 3 * s.dc), BF16)
    v["wqkv"] = ((L, s.nzx, 2, s.dr, 3 * s.dc), BF16)
    v["wup"] = ((L, s.nzx, 2, s.dr, s.fc), BF16)
    v["wproj"] = ((L, s.dc, s.d), BF16)
    v["wdown"] = ((L, s.fc, s.d), BF16)
    v["wp_own"] = ((L, s.dr, s.dc), BF16)
    v["wd_own"] = ((L, s.fr, s.dc), BF16)
    v["gqkv"] = ((s.nzx, 2, s.dr, 3 * s.dc), BF16)
    v["gup"] = ((s.nzx, 2, s.dr, s.fc), BF16)
    v["gproj"] = ((s.dc, s.d), BF16)
    v["gdown"] = ((s.fc, s.d), BF16)
    v["gqkv_c"] = ((L, s.nzx, s.dr, 3 * s.dc), BF16)
    v["gup_c"] = ((L, s.nzx, s.dr, s.fc), BF16)
    v["gproj_c"] = ((L, s.dr, s.d), BF16)
    v["gdown_c"] = ((L, s.fr, s.d), BF16)
    v["gqkv_in"] = ((L, s.nzx, s.dr, 3 * s.dc), BF16)
    v["gup_in"] = ((L, s.nzx, s.dr, s.fc), BF16)
    v["gproj_in"] = ((L, s.dr, s.d), BF16)
    for name, shape in (("gq", (s.dr, 3 * s.dc)), ("gp", (s.dr, s.dc)), ("gu", (s.dr, s.fc)), ("gd", (s.fr, s.dc))):
        v[f"t_{name}"] = (shape, F32)
        v[f"t_{name}_out"] = ((L,) + shape, BF16)
        v[f"t_{name}_in"] = ((L,) + shape, BF16)
    v["gdown_in"] = ((L, s.fr, s.d), BF16)
    v["gproj_out"] = ((L, s.dr, s.dc), BF16)
    v["gdown_out"] = ((L, s.fr, s.dc), BF16)
    v["gproj_fin"] = ((L, s.dr, s.dc), BF16)
    v["gdown_fin"] = ((L, s.fr, s.dc), BF16)
    v["vec"] = ((L * VEC_ROWS, s.d), F32)
    v["vec_in"] = ((s.nc, L * VEC_ROWS, s.dc), F32)
    v["own"] = ((L * 2 * VEC_ROWS, s.dc), F32)
    v["own_in"] = ((s.nr, L * 2 * VEC_ROWS, s.dc), F32)
    return v


INPUTS = ("x", "cotan", "wq", "wk", "wv", "wp", "wu", "wd", "qb", "vb", "pb", "upb", "db", "g1", "s1", "g2", "s2", "segq",
          "segk")
OUTPUTS = ("o_act", "o_in", "o_q", "o_k", "o_v", "o_proj", "o_up", "o_down", "o_vec")
ROW_PHASES = ("wq", "wp", "wu", "wd", "kva", "kvb", "dkva", "dkvb", "gq", "gp", "gu", "gd")
PHASES = (
    ["x", "cotan", "pvec", "act", "vec", "own", "wpt", "wdt"]
    + [f"{n}{l}" for l in range(LAYERS) for n in ("gpt", "gdt")]
    + [f"{n}{l}{a}" for l in range(LAYERS) for n in ("pr", "n1", "fr", "h", "df", "dn", "dr", "dx") for a in range(2)]
    + [f"{n}{l}{e}" for l in range(LAYERS) for n in ROW_PHASES
       for e in ("", "c", "x")]
)
IN_STEPS = ("wp0", "wu0", "wd0", "wq1", "wp1", "wu1", "wd1", "gu0", "gd0", "gp0", "gq1", "gp1", "gu1", "gd1")
KV = {"kva": 0, "kvb": 1}
DKV = {"dkva": 0, "dkvb": 1}
PHASE = {name: index for index, name in enumerate(PHASES)}


def kernel(s, *refs):
    names = INPUTS + OUTPUTS + tuple(scratch_of(s)) + ("send", "recv")
    m = SimpleNamespace(**dict(zip(names, refs)))
    L = LAYERS
    r, c = lax.axis_index("row"), lax.axis_index("col")
    zx, k = lax.div(r, 2), lax.rem(r, 2)
    z, x = lax.div(zx, 2), lax.rem(zx, 2)
    across = z * 2 + 1 - x
    other = zx * 2 + 1 - k
    at_home = zx == c
    chips, few = s.nzx - 1, s.nc - 1

    def remote(src, dst, phase, row, col):
        return pltpu.make_async_remote_copy(
            src_ref=src, dst_ref=dst, send_sem=m.send.at[PHASE[phase]], recv_sem=m.recv.at[PHASE[phase]],
            device_id=(row, col), device_id_type=MESH)

    def wait(sems, phase, ref):
        pltpu.make_async_copy(ref, ref, sems.at[PHASE[phase]]).wait()

    def each_col(fn):
        def step(q, carry):
            fn(lax.rem(c + q, s.nc))
            return carry
        lax.fori_loop(1, s.nc, step, 0)

    def each_row(fn):
        def step(q, carry):
            fn(lax.rem(r + q, s.nr))
            return carry
        lax.fori_loop(1, s.nr, step, 0)

    def each_chip(fn):
        def step(q, carry):
            fn(lax.rem(zx + q, s.nzx))
            return carry
        lax.fori_loop(1, s.nzx, step, 0)

    def each_z(fn):
        def step(q, carry):
            fn(lax.rem(z + q, s.nz))
            return carry
        lax.fori_loop(1, s.nz, step, 0)

    def rows(i, n):
        return pl.ds(pl.multiple_of(i * n, n), n)

    barrier = pltpu.get_barrier_semaphore()

    def greet(row, col):
        pl.semaphore_signal(barrier, inc=1, device_id=(row, col), device_id_type=MESH)

    swap_row, swap_col = c * 2 + k, zx
    each_col(lambda cc: greet(r, cc))
    each_row(lambda rr: greet(rr, c))

    @pl.when(jnp.logical_not(at_home))
    def _():
        greet(swap_row, swap_col)

    def weight(name, l):
        chips = s.nzx - (2 if f"{name}{l}" in IN_STEPS else 1)
        if name in KV:
            span = pl.ds(KV[name] * s.half, s.half)
            return ((lambda i, kk: m.kv.at[l, i, kk, span]), (lambda kk: m.kv.at[l, :, kk, span]),
                    m.kv.at[l, pl.ds(0, chips), 0, span] if chips else None)
        if name in ("wq", "wu"):
            ref = {"wq": m.wqkv, "wu": m.wup}[name]
            return (lambda i, kk: ref.at[l, i, kk]), (lambda kk: ref.at[l, :, kk]), \
                ref.at[l, pl.ds(0, chips), 0] if chips else None
        ref, n = {"wp": (m.wproj, s.dr), "wd": (m.wdown, s.fr)}[name]
        return ((lambda i, kk: ref.at[l, rows(kk, n), rows(i, s.dc)]), (lambda kk: ref.at[l, rows(kk, n)]),
                ref.at[l, pl.ds(0, n), pl.ds(0, chips * s.dc)] if chips else None)

    def gather(name, l):
        piece = weight(name, l)[0](zx, k)
        if f"{name}{l}" not in IN_STEPS:
            each_chip(lambda i: remote(piece, piece, f"{name}{l}", i * 2 + k, c).start())
            return
        remote(piece, piece, f"{name}{l}x", across * 2 + k, c).start()
        each_z(lambda i: remote(piece, piece, f"{name}{l}", (i * 2 + x) * 2 + k, c).start())

    def forward(name, l):
        piece = weight(name, l)[0](across, k)
        wait(m.recv, f"{name}{l}x", piece)
        each_z(lambda i: remote(piece, piece, f"{name}{l}", (i * 2 + x) * 2 + k, c).start())

    def pass_on(name, l):
        _, half, many = weight(name, l)
        if many is not None:
            wait(m.recv, f"{name}{l}", many)
        remote(half(k), half(k), f"{name}{l}c", other, c).start()

    def gathered(name, l):
        wait(m.recv, f"{name}{l}c", weight(name, l)[1](1 - k))

    def sent_gather(name, l):
        piece, half, many = weight(name, l)
        if many is not None:
            wait(m.send, f"{name}{l}", many)
        if f"{name}{l}" in IN_STEPS:
            wait(m.send, f"{name}{l}x", piece(zx, k))
        wait(m.send, f"{name}{l}c", half(k))

    def partial_sum(name, l):
        if name in DKV:
            a = DKV[name]
            mid, got = m.dkv_c.at[l, a], m.dkv_in.at[l, a]
            return (lambda kk: m.dkv.at[a, :, kk]), mid, (lambda i: mid.at[i]), got
        if name in ("gq", "gu"):
            full, mid, got = {"gq": (m.gqkv, m.gqkv_c.at[l], m.gqkv_in.at[l]),
                              "gu": (m.gup, m.gup_c.at[l], m.gup_in.at[l])}[name]
            return (lambda kk: full.at[:, kk]), mid, (lambda i: mid.at[i]), got
        full, mid, got, n = {"gp": (m.gproj, m.gproj_c.at[l], m.gproj_in.at[l], s.dr),
                             "gd": (m.gdown, m.gdown_c.at[l], m.gdown_in.at[l], s.fr)}[name]
        return (lambda kk: full.at[rows(kk, n)]), mid, (lambda i: mid.at[:, rows(i, s.dc)]), got

    def reduce_start(name, l):
        half, mid, _, _ = partial_sum(name, l)
        remote(half(1 - k), mid, f"{name}{l}c", other, c).start()

    def both(name, mid, i):
        if name in ("gp", "gd"):
            return mid.at[:, rows(i, 2 * s.dc)]
        return mid.at[pl.ds(2 * i, 2)]

    def m_pair(name, got, i):
        if name in ("gp", "gd"):
            return got.at[:, rows(i, 2 * s.dc)]
        return got.at[pl.ds(2 * i, 2)]

    def reduce_turn(name, l):
        _, mid, piece, got = partial_sum(name, l)
        if s.nz > 1:
            wait(m.recv, f"{name}{l}", m_all(name, got))
        sums = []
        for which in (x, 1 - x):
            total = piece(z * 2 + which)[...].astype(F32)
            for q in range(1, s.nz):
                i = lax.rem(z + q, s.nz) * 2 + which
                arrived = got[:, rows(i, s.dc)] if name in ("gp", "gd") else got[i]
                total = total + arrived.astype(F32)
            sums.append(total)
        kept, out, back = turned(name, l)
        kept[...] = sums[0]
        out[...] = sums[1].astype(BF16)
        remote(out, back, f"{name}{l}x", across * 2 + k, c).start()

    def turned(name, l):
        return {"gq": (m.t_gq, m.t_gq_out.at[l], m.t_gq_in.at[l]), "gp": (m.t_gp, m.t_gp_out.at[l], m.t_gp_in.at[l]),
                "gu": (m.t_gu, m.t_gu_out.at[l], m.t_gu_in.at[l]), "gd": (m.t_gd, m.t_gd_out.at[l], m.t_gd_in.at[l])}[name]

    def m_all(name, got):
        if name in ("gp", "gd"):
            return got.at[:, pl.ds(0, 2 * (s.nz - 1) * s.dc)]
        return got.at[pl.ds(0, 2 * (s.nz - 1))]

    def reduce_mid(name, l):
        half, mid, piece, got = partial_sum(name, l)
        wait(m.recv, f"{name}{l}c", mid)
        mid[...] = (half(k)[...].astype(F32) + mid[...].astype(F32)).astype(BF16)
        if f"{name}{l}" in IN_STEPS:
            each_z(lambda i: remote(both(name, mid, i), m_pair(name, got, z), f"{name}{l}", (i * 2 + x) * 2 + k, c).start())
            return
        each_chip(lambda i: remote(piece(i), got.at[zx], f"{name}{l}", i * 2 + k, c).start())
        got[zx] = piece(zx)[...]

    def reduce_end(name, l):
        if f"{name}{l}" in IN_STEPS:
            kept, _, back = turned(name, l)
            wait(m.recv, f"{name}{l}x", back)
            return kept[...] + back[...].astype(F32)
        got = partial_sum(name, l)[3]
        wait(m.recv, f"{name}{l}", got.at[pl.ds(0, chips)])
        total = got[0].astype(F32)
        for i in range(1, s.nzx):
            total = total + got[i].astype(F32)
        return total

    def sent_half(name, l):
        wait(m.send, f"{name}{l}c", partial_sum(name, l)[1])

    def sent_pieces(name, l):
        if f"{name}{l}" in IN_STEPS:
            if s.nz > 1:
                wait(m.send, f"{name}{l}", m_all(name, partial_sum(name, l)[3]))
            wait(m.send, f"{name}{l}x", turned(name, l)[1])
            return
        wait(m.send, f"{name}{l}", partial_sum(name, l)[3].at[pl.ds(0, chips)])

    m.xf[0, :, :, rows(c, s.dc)] = m.x[...]
    m.cot[:, :, rows(c, s.dc)] = m.cotan[:, rows(c, s.t), :]
    m.pv[:, rows(c, s.dc)] = jnp.zeros((L * VEC_ROWS, s.dc), F32)
    for l in range(L):
        for which, ref in enumerate((m.pb, m.db, m.g1, m.s1, m.g2, m.s2)):
            m.pv[l * VEC_ROWS + which : l * VEC_ROWS + which + 1, rows(c, s.dc)] = ref[l : l + 1, :].astype(F32)
        for which, ref in enumerate((m.wq, m.wk, m.wv)):
            m.wqkv[l, zx, k, :, which * s.dc : (which + 1) * s.dc] = ref[l]
        m.wup[l, zx, k] = m.wu[l]

    pl.semaphore_wait(barrier, s.nc - 1 + s.nr - 1 + 1 - at_home.astype(jnp.int32))

    gather("wq", 0)
    each_col(lambda cc: remote(m.x, m.xf.at[0, :, :, rows(c, s.dc)], "x", r, cc).start())

    @pl.when(jnp.logical_not(at_home))
    def _():
        remote(m.wp, m.wp_own, "wpt", swap_row, swap_col).start()
        remote(m.wd, m.wd_own, "wdt", swap_row, swap_col).start()
    mine = m.pv.at[:, rows(c, s.dc)]
    each_col(lambda cc: remote(mine, mine, "pvec", r, cc).start())
    each_col(lambda cc: remote(
        m.cotan.at[:, rows(cc, s.t)], m.cot.at[:, :, rows(c, s.dc)], "cotan", r, cc).start())
    m.vec[...] = jnp.zeros(m.vec.shape, F32)
    m.own[...] = jnp.zeros(m.own.shape, F32)

    def vector(l, which):
        return m.pv[l * VEC_ROWS + which : l * VEC_ROWS + which + 1, :]

    def share(buf, value, phase):
        buf[rows(c, s.t), :] = value
        each_col(lambda cc: remote(buf.at[rows(c, s.t)], buf.at[rows(c, s.t)], phase, r, cc).start())

    def shared(buf, phase):
        for sems in (m.recv, m.send):
            wait(sems, phase, buf.at[pl.ds(0, few * s.t)])

    def scatter(a, value, phase):
        m.part[a] = value.astype(BF16)
        each_col(lambda cc: remote(m.part.at[a, rows(cc, s.t)], m.got.at[a, c], phase, r, cc).start())
        m.got[a, c] = m.part[a, rows(c, s.t), :]

    def scattered(a, phase):
        for sems in (m.recv, m.send):
            wait(sems, phase, m.got.at[a, pl.ds(0, few)])
        total = m.got[a, 0].astype(F32)
        for i in range(1, s.nc):
            total = total + m.got[a, i].astype(F32)
        return total

    def norm(u, l, a, gain, shift, n_ref, r_ref):
        mean = jnp.sum(u, axis=1, keepdims=True) / s.d
        var = jnp.sum(u * u, axis=1, keepdims=True) / s.d - mean * mean
        inv = lax.rsqrt(var + 1e-12)
        n = (u - mean) * inv
        n_ref[l, a] = n
        r_ref[l, a] = inv
        return n * vector(l, gain) + vector(l, shift)

    def add_row(ref, at, value):
        ref[at : at + 1, :] += jnp.sum(value, axis=0, keepdims=True)

    def norm_back(g, l, a, gain, shift, n_ref, r_ref):
        n = n_ref[l, a]
        w = g * vector(l, gain)
        first = jnp.sum(w, axis=1, keepdims=True) / s.d
        second = jnp.sum(w * n, axis=1, keepdims=True) / s.d
        add_row(m.vec, l * VEC_ROWS + gain, g * n)
        add_row(m.vec, l * VEC_ROWS + shift, g)
        return r_ref[l, a] * (w - first - n * second)

    low_lanes = lax.broadcasted_iota(jnp.int32, (s.qc, s.dc), 1) < HEAD_DIM

    def two_heads(block):
        block = block.astype(F32)
        return jnp.concatenate([jnp.where(low_lanes, block, 0.0), jnp.where(low_lanes, 0.0, block)], axis=0)

    def one_block(pair):
        return jnp.where(low_lanes, pair[: s.qc], pair[s.qc :])

    def keys(l, j, value):
        lanes = pl.ds(s.dc if value else 0, s.dc)
        return m.kv[l, :, :, pl.ds(j * s.qc, s.qc), lanes].reshape(s.nr * s.qc, s.dc)

    def swapped(l):
        m.wproj[l, rows(k, s.dr), rows(zx, s.dc)] = m.wp_own[l]
        m.wdown[l, rows(k, s.fr), rows(zx, s.dc)] = m.wd_own[l]

    pass_on("wq", 0)
    wait(m.recv, "x", m.xf.at[0, :, :, pl.ds(0, few * s.dc)])
    wait(m.recv, "pvec", m.pv.at[:, pl.ds(0, few * s.dc)])

    @pl.when(at_home)
    def _():
        m.wp_own[...] = m.wp[...]
        m.wd_own[...] = m.wd[...]

    @pl.when(jnp.logical_not(at_home))
    def _():
        wait(m.recv, "wpt", m.wp_own)
        wait(m.recv, "wdt", m.wd_own)
    swapped(0)

    def attend(l, i):
        queries = m.q2[l, i]
        ids = m.segq[i]
        scores = []
        for _, j in KEYS_OF[i]:
            raw = dot_nt(queries, keys(l, j, False))
            scores.append(jnp.where(ids == m.segk[j : j + 1, :], raw, -1e9))
        top = functools.reduce(jnp.maximum, [jnp.max(x, axis=1, keepdims=True) for x in scores])
        raised = [jnp.exp(x - top) for x in scores]
        inverse = 1.0 / sum(jnp.sum(x, axis=1, keepdims=True) for x in raised)
        out = jnp.zeros((2 * s.qc, s.dc), F32)
        for (n, j), x in zip(KEYS_OF[i], raised):
            prob = (x * inverse).astype(BF16)
            m.probs[l, n] = prob
            out = out + dot(prob, keys(l, j, True))
        m.att[l, i * s.qc : (i + 1) * s.qc, :] = one_block(out)

    def span(a):
        return pl.ds(a * s.half, s.half)

    for l in range(L):
        for a in range(2):
            if l:
                shared(m.xf.at[l, a], f"h{l - 1}{a}")
            elif a == 0:
                gathered("wq", 0)
                for b in range(2):
                    m.carry[b] = m.xf[0, b, rows(c, s.t), :].astype(F32)
            if l and a == 0:
                gathered("wq", l)
            qkv = dot(m.xf[l, a], m.wqkv[l].reshape(s.d, 3 * s.dc))
            keep = (qkv[:, 2 * s.dc :] + m.vb[l : l + 1, :].astype(F32)).astype(BF16)
            m.kv[l, zx, k, span(a), : s.dc] = qkv[:, s.dc : 2 * s.dc].astype(BF16)
            m.kv[l, zx, k, span(a), s.dc :] = keep
            gather("kva" if a == 0 else "kvb", l)
            for i in range(2):
                block = (qkv[i * s.qc : (i + 1) * s.qc, : s.dc] + m.qb[l : l + 1, :].astype(F32)).astype(BF16)
                m.q2[l, 2 * a + i] = (two_heads(block) * HEAD_DIM ** (-0.5)).astype(BF16)
        if l == 0:
            gather("wp", 0)
        if l == 0:
            forward("wp", 0)
        pass_on("kva", l)
        pass_on("kvb", l)
        if l == 0:
            gather("wu", 0)
            gather("wd", 0)
            pass_on("wp", 0)
        else:
            pass_on("wu", 1)
            pass_on("wd", 1)
        gathered("kva", l)
        attend(l, 0)
        gathered("kvb", l)
        attend(l, 1)
        gathered("wp", l)
        scatter(0, dot(m.att[l, span(0), :].astype(BF16), m.wproj[l]), f"pr{l}0")
        attend(l, 2)
        attend(l, 3)
        scatter(1, dot(m.att[l, span(1), :].astype(BF16), m.wproj[l]), f"pr{l}1")
        if l == 0:
            forward("wu", 0)
            forward("wd", 0)
            swapped(1)
        for a in range(2):
            u = scattered(a, f"pr{l}{a}") + vector(l, PROJ_B) + m.carry[a]
            first_out = norm(u, l, a, GAIN1, SHIFT1, m.n1, m.r1)
            share(m.x1.at[l, a], first_out.astype(BF16), f"n1{l}{a}")
            m.carry[a] = first_out
        if l == 0:
            pass_on("wu", 0)
            pass_on("wd", 0)
            gather("wq", 1)
            gather("wp", 1)
        gathered("wu", l)
        for a in range(2):
            shared(m.x1.at[l, a], f"n1{l}{a}")
            pre = dot(m.x1[l, a], m.wup[l].reshape(s.d, s.fc)) + m.upb[l : l + 1, :].astype(F32)
            cdf = 0.5 * (1.0 + lax.erf(pre * 0.5**0.5))
            m.gate[l, a] = (pre * cdf).astype(BF16)
            if a == 0:
                gathered("wd", l)
            scatter(a, dot(m.gate[l, a], m.wdown[l]), f"fr{l}{a}")
            m.slope[l, a] = cdf + pre * (jnp.exp(-0.5 * pre * pre) * 0.3989422804014327)
        if l == 0:
            forward("wq", 1)
            forward("wp", 1)
            gather("wu", 1)
            gather("wd", 1)
        for a in range(2):
            u = scattered(a, f"fr{l}{a}") + vector(l, DOWN_B) + m.carry[a]
            hidden = norm(u, l, a, GAIN2, SHIFT2, m.n2, m.r2)
            if l == 0:
                share(m.xf.at[1, a], hidden.astype(BF16), f"h0{a}")
                m.carry[a] = hidden
            else:
                m.act_out[a] = hidden.astype(BF16)
        if l == 0:
            pass_on("wq", 1)
            pass_on("wp", 1)
            forward("wu", 1)
            forward("wd", 1)

    def swap_back(l, name, total):
        out, fin, phase = {"gp": (m.gproj_out, m.gproj_fin, f"gpt{l}"), "gd": (m.gdown_out, m.gdown_fin, f"gdt{l}")}[name]
        out[l] = total.astype(BF16)

        @pl.when(jnp.logical_not(at_home))
        def _():
            remote(out.at[l], fin.at[l], phase, swap_row, swap_col).start()

        @pl.when(at_home)
        def _():
            fin[l] = out[l]

    def swap_end(l, name, out):
        fin, phase = {"gp": (m.gproj_fin, f"gpt{l}"), "gd": (m.gdown_fin, f"gdt{l}")}[name]

        @pl.when(jnp.logical_not(at_home))
        def _():
            wait(m.recv, phase, fin.at[l])
        out[l] = fin[l].astype(F32)

    def attend_back(l, j):
        key_grad = jnp.zeros((s.nr * s.qc, s.dc), F32)
        value_grad = jnp.zeros((s.nr * s.qc, s.dc), F32)
        for n, i in QUERIES_OF[j]:
            prob = m.probs[l, n]
            prob_grad = dot_nt(m.do2[i], keys(l, j, True))
            score_grad = (prob.astype(F32) * (prob_grad - m.delta[i])).astype(BF16)
            m.dq2[i] += dot(score_grad, keys(l, j, False))
            key_grad = key_grad + dot_tn(score_grad, m.q2[l, i])
            value_grad = value_grad + dot_tn(prob, m.do2[i])
        shape = (s.nzx, 2, s.qc, s.dc)
        place = pl.ds(j % 2 * s.qc, s.qc)
        m.dkv[j // 2, :, :, place, pl.ds(0, s.dc)] = key_grad.astype(BF16).reshape(shape)
        m.dkv[j // 2, :, :, place, pl.ds(s.dc, s.dc)] = value_grad.astype(BF16).reshape(shape)

    wait(m.recv, "cotan", m.cot.at[:, :, pl.ds(0, few * s.dc)])
    for l in reversed(range(L)):
        at = l * VEC_ROWS
        own = l * 2 * VEC_ROWS
        for a in range(2):
            if l + 1 < L:
                grad = scattered(a, f"dx{l + 1}{a}") + m.carry[a]
            else:
                grad = m.cot[a].astype(F32)
            dz = norm_back(grad, l, a, GAIN2, SHIFT2, m.n2, m.r2)
            m.carry[a] = dz
            low = dz.astype(BF16)
            share(m.dff.at[l, a], low, f"df{l}{a}")
            add_row(m.vec, at + DOWN_B, low.astype(F32))
        if l + 1 == L:
            each_col(lambda cc: remote(
                m.act_out.at[:, :, rows(cc, s.dc)], m.act_in.at[:, rows(c, s.t)], "act", r, cc).start())
            m.act_in[:, rows(c, s.t), :] = m.act_out[:, :, rows(c, s.dc)]
        else:
            reduce_mid("gq", l + 1)
            reduce_turn("gp", l + 1)
        for a in range(2):
            shared(m.dff.at[l, a], f"df{l}{a}")
            de = (dot_nt(m.dff[l, a], m.wdown[l]) * m.slope[l, a]).astype(BF16)
            m.de[a] = de
            scatter(a, dot_nt(de, m.wup[l].reshape(s.d, s.fc)), f"dn{l}{a}")
            sums = jnp.sum(de.astype(F32), axis=0, keepdims=True)
            for i in range(s.fc // LANES):
                m.own[own + i : own + i + 1, :] += sums[:, i * LANES : (i + 1) * LANES]
        if l + 1 < L:
            reduce_turn("gq", l + 1)
            swap_back(l + 1, "gp", reduce_end("gp", l + 1))
            sent_half("gd", l + 1)
            sent_half("gu", l + 1)
        m.gdown[...] = dot_tn(m.gate[l].reshape(s.tok, s.fc), m.dff[l].reshape(s.tok, s.d)).astype(BF16)
        reduce_start("gd", l)
        for a in range(2):
            grad = scattered(a, f"dn{l}{a}") + m.carry[a]
            du = norm_back(grad, l, a, GAIN1, SHIFT1, m.n1, m.r1)
            m.carry[a] = du
            low = du.astype(BF16)
            share(m.drf.at[l, a], low, f"dr{l}{a}")
            add_row(m.vec, at + PROJ_B, low.astype(F32))
        m.gup[...] = dot_tn(m.x1[l].reshape(s.tok, s.d), m.de[...].reshape(s.tok, s.fc)).astype(BF16).reshape(m.gup.shape)
        reduce_start("gu", l)
        reduce_mid("gd", l)
        if l == 0:
            each_col(lambda cc: remote(m.vec.at[:, rows(cc, s.dc)], m.vec_in.at[c], "vec", r, cc).start())
            m.vec_in[c] = m.vec[:, rows(c, s.dc)]
        if l + 1 < L:
            sent_half("dkva", l + 1)
            sent_half("dkvb", l + 1)
        for a in range(2):
            shared(m.drf.at[l, a], f"dr{l}{a}")
            dout = dot_nt(m.drf[l, a], m.wproj[l]).astype(BF16)
            for b in range(2):
                i = 2 * a + b
                block = two_heads(dout[b * s.qc : (b + 1) * s.qc, :])
                kept = m.att[l, i * s.qc : (i + 1) * s.qc, :]
                m.do2[i] = block.astype(BF16)
                m.delta[i] = jnp.sum(block * jnp.concatenate([kept, kept], axis=0), axis=1, keepdims=True)
                m.dq2[i] = jnp.zeros((2 * s.qc, s.dc), F32)
            if a == 0:
                attend_back(l, 0)
                reduce_mid("gu", l)
        attend_back(l, 1)
        reduce_start("dkva", l)
        attend_back(l, 2)
        reduce_mid("dkva", l)
        attend_back(l, 3)
        reduce_start("dkvb", l)
        for i in range(4):
            m.dqkv[i * s.qc : (i + 1) * s.qc, : s.dc] = (one_block(m.dq2[i]) * HEAD_DIM ** (-0.5)).astype(BF16)
        reduce_mid("dkvb", l)
        reduce_turn("gd", l)
        if l + 1 < L:
            sent_half("gp", l + 1)
            sent_half("gq", l + 1)
        m.gproj[...] = dot_tn(m.att[l].astype(BF16), m.drf[l].reshape(s.tok, s.d)).astype(BF16)
        reduce_start("gp", l)
        reduce_turn("gu", l)
        if l == 0:
            wait(m.recv, "vec", m.vec_in.at[pl.ds(0, few)])
            total = m.vec_in[0]
            for i in range(1, s.nc):
                total = total + m.vec_in[i]
            for i in range(L):
                to = i * 2 * VEC_ROWS + VEC_ROWS
                m.own[to : to + VEC_ROWS, :] = total[i * VEC_ROWS : (i + 1) * VEC_ROWS]
        for a in range(2):
            m.dqkv[span(a), s.dc :] = reduce_end("dkva" if a == 0 else "dkvb", l).astype(BF16)
            back = dot_nt(m.dqkv[span(a), :], m.wqkv[l].reshape(s.d, 3 * s.dc))
            if l:
                scatter(a, back, f"dx{l}{a}")
            else:
                m.part[a] = back.astype(BF16)
                mine = m.part[a, rows(c, s.t), :].astype(F32) + m.carry[a]
                m.part[a, rows(c, s.t), :] = mine.astype(BF16)
                each_col(lambda cc: remote(m.part.at[a, :, rows(cc, s.dc)], m.got_in.at[a, c], f"dx0{a}", r, cc).start())
                m.got_in[a, c] = m.part[a, :, rows(c, s.dc)]
        m.gqkv[...] = dot_tn(m.xf[l].reshape(s.tok, s.d), m.dqkv[...]).astype(BF16).reshape(m.gqkv.shape)
        reduce_start("gq", l)
        sums = jnp.sum(m.dqkv[...].astype(F32), axis=0, keepdims=True)
        m.own[own + 4 : own + 5, :] = sums[:, : s.dc]
        m.own[own + 5 : own + 6, :] = sums[:, 2 * s.dc :]
        reduce_mid("gp", l)
        swap_back(l, "gd", reduce_end("gd", l))
        m.o_up[l] = reduce_end("gu", l)
        if l + 1 < L:
            swap_end(l + 1, "gd", m.o_down)
            swap_end(l + 1, "gp", m.o_proj)
            total = reduce_end("gq", l + 1)
            for which, out in enumerate((m.o_q, m.o_k, m.o_v)):
                out[l + 1] = total[:, which * s.dc : (which + 1) * s.dc]

    m.own_in[r] = m.own[...]
    each_row(lambda rr: remote(m.own, m.own_in.at[r], "own", rr, c).start())
    reduce_mid("gq", 0)
    reduce_turn("gp", 0)
    swap_end(0, "gd", m.o_down)
    wait(m.recv, "act", m.act_in.at[:, pl.ds(0, few * s.t)])
    m.o_act[...] = m.act_in[...]
    for a in range(2):
        wait(m.recv, f"dx0{a}", m.got_in.at[a, pl.ds(0, few)])
        total = m.got_in[a, 0].astype(F32)
        for i in range(1, s.nc):
            total = total + m.got_in[a, i].astype(F32)
        m.o_in[a] = total
    swap_back(0, "gp", reduce_end("gp", 0))
    wait(m.recv, "own", m.own_in.at[pl.ds(0, s.nr - 1)])
    total = m.own_in[0]
    for i in range(1, s.nr):
        total = total + m.own_in[i]
    m.o_vec[...] = total
    total = reduce_end("gq", 0)
    for which, out in enumerate((m.o_q, m.o_k, m.o_v)):
        out[0] = total[:, which * s.dc : (which + 1) * s.dc]
    swap_end(0, "gp", m.o_proj)

    wait(m.send, "x", m.xf.at[0, :, :, pl.ds(0, few * s.dc)])
    wait(m.send, "pvec", m.pv.at[:, pl.ds(0, few * s.dc)])
    wait(m.send, "cotan", m.cot.at[:, :, pl.ds(0, few * s.dc)])
    wait(m.send, "act", m.act_in.at[:, pl.ds(0, few * s.t)])
    for a in range(2):
        wait(m.send, f"dx0{a}", m.got_in.at[a, pl.ds(0, few)])
    wait(m.send, "vec", m.vec_in.at[pl.ds(0, few)])
    wait(m.send, "own", m.own_in.at[pl.ds(0, s.nr - 1)])

    @pl.when(jnp.logical_not(at_home))
    def _():
        wait(m.send, "wpt", m.wp_own)
        wait(m.send, "wdt", m.wd_own)
        for l in range(L):
            wait(m.send, f"gpt{l}", m.gproj_fin.at[l])
            wait(m.send, f"gdt{l}", m.gdown_fin.at[l])
    for l in range(L):
        for name in ("wq", "wp", "wu", "wd", "kva", "kvb"):
            sent_gather(name, l)
        for name in ("gq", "gp", "gu", "gd", "dkva", "dkvb"):
            sent_pieces(name, l)
    for name in ("gq", "gp", "gu", "gd", "dkva", "dkvb"):
        sent_half(name, 0)


def body(s, layer_input, query_weight, key_weight, value_weight, proj_weight, up_weight, down_weight, query_shift,
         value_shift, proj_shift, up_shift, down_shift, first_gain, first_shift, second_gain, second_shift, segment_ids,
         cotangent):
    L = LAYERS
    places = segment_ids[: s.tok].reshape(4, 1, s.qc)
    segq = jnp.tile(places, (1, 2, 1)).reshape(4, 2 * s.qc, 1)
    segk = jnp.tile(places, (1, s.nr, 1)).reshape(4, s.nr * s.qc)
    shapes = scratch_of(s)
    halves = (2, s.half, s.dc)
    square = jax.ShapeDtypeStruct((L, s.dr, s.dc), F32)
    out_shape = (
        jax.ShapeDtypeStruct((2, s.half, s.dc), BF16),
        jax.ShapeDtypeStruct((2, s.half, s.dc), F32),
        square, square, square, square,
        jax.ShapeDtypeStruct((L, s.dr, s.fc), F32),
        jax.ShapeDtypeStruct((L, s.fr, s.dc), F32),
        jax.ShapeDtypeStruct((L * 2 * VEC_ROWS, s.dc), F32),
    )
    vmem = pl.BlockSpec(memory_space=pltpu.VMEM)
    o_act, o_in, *arrays, o_vec = pl.pallas_call(
        functools.partial(kernel, s),
        out_shape=out_shape,
        in_specs=[vmem] * len(INPUTS),
        out_specs=[vmem] * len(OUTPUTS),
        scratch_shapes=[pltpu.VMEM(shape, dtype) for shape, dtype in shapes.values()]
        + [pltpu.SemaphoreType.DMA((len(PHASES),))] * 2,
        compiler_params=pltpu.CompilerParams(
            collective_id=0, has_side_effects=True, vmem_limit_bytes=60 * 2**20),
        name="encoder",
    )(layer_input.reshape(halves), cotangent.reshape(halves), query_weight, key_weight, value_weight, proj_weight, up_weight, down_weight, query_shift,
      value_shift, proj_shift, up_shift, down_shift, first_gain, first_shift, second_gain, second_shift, segq, segk)
    own = o_vec.reshape(L, 2 * VEC_ROWS, s.dc)
    up_rows = s.fc // LANES
    vectors = own[:, VEC_ROWS:]
    return (
        o_act.reshape(s.tok, s.dc), o_in.reshape(s.tok, s.dc), *arrays, own[:, 4], own[:, 5], vectors[:, PROJ_B], own[:, :up_rows].reshape(L, s.fc), vectors[:, DOWN_B],
        vectors[:, GAIN1], vectors[:, SHIFT1], vectors[:, GAIN2], vectors[:, SHIFT2],
    )


def build(mesh, tok, d, ff):
    s = Sizes(mesh.shape["row"], mesh.shape["col"], tok, d, ff)
    return jax.shard_map(
        functools.partial(body, s),
        mesh=mesh,
        in_specs=(P("row", "col"),) + (P(None, "row", "col"),) * 6 + (P(None, "col"),) * 9 + (P(), P("row", "col")),
        out_specs=(P("row", "col"),) * 2 + (P(None, "row", "col"),) * 6 + (P(None, "col"),) * 9,
        check_vma=False,
    )


def solution(mesh):
    return build(mesh, 256, 1024, 4096)
```

```python
import functools
from types import SimpleNamespace

import jax
import jax.numpy as jnp
from jax import lax
from jax.experimental import pallas as pl
from jax.experimental.pallas import tpu as pltpu
from jax.sharding import PartitionSpec as P

MESH = pl.DeviceIdType.MESH
LAYERS = 2
HEAD_DIM = 64
LANES = 128
F32 = jnp.float32
BF16 = jnp.bfloat16
PAIRS = ((0, 0), (1, 1), (1, 2), (2, 1), (2, 2), (2, 3), (3, 2), (3, 3))
KEYS_OF = {i: [(n, j) for n, (a, j) in enumerate(PAIRS) if a == i] for i in range(4)}
QUERIES_OF = {j: [(n, i) for n, (i, b) in enumerate(PAIRS) if b == j] for j in range(4)}

PROJ_B, DOWN_B, GAIN1, SHIFT1, GAIN2, SHIFT2 = range(6)
VEC_ROWS = 8


def dot(a, b):
    return jnp.dot(a, b, preferred_element_type=F32)


def dot_nt(a, b):
    return lax.dot_general(a, b, (((1,), (1,)), ((), ())), preferred_element_type=F32)


def dot_tn(a, b):
    return lax.dot_general(a, b, (((0,), (0,)), ((), ())), preferred_element_type=F32)


class Sizes:
    def __init__(self, nr, nc, tok, d, ff):
        self.nr, self.nc, self.tok, self.d, self.ff = nr, nc, tok, d, ff
        self.half = tok // 2
        self.t = self.half // nc
        self.dc, self.fc = d // nc, ff // nc
        self.dr, self.fr = d // nr, ff // nr
        self.nz = nr // 4
        self.nzx = nr // 2
        self.qc = tok // 4


def scratch_of(s):
    L = LAYERS
    v = SimpleNamespace()
    v.xf = ((L, 2, s.half, s.d), BF16)
    v.x1 = ((L, 2, s.half, s.d), BF16)
    v.dff = ((L, 2, s.half, s.d), BF16)
    v.drf = ((L, 2, s.half, s.d), BF16)
    v.part = ((2, s.half, s.d), BF16)
    v.got = ((2, s.nc, s.t, s.d), BF16)
    v.got_in = ((2, s.nc, s.half, s.dc), BF16)
    v.act_out = ((2, s.t, s.d), BF16)
    v.act_in = ((2, s.half, s.dc), BF16)
    v.cot = ((2, s.t, s.d), BF16)
    v.pv = ((L * VEC_ROWS, s.d), F32)
    v.kv = ((L, s.nzx, 2, s.tok, 2 * s.dc), BF16)
    v.dkv = ((2, s.nzx, 2, s.half, 2 * s.dc), BF16)
    v.dkv_c = ((L, 2, s.nzx, s.half, 2 * s.dc), BF16)
    v.dkv_in = ((L, 2, s.nzx, s.half, 2 * s.dc), BF16)
    v.probs = ((L, len(PAIRS), 2 * s.qc, s.nr * s.qc), BF16)
    v.q2 = ((L, 4, 2 * s.qc, s.dc), BF16)
    v.do2 = ((4, 2 * s.qc, s.dc), BF16)
    v.delta = ((4, 2 * s.qc, 1), F32)
    v.dq2 = ((4, 2 * s.qc, s.dc), F32)
    v.att = ((L, s.tok, s.dc), F32)
    v.gate = ((L, 2, s.half, s.fc), BF16)
    v.slope = ((L, 2, s.half, s.fc), F32)
    v.de = ((2, s.half, s.fc), BF16)
    v.n1 = ((L, 2, s.t, s.d), F32)
    v.n2 = ((L, 2, s.t, s.d), F32)
    v.r1 = ((L, 2, s.t, 1), F32)
    v.r2 = ((L, 2, s.t, 1), F32)
    v.carry = ((2, s.t, s.d), F32)
    v.dqkv = ((s.tok, 3 * s.dc), BF16)
    v.wqkv = ((L, s.nzx, 2, s.dr, 3 * s.dc), BF16)
    v.wup = ((L, s.nzx, 2, s.dr, s.fc), BF16)
    v.wproj = ((L, s.dc, s.d), BF16)
    v.wdown = ((L, s.fc, s.d), BF16)
    v.wp_own = ((L, s.dr, s.dc), BF16)
    v.wd_own = ((L, s.fr, s.dc), BF16)
    v.gqkv = ((s.nzx, 2, s.dr, 3 * s.dc), BF16)
    v.gup = ((s.nzx, 2, s.dr, s.fc), BF16)
    v.gproj = ((s.dc, s.d), BF16)
    v.gdown = ((s.fc, s.d), BF16)
    v.gqkv_c = ((L, s.nzx, s.dr, 3 * s.dc), BF16)
    v.gup_c = ((L, s.nzx, s.dr, s.fc), BF16)
    v.gproj_c = ((L, s.dr, s.d), BF16)
    v.gdown_c = ((L, s.fr, s.d), BF16)
    v.gqkv_in = ((L, s.nzx, s.dr, 3 * s.dc), BF16)
    v.gup_in = ((L, s.nzx, s.dr, s.fc), BF16)
    v.gproj_in = ((L, s.dr, s.d), BF16)
    v.t_gq, v.t_gp = ((s.dr, 3 * s.dc), F32), ((s.dr, s.dc), F32)
    v.t_gu, v.t_gd = ((s.dr, s.fc), F32), ((s.fr, s.dc), F32)
    v.t_gq_out = v.t_gq_in = ((L, s.dr, 3 * s.dc), BF16)
    v.t_gp_out = v.t_gp_in = ((L, s.dr, s.dc), BF16)
    v.t_gu_out = v.t_gu_in = ((L, s.dr, s.fc), BF16)
    v.t_gd_out = v.t_gd_in = ((L, s.fr, s.dc), BF16)
    v.gdown_in = ((L, s.fr, s.d), BF16)
    v.gproj_out = ((L, s.dr, s.dc), BF16)
    v.gdown_out = ((L, s.fr, s.dc), BF16)
    v.gproj_fin = ((L, s.dr, s.dc), BF16)
    v.gdown_fin = ((L, s.fr, s.dc), BF16)
    v.vec = ((L * VEC_ROWS, s.d), F32)
    v.vec_in = ((s.nc, L * VEC_ROWS, s.dc), F32)
    v.segq = ((4, 2 * s.qc, 1), jnp.int32)
    v.segk = ((4, s.nr * s.qc), jnp.int32)
    v.own = ((L * 2 * VEC_ROWS, s.dc), F32)
    v.own_in = ((s.nr, L * 2 * VEC_ROWS, s.dc), F32)
    return vars(v)


INPUTS = tuple(dict(x=0, cotan=0, wq=0, wk=0, wv=0, wp=0, wu=0, wd=0, qb=0, vb=0, pb=0, upb=0, db=0, g1=0, s1=0, g2=0, s2=0,
                    places=0))
OUTPUTS = tuple(dict(o_act=0, o_in=0, o_q=0, o_k=0, o_v=0, o_proj=0, o_up=0, o_down=0, o_vec=0))

(X_IN, COTAN, PVEC, ACT, VEC, OWN, WPT, WDT, GPT, GDT, PR, N1, FR, H, DF, DN, DR, DX,
 WQ, WP, WU, WD, KVA, KVB, DKVA, DKVB, GQ, GP, GU, GD) = range(30)
CORE, ACROSS = 1, 2
IN_STEPS = {(n, l) for n in (WP, WU, WD, KVA, KVB, GP, GU, GD) for l in range(LAYERS)} | {(WQ, 1), (GQ, 1)}
KV = {KVA: 0, KVB: 1}
DKV = {DKVA: 0, DKVB: 1}
KEYS = (
    [(n, 0, 0) for n in range(X_IN, GPT)]
    + [(n, l, 0) for n in range(GPT, PR) for l in range(LAYERS)]
    + [(n, l, a) for n in range(PR, WQ) for l in range(LAYERS) for a in range(2)]
    + [(n, l, step) for n in range(WQ, GD + 1) for l in range(LAYERS) for step in range(3)]
)
PHASE = {key: index for index, key in enumerate(KEYS)}


def kernel(s, *refs):
    names = INPUTS + OUTPUTS + tuple(scratch_of(s)) + ("send", "recv")
    m = SimpleNamespace(**dict(zip(names, refs)))
    L = LAYERS
    r, c = lax.axis_index("row"), lax.axis_index("col")
    zx, k = lax.div(r, 2), lax.rem(r, 2)
    z, x = lax.div(zx, 2), lax.rem(zx, 2)
    across = z * 2 + 1 - x
    other = zx * 2 + 1 - k
    at_home = zx == c
    chips, few = s.nzx - 1, s.nc - 1

    def remote(src, dst, phase, row, col):
        return pltpu.make_async_remote_copy(
            src_ref=src, dst_ref=dst, send_sem=m.send.at[PHASE[phase]], recv_sem=m.recv.at[PHASE[phase]],
            device_id=(row, col), device_id_type=MESH)

    def wait(sems, phase, ref):
        pltpu.make_async_copy(ref, ref, sems.at[PHASE[phase]]).wait()

    def each_col(fn):
        def step(q, carry):
            fn(lax.rem(c + q, s.nc))
            return carry
        lax.fori_loop(1, s.nc, step, 0)

    def each_row(fn):
        def step(q, carry):
            fn(lax.rem(r + q, s.nr))
            return carry
        lax.fori_loop(1, s.nr, step, 0)

    def each_chip(fn):
        def step(q, carry):
            fn(lax.rem(zx + q, s.nzx))
            return carry
        lax.fori_loop(1, s.nzx, step, 0)

    def each_z(fn):
        def step(q, carry):
            fn(lax.rem(z + q, s.nz))
            return carry
        lax.fori_loop(1, s.nz, step, 0)

    def rows(i, n):
        return pl.ds(pl.multiple_of(i * n, n), n)

    barrier = pltpu.get_barrier_semaphore()

    def greet(row, col):
        pl.semaphore_signal(barrier, inc=1, device_id=(row, col), device_id_type=MESH)

    swap_row, swap_col = c * 2 + k, zx
    each_col(lambda cc: greet(r, cc))
    each_row(lambda rr: greet(rr, c))

    @pl.when(jnp.logical_not(at_home))
    def _():
        greet(swap_row, swap_col)

    def weight(name, l):
        chips = s.nzx - (2 if (name, l) in IN_STEPS else 1)
        if name in KV:
            span = pl.ds(KV[name] * s.half, s.half)
            return ((lambda i, kk: m.kv.at[l, i, kk, span]), (lambda kk: m.kv.at[l, :, kk, span]),
                    m.kv.at[l, pl.ds(0, chips), 0, span] if chips else None)
        if name in (WQ, WU):
            ref = {WQ: m.wqkv, WU: m.wup}[name]
            return (lambda i, kk: ref.at[l, i, kk]), (lambda kk: ref.at[l, :, kk]), \
                ref.at[l, pl.ds(0, chips), 0] if chips else None
        ref, n = {WP: (m.wproj, s.dr), WD: (m.wdown, s.fr)}[name]
        return ((lambda i, kk: ref.at[l, rows(kk, n), rows(i, s.dc)]), (lambda kk: ref.at[l, rows(kk, n)]),
                ref.at[l, pl.ds(0, n), pl.ds(0, chips * s.dc)] if chips else None)

    def gather(name, l):
        piece = weight(name, l)[0](zx, k)
        if (name, l) not in IN_STEPS:
            each_chip(lambda i: remote(piece, piece, (name, l, 0), i * 2 + k, c).start())
            return
        remote(piece, piece, (name, l, ACROSS), across * 2 + k, c).start()
        each_z(lambda i: remote(piece, piece, (name, l, 0), (i * 2 + x) * 2 + k, c).start())

    def forward(name, l):
        piece = weight(name, l)[0](across, k)
        wait(m.recv, (name, l, ACROSS), piece)
        each_z(lambda i: remote(piece, piece, (name, l, 0), (i * 2 + x) * 2 + k, c).start())

    def pass_on(name, l):
        _, half, many = weight(name, l)
        if many is not None:
            wait(m.recv, (name, l, 0), many)
        remote(half(k), half(k), (name, l, CORE), other, c).start()

    def gathered(name, l):
        wait(m.recv, (name, l, CORE), weight(name, l)[1](1 - k))

    def sent_gather(name, l):
        piece, half, many = weight(name, l)
        if many is not None:
            wait(m.send, (name, l, 0), many)
        if (name, l) in IN_STEPS:
            wait(m.send, (name, l, ACROSS), piece(zx, k))
        wait(m.send, (name, l, CORE), half(k))

    def partial_sum(name, l):
        if name in DKV:
            a = DKV[name]
            mid, got = m.dkv_c.at[l, a], m.dkv_in.at[l, a]
            return (lambda kk: m.dkv.at[a, :, kk]), mid, (lambda i: mid.at[i]), got
        if name in (GQ, GU):
            full, mid, got = {GQ: (m.gqkv, m.gqkv_c.at[l], m.gqkv_in.at[l]),
                              GU: (m.gup, m.gup_c.at[l], m.gup_in.at[l])}[name]
            return (lambda kk: full.at[:, kk]), mid, (lambda i: mid.at[i]), got
        full, mid, got, n = {GP: (m.gproj, m.gproj_c.at[l], m.gproj_in.at[l], s.dr),
                             GD: (m.gdown, m.gdown_c.at[l], m.gdown_in.at[l], s.fr)}[name]
        return (lambda kk: full.at[rows(kk, n)]), mid, (lambda i: mid.at[:, rows(i, s.dc)]), got

    def reduce_start(name, l):
        half, mid, _, _ = partial_sum(name, l)
        remote(half(1 - k), mid, (name, l, CORE), other, c).start()

    def both(name, mid, i):
        if name in (GP, GD):
            return mid.at[:, rows(i, 2 * s.dc)]
        return mid.at[pl.ds(2 * i, 2)]

    def m_pair(name, got, i):
        if name in (GP, GD):
            return got.at[:, rows(i, 2 * s.dc)]
        return got.at[pl.ds(2 * i, 2)]

    def reduce_turn(name, l):
        _, mid, piece, got = partial_sum(name, l)
        if s.nz > 1:
            wait(m.recv, (name, l, 0), m_all(name, got))
        sums = []
        for which in (x, 1 - x):
            total = piece(z * 2 + which)[...].astype(F32)
            for q in range(1, s.nz):
                i = lax.rem(z + q, s.nz) * 2 + which
                arrived = got[:, rows(i, s.dc)] if name in (GP, GD) else got[i]
                total = total + arrived.astype(F32)
            sums.append(total)
        kept, out, back = turned(name, l)
        kept[...] = sums[0]
        out[...] = sums[1].astype(BF16)
        remote(out, back, (name, l, ACROSS), across * 2 + k, c).start()

    def turned(name, l):
        return {GQ: (m.t_gq, m.t_gq_out.at[l], m.t_gq_in.at[l]), GP: (m.t_gp, m.t_gp_out.at[l], m.t_gp_in.at[l]),
                GU: (m.t_gu, m.t_gu_out.at[l], m.t_gu_in.at[l]), GD: (m.t_gd, m.t_gd_out.at[l], m.t_gd_in.at[l])}[name]

    def m_all(name, got):
        if name in (GP, GD):
            return got.at[:, pl.ds(0, 2 * (s.nz - 1) * s.dc)]
        return got.at[pl.ds(0, 2 * (s.nz - 1))]

    def reduce_mid(name, l):
        half, mid, piece, got = partial_sum(name, l)
        wait(m.recv, (name, l, CORE), mid)
        mid[...] = (half(k)[...].astype(F32) + mid[...].astype(F32)).astype(BF16)
        if (name, l) in IN_STEPS:
            each_z(lambda i: remote(both(name, mid, i), m_pair(name, got, z), (name, l, 0), (i * 2 + x) * 2 + k, c).start())
            return
        each_chip(lambda i: remote(piece(i), got.at[zx], (name, l, 0), i * 2 + k, c).start())
        got[zx] = piece(zx)[...]

    def reduce_end(name, l):
        if (name, l) in IN_STEPS:
            kept, _, back = turned(name, l)
            wait(m.recv, (name, l, ACROSS), back)
            return kept[...] + back[...].astype(F32)
        got = partial_sum(name, l)[3]
        wait(m.recv, (name, l, 0), got.at[pl.ds(0, chips)])
        total = got[0].astype(F32)
        for i in range(1, s.nzx):
            total = total + got[i].astype(F32)
        return total

    def sent_half(name, l):
        wait(m.send, (name, l, CORE), partial_sum(name, l)[1])

    def sent_pieces(name, l):
        if (name, l) in IN_STEPS:
            if s.nz > 1:
                wait(m.send, (name, l, 0), m_all(name, partial_sum(name, l)[3]))
            wait(m.send, (name, l, ACROSS), turned(name, l)[1])
            return
        wait(m.send, (name, l, 0), partial_sum(name, l)[3].at[pl.ds(0, chips)])

    m.xf[0, :, :, rows(c, s.dc)] = m.x[...]
    m.cot[:, :, rows(c, s.dc)] = m.cotan[:, rows(c, s.t), :]
    m.pv[:, rows(c, s.dc)] = jnp.zeros((L * VEC_ROWS, s.dc), F32)
    for l in range(L):
        for which, ref in enumerate((m.pb, m.db, m.g1, m.s1, m.g2, m.s2)):
            m.pv[l * VEC_ROWS + which : l * VEC_ROWS + which + 1, rows(c, s.dc)] = ref[l : l + 1, :].astype(F32)
        for which, ref in enumerate((m.wq, m.wk, m.wv)):
            m.wqkv[l, zx, k, :, which * s.dc : (which + 1) * s.dc] = ref[l]
        m.wup[l, zx, k] = m.wu[l]

    pl.semaphore_wait(barrier, s.nc - 1 + s.nr - 1 + 1 - at_home.astype(jnp.int32))

    gather(WQ, 0)
    each_col(lambda cc: remote(m.x, m.xf.at[0, :, :, rows(c, s.dc)], (X_IN, 0, 0), r, cc).start())

    @pl.when(jnp.logical_not(at_home))
    def _():
        remote(m.wp, m.wp_own, (WPT, 0, 0), swap_row, swap_col).start()
        remote(m.wd, m.wd_own, (WDT, 0, 0), swap_row, swap_col).start()
    mine = m.pv.at[:, rows(c, s.dc)]
    each_col(lambda cc: remote(mine, mine, (PVEC, 0, 0), r, cc).start())
    each_col(lambda cc: remote(
        m.cotan.at[:, rows(cc, s.t)], m.cot.at[:, :, rows(c, s.dc)], (COTAN, 0, 0), r, cc).start())
    square = (s.qc, s.qc)
    diagonal = lax.broadcasted_iota(jnp.int32, square, 0) == lax.broadcasted_iota(jnp.int32, square, 1)
    for i in range(4):
        numbers = m.places[i : i + 1, :]
        column = jnp.sum(jnp.where(diagonal, numbers[:, : s.qc], 0), axis=1, keepdims=True)
        m.segq[i] = jnp.concatenate([column, column], axis=0)
        m.segk[i : i + 1, :] = jnp.concatenate([numbers] * (s.nr * s.qc // numbers.shape[1]), axis=1)
    m.vec[...] = jnp.zeros(m.vec.shape, F32)
    m.own[...] = jnp.zeros(m.own.shape, F32)

    def vector(l, which):
        return m.pv[l * VEC_ROWS + which : l * VEC_ROWS + which + 1, :]

    def share(buf, value, phase):
        buf[rows(c, s.t), :] = value
        each_col(lambda cc: remote(buf.at[rows(c, s.t)], buf.at[rows(c, s.t)], phase, r, cc).start())

    def shared(buf, phase):
        for sems in (m.recv, m.send):
            wait(sems, phase, buf.at[pl.ds(0, few * s.t)])

    def scatter(a, value, phase):
        m.part[a] = value.astype(BF16)
        each_col(lambda cc: remote(m.part.at[a, rows(cc, s.t)], m.got.at[a, c], phase, r, cc).start())
        m.got[a, c] = m.part[a, rows(c, s.t), :]

    def scattered(a, phase):
        for sems in (m.recv, m.send):
            wait(sems, phase, m.got.at[a, pl.ds(0, few)])
        total = m.got[a, 0].astype(F32)
        for i in range(1, s.nc):
            total = total + m.got[a, i].astype(F32)
        return total

    def norm(u, l, a, gain, shift, n_ref, r_ref):
        mean = jnp.sum(u, axis=1, keepdims=True) / s.d
        var = jnp.sum(u * u, axis=1, keepdims=True) / s.d - mean * mean
        inv = lax.rsqrt(var + 1e-12)
        n = (u - mean) * inv
        n_ref[l, a] = n
        r_ref[l, a] = inv
        return n * vector(l, gain) + vector(l, shift)

    def add_row(ref, at, value):
        ref[at : at + 1, :] += jnp.sum(value, axis=0, keepdims=True)

    def norm_back(g, l, a, gain, shift, n_ref, r_ref):
        n = n_ref[l, a]
        w = g * vector(l, gain)
        first = jnp.sum(w, axis=1, keepdims=True) / s.d
        second = jnp.sum(w * n, axis=1, keepdims=True) / s.d
        add_row(m.vec, l * VEC_ROWS + gain, g * n)
        add_row(m.vec, l * VEC_ROWS + shift, g)
        return r_ref[l, a] * (w - first - n * second)

    low_lanes = lax.broadcasted_iota(jnp.int32, (s.qc, s.dc), 1) < HEAD_DIM

    def two_heads(block):
        block = block.astype(F32)
        return jnp.concatenate([jnp.where(low_lanes, block, 0.0), jnp.where(low_lanes, 0.0, block)], axis=0)

    def one_block(pair):
        return jnp.where(low_lanes, pair[: s.qc], pair[s.qc :])

    def keys(l, j, value):
        lanes = pl.ds(s.dc if value else 0, s.dc)
        return m.kv[l, :, :, pl.ds(j * s.qc, s.qc), lanes].reshape(s.nr * s.qc, s.dc)

    def swapped(l):
        m.wproj[l, rows(k, s.dr), rows(zx, s.dc)] = m.wp_own[l]
        m.wdown[l, rows(k, s.fr), rows(zx, s.dc)] = m.wd_own[l]

    pass_on(WQ, 0)
    wait(m.recv, (X_IN, 0, 0), m.xf.at[0, :, :, pl.ds(0, few * s.dc)])
    wait(m.recv, (PVEC, 0, 0), m.pv.at[:, pl.ds(0, few * s.dc)])

    @pl.when(at_home)
    def _():
        m.wp_own[...] = m.wp[...]
        m.wd_own[...] = m.wd[...]

    @pl.when(jnp.logical_not(at_home))
    def _():
        wait(m.recv, (WPT, 0, 0), m.wp_own)
        wait(m.recv, (WDT, 0, 0), m.wd_own)
    swapped(0)

    def attend(l, i):
        queries = m.q2[l, i]
        ids = m.segq[i]
        scores = []
        for _, j in KEYS_OF[i]:
            raw = dot_nt(queries, keys(l, j, False))
            scores.append(jnp.where(ids == m.segk[j : j + 1, :], raw, -1e9))
        top = functools.reduce(jnp.maximum, [jnp.max(x, axis=1, keepdims=True) for x in scores])
        raised = [jnp.exp(x - top) for x in scores]
        inverse = 1.0 / sum(jnp.sum(x, axis=1, keepdims=True) for x in raised)
        out = jnp.zeros((2 * s.qc, s.dc), F32)
        for (n, j), x in zip(KEYS_OF[i], raised):
            prob = (x * inverse).astype(BF16)
            m.probs[l, n] = prob
            out = out + dot(prob, keys(l, j, True))
        m.att[l, i * s.qc : (i + 1) * s.qc, :] = one_block(out)

    def span(a):
        return pl.ds(a * s.half, s.half)

    for l in range(L):
        for a in range(2):
            if l:
                shared(m.xf.at[l, a], (H, l - 1, a))
            elif a == 0:
                gathered(WQ, 0)
                for b in range(2):
                    m.carry[b] = m.xf[0, b, rows(c, s.t), :].astype(F32)
            if l and a == 0:
                gathered(WQ, l)
            qkv = dot(m.xf[l, a], m.wqkv[l].reshape(s.d, 3 * s.dc))
            keep = (qkv[:, 2 * s.dc :] + m.vb[l : l + 1, :].astype(F32)).astype(BF16)
            m.kv[l, zx, k, span(a), : s.dc] = qkv[:, s.dc : 2 * s.dc].astype(BF16)
            m.kv[l, zx, k, span(a), s.dc :] = keep
            gather(KVA if a == 0 else KVB, l)
            for i in range(2):
                block = (qkv[i * s.qc : (i + 1) * s.qc, : s.dc] + m.qb[l : l + 1, :].astype(F32)).astype(BF16)
                m.q2[l, 2 * a + i] = (two_heads(block) * HEAD_DIM ** (-0.5)).astype(BF16)
        if l == 0:
            gather(WP, 0)
        if l == 0:
            forward(WP, 0)
        forward(KVA, l)
        forward(KVB, l)
        pass_on(KVA, l)
        pass_on(KVB, l)
        if l == 0:
            gather(WU, 0)
            gather(WD, 0)
            pass_on(WP, 0)
        else:
            pass_on(WU, 1)
            pass_on(WD, 1)
        gathered(KVA, l)
        attend(l, 0)
        gathered(KVB, l)
        attend(l, 1)
        gathered(WP, l)
        scatter(0, dot(m.att[l, span(0), :].astype(BF16), m.wproj[l]), (PR, l, 0))
        attend(l, 2)
        attend(l, 3)
        scatter(1, dot(m.att[l, span(1), :].astype(BF16), m.wproj[l]), (PR, l, 1))
        if l == 0:
            forward(WU, 0)
            forward(WD, 0)
            swapped(1)
        for a in range(2):
            u = scattered(a, (PR, l, a)) + vector(l, PROJ_B) + m.carry[a]
            first_out = norm(u, l, a, GAIN1, SHIFT1, m.n1, m.r1)
            share(m.x1.at[l, a], first_out.astype(BF16), (N1, l, a))
            m.carry[a] = first_out
        if l == 0:
            pass_on(WU, 0)
            pass_on(WD, 0)
            gather(WQ, 1)
            gather(WP, 1)
        gathered(WU, l)
        for a in range(2):
            shared(m.x1.at[l, a], (N1, l, a))
            pre = dot(m.x1[l, a], m.wup[l].reshape(s.d, s.fc)) + m.upb[l : l + 1, :].astype(F32)
            cdf = 0.5 * (1.0 + lax.erf(pre * 0.5**0.5))
            m.gate[l, a] = (pre * cdf).astype(BF16)
            if a == 0:
                gathered(WD, l)
            scatter(a, dot(m.gate[l, a], m.wdown[l]), (FR, l, a))
            m.slope[l, a] = cdf + pre * (jnp.exp(-0.5 * pre * pre) * 0.3989422804014327)
        if l == 0:
            forward(WQ, 1)
            forward(WP, 1)
            gather(WU, 1)
            gather(WD, 1)
        for a in range(2):
            u = scattered(a, (FR, l, a)) + vector(l, DOWN_B) + m.carry[a]
            hidden = norm(u, l, a, GAIN2, SHIFT2, m.n2, m.r2)
            if l == 0:
                share(m.xf.at[1, a], hidden.astype(BF16), (H, 0, a))
                m.carry[a] = hidden
            else:
                m.act_out[a] = hidden.astype(BF16)
        if l == 0:
            pass_on(WQ, 1)
            pass_on(WP, 1)
            forward(WU, 1)
            forward(WD, 1)

    def swap_back(l, name, total):
        out, fin, phase = {GP: (m.gproj_out, m.gproj_fin, (GPT, l, 0)), GD: (m.gdown_out, m.gdown_fin, (GDT, l, 0))}[name]
        out[l] = total.astype(BF16)

        @pl.when(jnp.logical_not(at_home))
        def _():
            remote(out.at[l], fin.at[l], phase, swap_row, swap_col).start()

        @pl.when(at_home)
        def _():
            fin[l] = out[l]

    def swap_end(l, name, out):
        fin, phase = {GP: (m.gproj_fin, (GPT, l, 0)), GD: (m.gdown_fin, (GDT, l, 0))}[name]

        @pl.when(jnp.logical_not(at_home))
        def _():
            wait(m.recv, phase, fin.at[l])
        out[l] = fin[l].astype(F32)

    def attend_back(l, j):
        key_grad = jnp.zeros((s.nr * s.qc, s.dc), F32)
        value_grad = jnp.zeros((s.nr * s.qc, s.dc), F32)
        for n, i in QUERIES_OF[j]:
            prob = m.probs[l, n]
            prob_grad = dot_nt(m.do2[i], keys(l, j, True))
            score_grad = (prob.astype(F32) * (prob_grad - m.delta[i])).astype(BF16)
            m.dq2[i] += dot(score_grad, keys(l, j, False))
            key_grad = key_grad + dot_tn(score_grad, m.q2[l, i])
            value_grad = value_grad + dot_tn(prob, m.do2[i])
        shape = (s.nzx, 2, s.qc, s.dc)
        place = pl.ds(j % 2 * s.qc, s.qc)
        m.dkv[j // 2, :, :, place, pl.ds(0, s.dc)] = key_grad.astype(BF16).reshape(shape)
        m.dkv[j // 2, :, :, place, pl.ds(s.dc, s.dc)] = value_grad.astype(BF16).reshape(shape)

    wait(m.recv, (COTAN, 0, 0), m.cot.at[:, :, pl.ds(0, few * s.dc)])
    for l in reversed(range(L)):
        at = l * VEC_ROWS
        own = l * 2 * VEC_ROWS
        for a in range(2):
            if l + 1 < L:
                grad = scattered(a, (DX, l + 1, a)) + m.carry[a]
            else:
                grad = m.cot[a].astype(F32)
            dz = norm_back(grad, l, a, GAIN2, SHIFT2, m.n2, m.r2)
            m.carry[a] = dz
            low = dz.astype(BF16)
            share(m.dff.at[l, a], low, (DF, l, a))
            add_row(m.vec, at + DOWN_B, low.astype(F32))
        if l + 1 == L:
            each_col(lambda cc: remote(
                m.act_out.at[:, :, rows(cc, s.dc)], m.act_in.at[:, rows(c, s.t)], (ACT, 0, 0), r, cc).start())
            m.act_in[:, rows(c, s.t), :] = m.act_out[:, :, rows(c, s.dc)]
        else:
            reduce_mid(GQ, l + 1)
            reduce_turn(GP, l + 1)
        for a in range(2):
            shared(m.dff.at[l, a], (DF, l, a))
            de = (dot_nt(m.dff[l, a], m.wdown[l]) * m.slope[l, a]).astype(BF16)
            m.de[a] = de
            scatter(a, dot_nt(de, m.wup[l].reshape(s.d, s.fc)), (DN, l, a))
            sums = jnp.sum(de.astype(F32), axis=0, keepdims=True)
            for i in range(s.fc // LANES):
                m.own[own + i : own + i + 1, :] += sums[:, i * LANES : (i + 1) * LANES]
        if l + 1 < L:
            reduce_turn(GQ, l + 1)
            swap_back(l + 1, GP, reduce_end(GP, l + 1))
            sent_half(GD, l + 1)
            sent_half(GU, l + 1)
        m.gdown[...] = dot_tn(m.gate[l].reshape(s.tok, s.fc), m.dff[l].reshape(s.tok, s.d)).astype(BF16)
        reduce_start(GD, l)
        for a in range(2):
            grad = scattered(a, (DN, l, a)) + m.carry[a]
            du = norm_back(grad, l, a, GAIN1, SHIFT1, m.n1, m.r1)
            m.carry[a] = du
            low = du.astype(BF16)
            share(m.drf.at[l, a], low, (DR, l, a))
            add_row(m.vec, at + PROJ_B, low.astype(F32))
        m.gup[...] = dot_tn(m.x1[l].reshape(s.tok, s.d), m.de[...].reshape(s.tok, s.fc)).astype(BF16).reshape(m.gup.shape)
        reduce_start(GU, l)
        reduce_mid(GD, l)
        if l == 0:
            each_col(lambda cc: remote(m.vec.at[:, rows(cc, s.dc)], m.vec_in.at[c], (VEC, 0, 0), r, cc).start())
            m.vec_in[c] = m.vec[:, rows(c, s.dc)]
        if l + 1 < L:
            sent_half(DKVA, l + 1)
            sent_half(DKVB, l + 1)
        for a in range(2):
            shared(m.drf.at[l, a], (DR, l, a))
            dout = dot_nt(m.drf[l, a], m.wproj[l]).astype(BF16)
            for b in range(2):
                i = 2 * a + b
                block = two_heads(dout[b * s.qc : (b + 1) * s.qc, :])
                kept = m.att[l, i * s.qc : (i + 1) * s.qc, :]
                m.do2[i] = block.astype(BF16)
                m.delta[i] = jnp.sum(block * jnp.concatenate([kept, kept], axis=0), axis=1, keepdims=True)
                m.dq2[i] = jnp.zeros((2 * s.qc, s.dc), F32)
            if a == 0:
                attend_back(l, 0)
                reduce_mid(GU, l)
        attend_back(l, 1)
        reduce_start(DKVA, l)
        attend_back(l, 2)
        reduce_mid(DKVA, l)
        attend_back(l, 3)
        reduce_start(DKVB, l)
        for i in range(4):
            m.dqkv[i * s.qc : (i + 1) * s.qc, : s.dc] = (one_block(m.dq2[i]) * HEAD_DIM ** (-0.5)).astype(BF16)
        reduce_mid(DKVB, l)
        reduce_turn(GD, l)
        if l + 1 < L:
            sent_half(GP, l + 1)
            sent_half(GQ, l + 1)
        m.gproj[...] = dot_tn(m.att[l].astype(BF16), m.drf[l].reshape(s.tok, s.d)).astype(BF16)
        reduce_start(GP, l)
        reduce_turn(GU, l)
        if l == 0:
            wait(m.recv, (VEC, 0, 0), m.vec_in.at[pl.ds(0, few)])
            total = m.vec_in[0]
            for i in range(1, s.nc):
                total = total + m.vec_in[i]
            for i in range(L):
                to = i * 2 * VEC_ROWS + VEC_ROWS
                m.own[to : to + VEC_ROWS, :] = total[i * VEC_ROWS : (i + 1) * VEC_ROWS]
        for a in range(2):
            m.dqkv[span(a), s.dc :] = reduce_end(DKVA if a == 0 else DKVB, l).astype(BF16)
            back = dot_nt(m.dqkv[span(a), :], m.wqkv[l].reshape(s.d, 3 * s.dc))
            if l:
                scatter(a, back, (DX, l, a))
            else:
                m.part[a] = back.astype(BF16)
                mine = m.part[a, rows(c, s.t), :].astype(F32) + m.carry[a]
                m.part[a, rows(c, s.t), :] = mine.astype(BF16)
                each_col(lambda cc: remote(m.part.at[a, :, rows(cc, s.dc)], m.got_in.at[a, c], (DX, 0, a), r, cc).start())
                m.got_in[a, c] = m.part[a, :, rows(c, s.dc)]
        m.gqkv[...] = dot_tn(m.xf[l].reshape(s.tok, s.d), m.dqkv[...]).astype(BF16).reshape(m.gqkv.shape)
        reduce_start(GQ, l)
        sums = jnp.sum(m.dqkv[...].astype(F32), axis=0, keepdims=True)
        m.own[own + 4 : own + 5, :] = sums[:, : s.dc]
        m.own[own + 5 : own + 6, :] = sums[:, 2 * s.dc :]
        reduce_mid(GP, l)
        swap_back(l, GD, reduce_end(GD, l))
        m.o_up[l] = reduce_end(GU, l)
        if l + 1 < L:
            swap_end(l + 1, GD, m.o_down)
            swap_end(l + 1, GP, m.o_proj)
            total = reduce_end(GQ, l + 1)
            for which, out in enumerate((m.o_q, m.o_k, m.o_v)):
                out[l + 1] = total[:, which * s.dc : (which + 1) * s.dc]

    m.own_in[r] = m.own[...]
    each_row(lambda rr: remote(m.own, m.own_in.at[r], (OWN, 0, 0), rr, c).start())
    reduce_mid(GQ, 0)
    reduce_turn(GP, 0)
    swap_end(0, GD, m.o_down)
    wait(m.recv, (ACT, 0, 0), m.act_in.at[:, pl.ds(0, few * s.t)])
    m.o_act[...] = m.act_in[...]
    for a in range(2):
        wait(m.recv, (DX, 0, a), m.got_in.at[a, pl.ds(0, few)])
        total = m.got_in[a, 0].astype(F32)
        for i in range(1, s.nc):
            total = total + m.got_in[a, i].astype(F32)
        m.o_in[a] = total
    swap_back(0, GP, reduce_end(GP, 0))
    wait(m.recv, (OWN, 0, 0), m.own_in.at[pl.ds(0, s.nr - 1)])
    total = m.own_in[0]
    for i in range(1, s.nr):
        total = total + m.own_in[i]
    m.o_vec[...] = total
    total = reduce_end(GQ, 0)
    for which, out in enumerate((m.o_q, m.o_k, m.o_v)):
        out[0] = total[:, which * s.dc : (which + 1) * s.dc]
    swap_end(0, GP, m.o_proj)

    wait(m.send, (X_IN, 0, 0), m.xf.at[0, :, :, pl.ds(0, few * s.dc)])
    wait(m.send, (PVEC, 0, 0), m.pv.at[:, pl.ds(0, few * s.dc)])
    wait(m.send, (COTAN, 0, 0), m.cot.at[:, :, pl.ds(0, few * s.dc)])
    wait(m.send, (ACT, 0, 0), m.act_in.at[:, pl.ds(0, few * s.t)])
    for a in range(2):
        wait(m.send, (DX, 0, a), m.got_in.at[a, pl.ds(0, few)])
    wait(m.send, (VEC, 0, 0), m.vec_in.at[pl.ds(0, few)])
    wait(m.send, (OWN, 0, 0), m.own_in.at[pl.ds(0, s.nr - 1)])

    @pl.when(jnp.logical_not(at_home))
    def _():
        wait(m.send, (WPT, 0, 0), m.wp_own)
        wait(m.send, (WDT, 0, 0), m.wd_own)
        for l in range(L):
            wait(m.send, (GPT, l, 0), m.gproj_fin.at[l])
            wait(m.send, (GDT, l, 0), m.gdown_fin.at[l])
    for l in range(L):
        for name in (WQ, WP, WU, WD, KVA, KVB):
            sent_gather(name, l)
        for name in (GQ, GP, GU, GD, DKVA, DKVB):
            sent_pieces(name, l)
    for name in (GQ, GP, GU, GD, DKVA, DKVB):
        sent_half(name, 0)


def body(s, layer_input, query_weight, key_weight, value_weight, proj_weight, up_weight, down_weight, query_shift,
         value_shift, proj_shift, up_shift, down_shift, first_gain, first_shift, second_gain, second_shift, segment_ids,
         cotangent):
    L = LAYERS
    places = jnp.tile(segment_ids[: s.tok].reshape(4, s.qc), (1, LANES // s.qc))
    shapes = scratch_of(s)
    halves = (2, s.half, s.dc)
    square = jax.ShapeDtypeStruct((L, s.dr, s.dc), F32)
    out_shape = (
        jax.ShapeDtypeStruct((2, s.half, s.dc), BF16),
        jax.ShapeDtypeStruct((2, s.half, s.dc), F32),
        square, square, square, square,
        jax.ShapeDtypeStruct((L, s.dr, s.fc), F32),
        jax.ShapeDtypeStruct((L, s.fr, s.dc), F32),
        jax.ShapeDtypeStruct((L * 2 * VEC_ROWS, s.dc), F32),
    )
    vmem = pl.BlockSpec(memory_space=pltpu.VMEM)
    results = pl.pallas_call(
        functools.partial(kernel, s),
        out_shape=out_shape,
        in_specs=[vmem] * len(INPUTS),
        out_specs=[vmem] * len(OUTPUTS),
        scratch_shapes=[pltpu.VMEM(shape, dtype) for shape, dtype in shapes.values()]
        + [pltpu.SemaphoreType.DMA((len(KEYS),))] * 2,
        compiler_params=pltpu.CompilerParams(
            collective_id=0, has_side_effects=True, vmem_limit_bytes=60 * 2**20),
        name="encoder",
    )(layer_input.reshape(halves), cotangent.reshape(halves), query_weight, key_weight, value_weight, proj_weight, up_weight,
      down_weight, query_shift, value_shift, proj_shift, up_shift, down_shift, first_gain, first_shift, second_gain,
      second_shift, places)
    narrow, wide = jax.ShapeDtypeStruct((L, s.dc), F32), jax.ShapeDtypeStruct((L, s.fc), F32)
    o_act, o_in, *others = pl.pallas_call(
        functools.partial(hand_out, s),
        out_shape=out_shape[:-1] + (narrow,) * 3 + (wide,) + (narrow,) * 5,
        in_specs=[vmem] * len(OUTPUTS),
        out_specs=[vmem] * 17,
        name="results",
    )(*results)
    return (o_act.reshape(s.tok, s.dc), o_in.reshape(s.tok, s.dc), *others)


def hand_out(s, *refs):
    count = len(OUTPUTS)
    arrays, packed, outs = refs[: count - 1], refs[count - 1], refs[count:]
    for array, out in zip(arrays, outs):
        out[...] = array[...]
    qs, vs, ps, us, ds, fg, fs, sg, ss = outs[count - 1 :]
    for l in range(LAYERS):
        own = l * 2 * VEC_ROWS
        rows = [(qs, 4), (vs, 5)]
        rows += [(ref, VEC_ROWS + which) for ref, which in
                 ((ps, PROJ_B), (ds, DOWN_B), (fg, GAIN1), (fs, SHIFT1), (sg, GAIN2), (ss, SHIFT2))]
        for ref, at in rows:
            ref[l : l + 1, :] = packed[own + at : own + at + 1, :]
        for i in range(s.fc // LANES):
            us[l : l + 1, i * LANES : (i + 1) * LANES] = packed[own + i : own + i + 1, :]


def build(mesh, tok, d, ff):
    s = Sizes(mesh.shape["row"], mesh.shape["col"], tok, d, ff)
    return jax.shard_map(
        functools.partial(body, s),
        mesh=mesh,
        in_specs=(P("row", "col"),) + (P(None, "row", "col"),) * 6 + (P(None, "col"),) * 9 + (P(), P("row", "col")),
        out_specs=(P("row", "col"),) * 2 + (P(None, "row", "col"),) * 6 + (P(None, "col"),) * 9,
        check_vma=False,
    )


def solution(mesh):
    return build(mesh, 256, 1024, 4096)
```

```python
import functools
from types import SimpleNamespace

import jax
import jax.numpy as jnp
from jax import lax
from jax.experimental import pallas as pl
from jax.experimental.pallas import tpu as pltpu
from jax.sharding import PartitionSpec as P

MESH = pl.DeviceIdType.MESH
LAYERS = 2
HEAD_DIM = 64
LANES = 128
F32 = jnp.float32
BF16 = jnp.bfloat16
PAIRS = ((0, 0), (1, 1), (1, 2), (2, 1), (2, 2), (2, 3), (3, 2), (3, 3))
KEYS_OF = {i: [(n, j) for n, (a, j) in enumerate(PAIRS) if a == i] for i in range(4)}
QUERIES_OF = {j: [(n, i) for n, (i, b) in enumerate(PAIRS) if b == j] for j in range(4)}

PROJ_B, DOWN_B, GAIN1, SHIFT1, GAIN2, SHIFT2 = range(6)
VEC_ROWS = 8


def dot(a, b):
    return jnp.dot(a, b, preferred_element_type=F32)


def dot_nt(a, b):
    return lax.dot_general(a, b, (((1,), (1,)), ((), ())), preferred_element_type=F32)


def dot_tn(a, b):
    return lax.dot_general(a, b, (((0,), (0,)), ((), ())), preferred_element_type=F32)


class Sizes:
    def __init__(self, nr, nc, tok, d, ff):
        self.nr, self.nc, self.tok, self.d, self.ff = nr, nc, tok, d, ff
        self.half = tok // 2
        self.t = self.half // nc
        self.dc, self.fc = d // nc, ff // nc
        self.dr, self.fr = d // nr, ff // nr
        self.nz = nr // 4
        self.nzx = nr // 2
        self.qc = tok // 4


def scratch_of(s):
    L = LAYERS
    v = SimpleNamespace()
    v.xf = ((L, 2, s.half, s.d), BF16)
    v.x1 = ((L, 2, s.half, s.d), BF16)
    v.dff = ((L, 2, s.half, s.d), BF16)
    v.drf = ((L, 2, s.half, s.d), BF16)
    v.part = ((2, s.half, s.d), BF16)
    v.got = ((2, s.nc, s.t, s.d), BF16)
    v.got_in = ((2, s.nc, s.half, s.dc), BF16)
    v.act_out = ((2, s.t, s.d), BF16)
    v.act_in = ((2, s.half, s.dc), BF16)
    v.cot = ((2, s.t, s.d), BF16)
    v.pv = ((L * VEC_ROWS, s.d), F32)
    v.kv = ((L, s.nzx, 2, s.tok, 2 * s.dc), BF16)
    v.dkv = ((4, s.nzx, 2, s.qc, 2 * s.dc), BF16)
    v.dkv_c = ((L, 4, s.nzx, s.qc, 2 * s.dc), BF16)
    v.dkv_in = ((L, 4, s.nzx, s.qc, 2 * s.dc), BF16)
    v.probs = ((L, len(PAIRS), 2 * s.qc, s.nr * s.qc), BF16)
    v.q2 = ((L, 4, 2 * s.qc, s.dc), BF16)
    v.do2 = ((4, 2 * s.qc, s.dc), BF16)
    v.delta = ((4, 2 * s.qc, 1), F32)
    v.dq2 = ((4, 2 * s.qc, s.dc), F32)
    v.att = ((L, s.tok, s.dc), F32)
    v.gate = ((L, 2, s.half, s.fc), BF16)
    v.slope = ((L, 2, s.half, s.fc), F32)
    v.de = ((2, s.half, s.fc), BF16)
    v.n1 = ((L, 2, s.t, s.d), F32)
    v.n2 = ((L, 2, s.t, s.d), F32)
    v.r1 = ((L, 2, s.t, 1), F32)
    v.r2 = ((L, 2, s.t, 1), F32)
    v.carry = ((2, s.t, s.d), F32)
    v.dqkv = ((s.tok, 3 * s.dc), BF16)
    v.wqkv = ((L, s.nzx, 2, s.dr, 3 * s.dc), BF16)
    v.wup = ((L, s.nzx, 2, s.dr, s.fc), BF16)
    v.wproj = ((L, s.dc, s.d), BF16)
    v.wdown = ((L, s.fc, s.d), BF16)
    v.wp_own = ((L, s.dr, s.dc), BF16)
    v.wd_own = ((L, s.fr, s.dc), BF16)
    v.gqkv = ((s.nzx, 2, s.dr, 3 * s.dc), BF16)
    v.gup = ((s.nzx, 2, s.dr, s.fc), BF16)
    v.gproj = ((s.dc, s.d), BF16)
    v.gdown = ((s.fc, s.d), BF16)
    v.gqkv_c = ((L, s.nzx, s.dr, 3 * s.dc), BF16)
    v.gup_c = ((L, s.nzx, s.dr, s.fc), BF16)
    v.gproj_c = ((L, s.dr, s.d), BF16)
    v.gdown_c = ((L, s.fr, s.d), BF16)
    v.gqkv_in = ((L, s.nzx, s.dr, 3 * s.dc), BF16)
    v.gup_in = ((L, s.nzx, s.dr, s.fc), BF16)
    v.gproj_in = ((L, s.dr, s.d), BF16)
    v.t_gq, v.t_gp = ((s.dr, 3 * s.dc), F32), ((s.dr, s.dc), F32)
    v.t_gu, v.t_gd = ((s.dr, s.fc), F32), ((s.fr, s.dc), F32)
    v.t_gq_out = v.t_gq_in = ((L, s.dr, 3 * s.dc), BF16)
    v.t_gp_out = v.t_gp_in = ((L, s.dr, s.dc), BF16)
    v.t_gu_out = v.t_gu_in = ((L, s.dr, s.fc), BF16)
    v.t_gd_out = v.t_gd_in = ((L, s.fr, s.dc), BF16)
    v.gdown_in = ((L, s.fr, s.d), BF16)
    v.gproj_out = ((L, s.dr, s.dc), BF16)
    v.gdown_out = ((L, s.fr, s.dc), BF16)
    v.gproj_fin = ((L, s.dr, s.dc), BF16)
    v.gdown_fin = ((L, s.fr, s.dc), BF16)
    v.vec = ((L * VEC_ROWS, s.d), F32)
    v.vec_in = ((s.nc, L * VEC_ROWS, s.dc), F32)
    v.segq = ((4, 2 * s.qc, 1), jnp.int32)
    v.segk = ((4, s.nr * s.qc), jnp.int32)
    v.own = ((L * 2 * VEC_ROWS, s.dc), F32)
    v.late = ((VEC_ROWS, s.dc), F32)
    v.late_in = ((s.nr, VEC_ROWS, s.dc), F32)
    v.own_in = ((s.nr, L * 2 * VEC_ROWS, s.dc), F32)
    return vars(v)


INPUTS = tuple(dict(x=0, cotan=0, wq=0, wk=0, wv=0, wp=0, wu=0, wd=0, qb=0, vb=0, pb=0, upb=0, db=0, g1=0, s1=0, g2=0, s2=0,
                    places=0))
OUTPUTS = tuple(dict(o_act=0, o_in=0, o_q=0, o_k=0, o_v=0, o_proj=0, o_up=0, o_down=0, o_vec=0))

(X_IN, COTAN, PVEC, ACT, VEC, OWN, WPT, WDT, GPT, GDT, PR, N1, FR, H, DF, DN, DR, DX,
 WQ, WP, WU, WD, KV0, KV1, KV2, KV3, DKV0, DKV1, DKV2, DKV3, GQ, GP, GU, GD) = range(34)
CORE, ACROSS = 1, 2
IN_STEPS = {(n, l) for n in (WP, WU, WD, KV0, KV1, KV2, KV3, GP, GU, GD) for l in range(LAYERS)} | {(WQ, 1), (GQ, 0), (GQ, 1)}
KV = {KV0: 0, KV1: 1, KV2: 2, KV3: 3}
DKV = {DKV0: 0, DKV1: 1, DKV2: 2, DKV3: 3}
KEYS = (
    [(X_IN, 0, 1), (OWN, 0, 1)] + [(n, 0, 0) for n in range(X_IN, GPT)]
    + [(n, l, 0) for n in range(GPT, PR) for l in range(LAYERS)]
    + [(n, l, a) for n in range(PR, WQ) for l in range(LAYERS) for a in range(2)]
    + [(n, l, step) for n in range(WQ, GD + 1) for l in range(LAYERS) for step in range(3)]
)
PHASE = {key: index for index, key in enumerate(KEYS)}


def kernel(s, *refs):
    names = INPUTS + OUTPUTS + tuple(scratch_of(s)) + ("send", "recv")
    m = SimpleNamespace(**dict(zip(names, refs)))
    L = LAYERS
    r, c = lax.axis_index("row"), lax.axis_index("col")
    zx, k = lax.div(r, 2), lax.rem(r, 2)
    z, x = lax.div(zx, 2), lax.rem(zx, 2)
    across = z * 2 + 1 - x
    other = zx * 2 + 1 - k
    at_home = zx == c
    chips, few = s.nzx - 1, s.nc - 1

    def remote(src, dst, phase, row, col):
        return pltpu.make_async_remote_copy(
            src_ref=src, dst_ref=dst, send_sem=m.send.at[PHASE[phase]], recv_sem=m.recv.at[PHASE[phase]],
            device_id=(row, col), device_id_type=MESH)

    def wait(sems, phase, ref):
        pltpu.make_async_copy(ref, ref, sems.at[PHASE[phase]]).wait()

    def each_col(fn):
        def step(q, carry):
            fn(lax.rem(c + q, s.nc))
            return carry
        lax.fori_loop(1, s.nc, step, 0)

    def each_row(fn):
        def step(q, carry):
            fn(lax.rem(r + q, s.nr))
            return carry
        lax.fori_loop(1, s.nr, step, 0)

    def each_chip(fn):
        def step(q, carry):
            fn(lax.rem(zx + q, s.nzx))
            return carry
        lax.fori_loop(1, s.nzx, step, 0)

    def each_z(fn):
        def step(q, carry):
            fn(lax.rem(z + q, s.nz))
            return carry
        lax.fori_loop(1, s.nz, step, 0)

    def rows(i, n):
        return pl.ds(pl.multiple_of(i * n, n), n)

    barrier = pltpu.get_barrier_semaphore()

    def greet(row, col):
        pl.semaphore_signal(barrier, inc=1, device_id=(row, col), device_id_type=MESH)

    swap_row, swap_col = c * 2 + k, zx
    each_col(lambda cc: greet(r, cc))
    each_row(lambda rr: greet(rr, c))

    @pl.when(jnp.logical_not(at_home))
    def _():
        greet(swap_row, swap_col)

    def weight(name, l):
        chips = s.nzx - (2 if (name, l) in IN_STEPS else 1)
        if name in KV:
            span = pl.ds(KV[name] * s.qc, s.qc)
            return ((lambda i, kk: m.kv.at[l, i, kk, span]), (lambda kk: m.kv.at[l, :, kk, span]),
                    m.kv.at[l, pl.ds(0, chips), 0, span] if chips else None)
        if name in (WQ, WU):
            ref = {WQ: m.wqkv, WU: m.wup}[name]
            return (lambda i, kk: ref.at[l, i, kk]), (lambda kk: ref.at[l, :, kk]), \
                ref.at[l, pl.ds(0, chips), 0] if chips else None
        ref, n = {WP: (m.wproj, s.dr), WD: (m.wdown, s.fr)}[name]
        return ((lambda i, kk: ref.at[l, rows(kk, n), rows(i, s.dc)]), (lambda kk: ref.at[l, rows(kk, n)]),
                ref.at[l, pl.ds(0, n), pl.ds(0, chips * s.dc)] if chips else None)

    def gather(name, l):
        piece = weight(name, l)[0](zx, k)
        if (name, l) not in IN_STEPS:
            each_chip(lambda i: remote(piece, piece, (name, l, 0), i * 2 + k, c).start())
            return
        remote(piece, piece, (name, l, ACROSS), across * 2 + k, c).start()
        each_z(lambda i: remote(piece, piece, (name, l, 0), (i * 2 + x) * 2 + k, c).start())

    def forward(name, l):
        piece = weight(name, l)[0](across, k)
        wait(m.recv, (name, l, ACROSS), piece)
        each_z(lambda i: remote(piece, piece, (name, l, 0), (i * 2 + x) * 2 + k, c).start())

    def pass_on(name, l):
        _, half, many = weight(name, l)
        if many is not None:
            wait(m.recv, (name, l, 0), many)
        remote(half(k), half(k), (name, l, CORE), other, c).start()

    def gathered(name, l):
        wait(m.recv, (name, l, CORE), weight(name, l)[1](1 - k))

    def sent_gather(name, l):
        piece, half, many = weight(name, l)
        if many is not None:
            wait(m.send, (name, l, 0), many)
        if (name, l) in IN_STEPS:
            wait(m.send, (name, l, ACROSS), piece(zx, k))
        wait(m.send, (name, l, CORE), half(k))

    def partial_sum(name, l):
        if name in DKV:
            a = DKV[name]
            mid, got = m.dkv_c.at[l, a], m.dkv_in.at[l, a]
            return (lambda kk: m.dkv.at[a, :, kk]), mid, (lambda i: mid.at[i]), got
        if name in (GQ, GU):
            full, mid, got = {GQ: (m.gqkv, m.gqkv_c.at[l], m.gqkv_in.at[l]),
                              GU: (m.gup, m.gup_c.at[l], m.gup_in.at[l])}[name]
            return (lambda kk: full.at[:, kk]), mid, (lambda i: mid.at[i]), got
        full, mid, got, n = {GP: (m.gproj, m.gproj_c.at[l], m.gproj_in.at[l], s.dr),
                             GD: (m.gdown, m.gdown_c.at[l], m.gdown_in.at[l], s.fr)}[name]
        return (lambda kk: full.at[rows(kk, n)]), mid, (lambda i: mid.at[:, rows(i, s.dc)]), got

    def reduce_start(name, l):
        half, mid, _, _ = partial_sum(name, l)
        remote(half(1 - k), mid, (name, l, CORE), other, c).start()

    def both(name, mid, i):
        if name in (GP, GD):
            return mid.at[:, rows(i, 2 * s.dc)]
        return mid.at[pl.ds(2 * i, 2)]

    def m_pair(name, got, i):
        if name in (GP, GD):
            return got.at[:, rows(i, 2 * s.dc)]
        return got.at[pl.ds(2 * i, 2)]

    def reduce_turn(name, l):
        _, mid, piece, got = partial_sum(name, l)
        if s.nz > 1:
            wait(m.recv, (name, l, 0), m_all(name, got))
        sums = []
        for which in (x, 1 - x):
            total = piece(z * 2 + which)[...].astype(F32)
            for q in range(1, s.nz):
                i = lax.rem(z + q, s.nz) * 2 + which
                arrived = got[:, rows(i, s.dc)] if name in (GP, GD) else got[i]
                total = total + arrived.astype(F32)
            sums.append(total)
        kept, out, back = turned(name, l)
        kept[...] = sums[0]
        out[...] = sums[1].astype(BF16)
        remote(out, back, (name, l, ACROSS), across * 2 + k, c).start()

    def turned(name, l):
        return {GQ: (m.t_gq, m.t_gq_out.at[l], m.t_gq_in.at[l]), GP: (m.t_gp, m.t_gp_out.at[l], m.t_gp_in.at[l]),
                GU: (m.t_gu, m.t_gu_out.at[l], m.t_gu_in.at[l]), GD: (m.t_gd, m.t_gd_out.at[l], m.t_gd_in.at[l])}[name]

    def m_all(name, got):
        if name in (GP, GD):
            return got.at[:, pl.ds(0, 2 * (s.nz - 1) * s.dc)]
        return got.at[pl.ds(0, 2 * (s.nz - 1))]

    def reduce_mid(name, l):
        half, mid, piece, got = partial_sum(name, l)
        wait(m.recv, (name, l, CORE), mid)
        mid[...] = (half(k)[...].astype(F32) + mid[...].astype(F32)).astype(BF16)
        if (name, l) in IN_STEPS:
            each_z(lambda i: remote(both(name, mid, i), m_pair(name, got, z), (name, l, 0), (i * 2 + x) * 2 + k, c).start())
            return
        each_chip(lambda i: remote(piece(i), got.at[zx], (name, l, 0), i * 2 + k, c).start())
        got[zx] = piece(zx)[...]

    def reduce_end(name, l):
        if (name, l) in IN_STEPS:
            kept, _, back = turned(name, l)
            wait(m.recv, (name, l, ACROSS), back)
            return kept[...] + back[...].astype(F32)
        got = partial_sum(name, l)[3]
        wait(m.recv, (name, l, 0), got.at[pl.ds(0, chips)])
        total = got[0].astype(F32)
        for i in range(1, s.nzx):
            total = total + got[i].astype(F32)
        return total

    def sent_half(name, l):
        wait(m.send, (name, l, CORE), partial_sum(name, l)[1])

    def sent_pieces(name, l):
        if (name, l) in IN_STEPS:
            if s.nz > 1:
                wait(m.send, (name, l, 0), m_all(name, partial_sum(name, l)[3]))
            wait(m.send, (name, l, ACROSS), turned(name, l)[1])
            return
        wait(m.send, (name, l, 0), partial_sum(name, l)[3].at[pl.ds(0, chips)])

    m.xf[0, :, :, rows(c, s.dc)] = m.x[...]
    m.cot[:, :, rows(c, s.dc)] = m.cotan[:, rows(c, s.t), :]
    m.pv[:, rows(c, s.dc)] = jnp.zeros((L * VEC_ROWS, s.dc), F32)
    for l in range(L):
        for which, ref in enumerate((m.pb, m.db, m.g1, m.s1, m.g2, m.s2)):
            m.pv[l * VEC_ROWS + which : l * VEC_ROWS + which + 1, rows(c, s.dc)] = ref[l : l + 1, :].astype(F32)
        for which, ref in enumerate((m.wq, m.wk, m.wv)):
            m.wqkv[l, zx, k, :, which * s.dc : (which + 1) * s.dc] = ref[l]
        m.wup[l, zx, k] = m.wu[l]

    pl.semaphore_wait(barrier, s.nc - 1 + s.nr - 1 + 1 - at_home.astype(jnp.int32))

    def send_x(a):
        each_col(lambda cc: remote(m.x.at[a], m.xf.at[0, a, :, rows(c, s.dc)], (X_IN, 0, a), r, cc).start())

    send_x(0)
    gather(WQ, 0)
    send_x(1)

    @pl.when(jnp.logical_not(at_home))
    def _():
        remote(m.wp, m.wp_own, (WPT, 0, 0), swap_row, swap_col).start()
        remote(m.wd, m.wd_own, (WDT, 0, 0), swap_row, swap_col).start()
    mine = m.pv.at[:, rows(c, s.dc)]
    each_col(lambda cc: remote(mine, mine, (PVEC, 0, 0), r, cc).start())
    each_col(lambda cc: remote(
        m.cotan.at[:, rows(cc, s.t)], m.cot.at[:, :, rows(c, s.dc)], (COTAN, 0, 0), r, cc).start())
    square = (s.qc, s.qc)
    diagonal = lax.broadcasted_iota(jnp.int32, square, 0) == lax.broadcasted_iota(jnp.int32, square, 1)
    for i in range(4):
        numbers = m.places[i : i + 1, :]
        column = jnp.sum(jnp.where(diagonal, numbers[:, : s.qc], 0), axis=1, keepdims=True)
        m.segq[i] = jnp.concatenate([column, column], axis=0)
        m.segk[i : i + 1, :] = jnp.concatenate([numbers] * (s.nr * s.qc // numbers.shape[1]), axis=1)
    m.vec[...] = jnp.zeros(m.vec.shape, F32)
    m.own[...] = jnp.zeros(m.own.shape, F32)
    m.late[...] = jnp.zeros(m.late.shape, F32)

    def vector(l, which):
        return m.pv[l * VEC_ROWS + which : l * VEC_ROWS + which + 1, :]

    unwaited = []
    in_flight = [None, None]

    def part_free(a):
        if in_flight[a] is not None:
            wait(m.send, in_flight[a], m.got.at[a, pl.ds(0, few)])

    def share(buf, value, phase):
        buf[rows(c, s.t), :] = value
        each_col(lambda cc: remote(buf.at[rows(c, s.t)], buf.at[rows(c, s.t)], phase, r, cc).start())

    def shared(buf, phase):
        wait(m.recv, phase, buf.at[pl.ds(0, few * s.t)])
        unwaited.append((phase, buf.at[pl.ds(0, few * s.t)]))

    def scatter(a, value, phase):
        part_free(a)
        in_flight[a] = phase
        m.part[a] = value.astype(BF16)
        each_col(lambda cc: remote(m.part.at[a, rows(cc, s.t)], m.got.at[a, c], phase, r, cc).start())
        m.got[a, c] = m.part[a, rows(c, s.t), :]

    def scattered(a, phase):
        wait(m.recv, phase, m.got.at[a, pl.ds(0, few)])
        total = m.got[a, 0].astype(F32)
        for i in range(1, s.nc):
            total = total + m.got[a, i].astype(F32)
        return total

    def norm(u, l, a, gain, shift, n_ref, r_ref):
        mean = jnp.sum(u, axis=1, keepdims=True) / s.d
        var = jnp.sum(u * u, axis=1, keepdims=True) / s.d - mean * mean
        inv = lax.rsqrt(var + 1e-12)
        n = (u - mean) * inv
        n_ref[l, a] = n
        r_ref[l, a] = inv
        return n * vector(l, gain) + vector(l, shift)

    def add_row(ref, at, value):
        ref[at : at + 1, :] += jnp.sum(value, axis=0, keepdims=True)

    def norm_back(g, l, a, gain, shift, n_ref, r_ref):
        n = n_ref[l, a]
        w = g * vector(l, gain)
        first = jnp.sum(w, axis=1, keepdims=True) / s.d
        second = jnp.sum(w * n, axis=1, keepdims=True) / s.d
        add_row(m.vec, l * VEC_ROWS + gain, g * n)
        add_row(m.vec, l * VEC_ROWS + shift, g)
        return r_ref[l, a] * (w - first - n * second)

    low_lanes = lax.broadcasted_iota(jnp.int32, (s.qc, s.dc), 1) < HEAD_DIM

    def two_heads(block):
        block = block.astype(F32)
        return jnp.concatenate([jnp.where(low_lanes, block, 0.0), jnp.where(low_lanes, 0.0, block)], axis=0)

    def one_block(pair):
        return jnp.where(low_lanes, pair[: s.qc], pair[s.qc :])

    def keys(l, j, value):
        lanes = pl.ds(s.dc if value else 0, s.dc)
        return m.kv[l, :, :, pl.ds(j * s.qc, s.qc), lanes].reshape(s.nr * s.qc, s.dc)

    def swapped(l):
        m.wproj[l, rows(k, s.dr), rows(zx, s.dc)] = m.wp_own[l]
        m.wdown[l, rows(k, s.fr), rows(zx, s.dc)] = m.wd_own[l]

    pass_on(WQ, 0)

    def attend(l, i):
        queries = m.q2[l, i]
        ids = m.segq[i]
        scores = []
        for _, j in KEYS_OF[i]:
            raw = dot_nt(queries, keys(l, j, False))
            scores.append(jnp.where(ids == m.segk[j : j + 1, :], raw, -1e9))
        top = functools.reduce(jnp.maximum, [jnp.max(x, axis=1, keepdims=True) for x in scores])
        raised = [jnp.exp(x - top) for x in scores]
        inverse = 1.0 / sum(jnp.sum(x, axis=1, keepdims=True) for x in raised)
        out = jnp.zeros((2 * s.qc, s.dc), F32)
        for (n, j), x in zip(KEYS_OF[i], raised):
            prob = (x * inverse).astype(BF16)
            m.probs[l, n] = prob
            out = out + dot(prob, keys(l, j, True))
        m.att[l, i * s.qc : (i + 1) * s.qc, :] = one_block(out)

    def span(a):
        return pl.ds(a * s.half, s.half)

    for l in range(L):
        for a in range(2):
            if l:
                shared(m.xf.at[l, a], (H, l - 1, a))
            else:
                wait(m.recv, (X_IN, 0, a), m.xf.at[0, a, :, pl.ds(0, few * s.dc)])
                m.carry[a] = m.xf[0, a, rows(c, s.t), :].astype(F32)
            if a == 0:
                gathered(WQ, l)
            qkv = dot(m.xf[l, a], m.wqkv[l].reshape(s.d, 3 * s.dc))
            keep = (qkv[:, 2 * s.dc :] + m.vb[l : l + 1, :].astype(F32)).astype(BF16)
            m.kv[l, zx, k, span(a), : s.dc] = qkv[:, s.dc : 2 * s.dc].astype(BF16)
            m.kv[l, zx, k, span(a), s.dc :] = keep
            gather(KV0 + 2 * a, l)
            gather(KV1 + 2 * a, l)
            for i in range(2):
                block = (qkv[i * s.qc : (i + 1) * s.qc, : s.dc] + m.qb[l : l + 1, :].astype(F32)).astype(BF16)
                m.q2[l, 2 * a + i] = (two_heads(block) * HEAD_DIM ** (-0.5)).astype(BF16)
        if l == 0:
            @pl.when(at_home)
            def _():
                m.wp_own[...] = m.wp[...]
                m.wd_own[...] = m.wd[...]

            @pl.when(jnp.logical_not(at_home))
            def _():
                wait(m.recv, (WPT, 0, 0), m.wp_own)
                wait(m.recv, (WDT, 0, 0), m.wd_own)
            swapped(0)
            gather(WP, 0)
        for name in KV:
            forward(name, l)
        if l == 0:
            forward(WP, 0)
        for name in KV:
            pass_on(name, l)
        if l == 0:
            gather(WU, 0)
            gather(WD, 0)
            pass_on(WP, 0)
        else:
            pass_on(WU, 1)
            pass_on(WD, 1)
        gathered(KV0, l)
        attend(l, 0)
        gathered(KV1, l)
        gathered(KV2, l)
        attend(l, 1)
        gathered(KV3, l)
        gathered(WP, l)
        scatter(0, dot(m.att[l, span(0), :].astype(BF16), m.wproj[l]), (PR, l, 0))
        attend(l, 2)
        attend(l, 3)
        scatter(1, dot(m.att[l, span(1), :].astype(BF16), m.wproj[l]), (PR, l, 1))
        if l == 0:
            forward(WU, 0)
            forward(WD, 0)
            swapped(1)
        if l == 0:
            wait(m.recv, (PVEC, 0, 0), m.pv.at[:, pl.ds(0, few * s.dc)])
        for a in range(2):
            u = scattered(a, (PR, l, a)) + vector(l, PROJ_B) + m.carry[a]
            first_out = norm(u, l, a, GAIN1, SHIFT1, m.n1, m.r1)
            share(m.x1.at[l, a], first_out.astype(BF16), (N1, l, a))
            m.carry[a] = first_out
        if l == 0:
            pass_on(WU, 0)
            pass_on(WD, 0)
            gather(WQ, 1)
            gather(WP, 1)
        gathered(WU, l)
        for a in range(2):
            shared(m.x1.at[l, a], (N1, l, a))
            pre = dot(m.x1[l, a], m.wup[l].reshape(s.d, s.fc)) + m.upb[l : l + 1, :].astype(F32)
            cdf = 0.5 * (1.0 + lax.erf(pre * 0.5**0.5))
            m.gate[l, a] = (pre * cdf).astype(BF16)
            if a == 0:
                gathered(WD, l)
            scatter(a, dot(m.gate[l, a], m.wdown[l]), (FR, l, a))
            m.slope[l, a] = cdf + pre * (jnp.exp(-0.5 * pre * pre) * 0.3989422804014327)
        if l == 0:
            forward(WQ, 1)
            forward(WP, 1)
            gather(WU, 1)
            gather(WD, 1)
        for a in range(2):
            u = scattered(a, (FR, l, a)) + vector(l, DOWN_B) + m.carry[a]
            hidden = norm(u, l, a, GAIN2, SHIFT2, m.n2, m.r2)
            if l == 0:
                share(m.xf.at[1, a], hidden.astype(BF16), (H, 0, a))
                m.carry[a] = hidden
            else:
                m.act_out[a] = hidden.astype(BF16)
        if l == 0:
            pass_on(WQ, 1)
            pass_on(WP, 1)
            forward(WU, 1)
            forward(WD, 1)

    def swap_back(l, name, total):
        out, fin, phase = {GP: (m.gproj_out, m.gproj_fin, (GPT, l, 0)), GD: (m.gdown_out, m.gdown_fin, (GDT, l, 0))}[name]
        out[l] = total.astype(BF16)

        @pl.when(jnp.logical_not(at_home))
        def _():
            remote(out.at[l], fin.at[l], phase, swap_row, swap_col).start()

        @pl.when(at_home)
        def _():
            fin[l] = out[l]

    def swap_end(l, name, out):
        fin, phase = {GP: (m.gproj_fin, (GPT, l, 0)), GD: (m.gdown_fin, (GDT, l, 0))}[name]

        @pl.when(jnp.logical_not(at_home))
        def _():
            wait(m.recv, phase, fin.at[l])
        out[l] = fin[l].astype(F32)

    def attend_back(l, j):
        key_grad = jnp.zeros((s.nr * s.qc, s.dc), F32)
        value_grad = jnp.zeros((s.nr * s.qc, s.dc), F32)
        for n, i in QUERIES_OF[j]:
            prob = m.probs[l, n]
            prob_grad = dot_nt(m.do2[i], keys(l, j, True))
            score_grad = (prob.astype(F32) * (prob_grad - m.delta[i])).astype(BF16)
            m.dq2[i] += dot(score_grad, keys(l, j, False))
            key_grad = key_grad + dot_tn(score_grad, m.q2[l, i])
            value_grad = value_grad + dot_tn(prob, m.do2[i])
        shape = (s.nzx, 2, s.qc, s.dc)
        m.dkv[j, :, :, :, pl.ds(0, s.dc)] = key_grad.astype(BF16).reshape(shape)
        m.dkv[j, :, :, :, pl.ds(s.dc, s.dc)] = value_grad.astype(BF16).reshape(shape)

    wait(m.recv, (COTAN, 0, 0), m.cot.at[:, :, pl.ds(0, few * s.dc)])
    for l in reversed(range(L)):
        at = l * VEC_ROWS
        own = l * 2 * VEC_ROWS
        for a in range(2):
            if l + 1 < L:
                grad = scattered(a, (DX, l + 1, a)) + m.carry[a]
            else:
                grad = m.cot[a].astype(F32)
            dz = norm_back(grad, l, a, GAIN2, SHIFT2, m.n2, m.r2)
            m.carry[a] = dz
            low = dz.astype(BF16)
            share(m.dff.at[l, a], low, (DF, l, a))
            add_row(m.vec, at + DOWN_B, low.astype(F32))
        if l + 1 == L:
            each_col(lambda cc: remote(
                m.act_out.at[:, :, rows(cc, s.dc)], m.act_in.at[:, rows(c, s.t)], (ACT, 0, 0), r, cc).start())
            m.act_in[:, rows(c, s.t), :] = m.act_out[:, :, rows(c, s.dc)]
        else:
            reduce_mid(GQ, l + 1)
            reduce_turn(GU, l + 1)
            swap_back(l + 1, GD, reduce_end(GD, l + 1))
            swap_back(l + 1, GP, reduce_end(GP, l + 1))
        for a in range(2):
            shared(m.dff.at[l, a], (DF, l, a))
            de = (dot_nt(m.dff[l, a], m.wdown[l]) * m.slope[l, a]).astype(BF16)
            m.de[a] = de
            scatter(a, dot_nt(de, m.wup[l].reshape(s.d, s.fc)), (DN, l, a))
            sums = jnp.sum(de.astype(F32), axis=0, keepdims=True)
            for i in range(s.fc // LANES):
                m.own[own + i : own + i + 1, :] += sums[:, i * LANES : (i + 1) * LANES]
        if l + 1 < L:
            reduce_turn(GQ, l + 1)
            m.o_up[l + 1] = reduce_end(GU, l + 1)
            sent_half(GD, l + 1)
            sent_half(GU, l + 1)
        m.gdown[...] = dot_tn(m.gate[l].reshape(s.tok, s.fc), m.dff[l].reshape(s.tok, s.d)).astype(BF16)
        reduce_start(GD, l)
        for a in range(2):
            grad = scattered(a, (DN, l, a)) + m.carry[a]
            du = norm_back(grad, l, a, GAIN1, SHIFT1, m.n1, m.r1)
            m.carry[a] = du
            low = du.astype(BF16)
            share(m.drf.at[l, a], low, (DR, l, a))
            add_row(m.vec, at + PROJ_B, low.astype(F32))
        m.gup[...] = dot_tn(m.x1[l].reshape(s.tok, s.d), m.de[...].reshape(s.tok, s.fc)).astype(BF16).reshape(m.gup.shape)
        reduce_start(GU, l)
        reduce_mid(GD, l)
        if l + 1 < L:
            swap_end(l + 1, GD, m.o_down)
            swap_end(l + 1, GP, m.o_proj)
            total = reduce_end(GQ, l + 1)
            for which, out in enumerate((m.o_q, m.o_k, m.o_v)):
                out[l + 1] = total[:, which * s.dc : (which + 1) * s.dc]
        if l == 0:
            each_col(lambda cc: remote(m.vec.at[:, rows(cc, s.dc)], m.vec_in.at[c], (VEC, 0, 0), r, cc).start())
            m.vec_in[c] = m.vec[:, rows(c, s.dc)]
        if l + 1 < L:
            for name in DKV:
                sent_half(name, l + 1)
        for a in range(2):
            shared(m.drf.at[l, a], (DR, l, a))
            dout = dot_nt(m.drf[l, a], m.wproj[l]).astype(BF16)
            for b in range(2):
                i = 2 * a + b
                block = two_heads(dout[b * s.qc : (b + 1) * s.qc, :])
                kept = m.att[l, i * s.qc : (i + 1) * s.qc, :]
                m.do2[i] = block.astype(BF16)
                m.delta[i] = jnp.sum(block * jnp.concatenate([kept, kept], axis=0), axis=1, keepdims=True)
                m.dq2[i] = jnp.zeros((2 * s.qc, s.dc), F32)
            if a == 0:
                attend_back(l, 0)
                reduce_start(DKV0, l)
        if l + 1 < L:
            sent_half(GP, l + 1)
        m.gproj[...] = dot_tn(m.att[l].astype(BF16), m.drf[l].reshape(s.tok, s.d)).astype(BF16)
        reduce_start(GP, l)
        attend_back(l, 1)
        reduce_start(DKV1, l)
        reduce_mid(DKV0, l)
        attend_back(l, 2)
        reduce_start(DKV2, l)
        reduce_mid(DKV1, l)
        reduce_mid(GP, l)
        attend_back(l, 3)
        reduce_start(DKV3, l)
        reduce_mid(DKV2, l)
        for i in range(4):
            m.dqkv[i * s.qc : (i + 1) * s.qc, : s.dc] = (one_block(m.dq2[i]) * HEAD_DIM ** (-0.5)).astype(BF16)
        reduce_mid(DKV3, l)
        reduce_mid(GU, l)
        reduce_turn(GD, l)
        for a in range(2):
            for j in (2 * a, 2 * a + 1):
                m.dqkv[j * s.qc : (j + 1) * s.qc, s.dc :] = reduce_end(DKV0 + j, l).astype(BF16)
            back = dot_nt(m.dqkv[span(a), :], m.wqkv[l].reshape(s.d, 3 * s.dc))
            if l:
                scatter(a, back, (DX, l, a))
            else:
                part_free(a)
                m.part[a] = back.astype(BF16)
                mine = m.part[a, rows(c, s.t), :].astype(F32) + m.carry[a]
                m.part[a, rows(c, s.t), :] = mine.astype(BF16)
                each_col(lambda cc: remote(m.part.at[a, :, rows(cc, s.dc)], m.got_in.at[a, c], (DX, 0, a), r, cc).start())
                m.got_in[a, c] = m.part[a, :, rows(c, s.dc)]
        if l + 1 < L:
            sent_half(GQ, l + 1)
        if l == 0:
            wait(m.recv, (VEC, 0, 0), m.vec_in.at[pl.ds(0, few)])
            total = m.vec_in[0]
            for i in range(1, s.nc):
                total = total + m.vec_in[i]
            for i in range(L):
                to = i * 2 * VEC_ROWS + VEC_ROWS
                m.own[to : to + VEC_ROWS, :] = total[i * VEC_ROWS : (i + 1) * VEC_ROWS]
            m.own_in[r] = m.own[...]
            each_row(lambda rr: remote(m.own, m.own_in.at[r], (OWN, 0, 0), rr, c).start())
        m.gqkv[...] = dot_tn(m.xf[l].reshape(s.tok, s.d), m.dqkv[...]).astype(BF16).reshape(m.gqkv.shape)
        reduce_start(GQ, l)
        sums = jnp.sum(m.dqkv[...].astype(F32), axis=0, keepdims=True)
        late, to = (m.own, own + 4) if l else (m.late, 0)
        late[to : to + 1, :] = sums[:, : s.dc]
        late[to + 1 : to + 2, :] = sums[:, 2 * s.dc :]
        reduce_turn(GP, l)
        if l == 0:
            reduce_turn(GU, l)
            swap_back(l, GD, reduce_end(GD, l))

    m.late_in[r] = m.late[...]
    each_row(lambda rr: remote(m.late, m.late_in.at[r], (OWN, 0, 1), rr, c).start())
    reduce_mid(GQ, 0)
    wait(m.recv, (ACT, 0, 0), m.act_in.at[:, pl.ds(0, few * s.t)])
    m.o_act[...] = m.act_in[...]
    swap_back(0, GP, reduce_end(GP, 0))
    m.o_up[0] = reduce_end(GU, 0)
    reduce_turn(GQ, 0)
    swap_end(0, GD, m.o_down)
    for a in range(2):
        wait(m.recv, (DX, 0, a), m.got_in.at[a, pl.ds(0, few)])
        total = m.got_in[a, 0].astype(F32)
        for i in range(1, s.nc):
            total = total + m.got_in[a, i].astype(F32)
        m.o_in[a] = total
    wait(m.recv, (OWN, 0, 0), m.own_in.at[pl.ds(0, s.nr - 1)])
    total = m.own_in[0]
    for i in range(1, s.nr):
        total = total + m.own_in[i]
    m.o_vec[...] = total
    wait(m.recv, (OWN, 0, 1), m.late_in.at[pl.ds(0, s.nr - 1)])
    total = m.late_in[0]
    for i in range(1, s.nr):
        total = total + m.late_in[i]
    m.o_vec[4:6, :] = total[:2]
    total = reduce_end(GQ, 0)
    for which, out in enumerate((m.o_q, m.o_k, m.o_v)):
        out[0] = total[:, which * s.dc : (which + 1) * s.dc]
    swap_end(0, GP, m.o_proj)

    for phase, ref in unwaited:
        wait(m.send, phase, ref)
    for a in range(2):
        wait(m.send, (X_IN, 0, a), m.xf.at[0, a, :, pl.ds(0, few * s.dc)])
    wait(m.send, (PVEC, 0, 0), m.pv.at[:, pl.ds(0, few * s.dc)])
    wait(m.send, (COTAN, 0, 0), m.cot.at[:, :, pl.ds(0, few * s.dc)])
    wait(m.send, (ACT, 0, 0), m.act_in.at[:, pl.ds(0, few * s.t)])
    for a in range(2):
        wait(m.send, (DX, 0, a), m.got_in.at[a, pl.ds(0, few)])
    wait(m.send, (VEC, 0, 0), m.vec_in.at[pl.ds(0, few)])
    wait(m.send, (OWN, 0, 0), m.own_in.at[pl.ds(0, s.nr - 1)])
    wait(m.send, (OWN, 0, 1), m.late_in.at[pl.ds(0, s.nr - 1)])

    @pl.when(jnp.logical_not(at_home))
    def _():
        wait(m.send, (WPT, 0, 0), m.wp_own)
        wait(m.send, (WDT, 0, 0), m.wd_own)
        for l in range(L):
            wait(m.send, (GPT, l, 0), m.gproj_fin.at[l])
            wait(m.send, (GDT, l, 0), m.gdown_fin.at[l])
    for l in range(L):
        for name in (WQ, WP, WU, WD, *KV):
            sent_gather(name, l)
        for name in (GQ, GP, GU, GD, *DKV):
            sent_pieces(name, l)
    for name in (GQ, GP, GU, GD, *DKV):
        sent_half(name, 0)


def body(s, layer_input, query_weight, key_weight, value_weight, proj_weight, up_weight, down_weight, query_shift,
         value_shift, proj_shift, up_shift, down_shift, first_gain, first_shift, second_gain, second_shift, segment_ids,
         cotangent):
    L = LAYERS
    places = jnp.tile(segment_ids[: s.tok].reshape(4, s.qc), (1, LANES // s.qc))
    shapes = scratch_of(s)
    halves = (2, s.half, s.dc)
    square = jax.ShapeDtypeStruct((L, s.dr, s.dc), F32)
    out_shape = (
        jax.ShapeDtypeStruct((2, s.half, s.dc), BF16),
        jax.ShapeDtypeStruct((2, s.half, s.dc), F32),
        square, square, square, square,
        jax.ShapeDtypeStruct((L, s.dr, s.fc), F32),
        jax.ShapeDtypeStruct((L, s.fr, s.dc), F32),
        jax.ShapeDtypeStruct((L * 2 * VEC_ROWS, s.dc), F32),
    )
    vmem = pl.BlockSpec(memory_space=pltpu.VMEM)
    results = pl.pallas_call(
        functools.partial(kernel, s),
        out_shape=out_shape,
        in_specs=[vmem] * len(INPUTS),
        out_specs=[vmem] * len(OUTPUTS),
        scratch_shapes=[pltpu.VMEM(shape, dtype) for shape, dtype in shapes.values()]
        + [pltpu.SemaphoreType.DMA((len(KEYS),))] * 2,
        compiler_params=pltpu.CompilerParams(
            collective_id=0, has_side_effects=True, vmem_limit_bytes=60 * 2**20),
        name="encoder",
    )(layer_input.reshape(halves), cotangent.reshape(halves), query_weight, key_weight, value_weight, proj_weight, up_weight,
      down_weight, query_shift, value_shift, proj_shift, up_shift, down_shift, first_gain, first_shift, second_gain,
      second_shift, places)
    narrow, wide = jax.ShapeDtypeStruct((L, s.dc), F32), jax.ShapeDtypeStruct((L, s.fc), F32)
    o_act, o_in, *others = pl.pallas_call(
        functools.partial(hand_out, s),
        out_shape=out_shape[:-1] + (narrow,) * 3 + (wide,) + (narrow,) * 5,
        in_specs=[vmem] * len(OUTPUTS),
        out_specs=[vmem] * 17,
        name="results",
    )(*results)
    return (o_act.reshape(s.tok, s.dc), o_in.reshape(s.tok, s.dc), *others)


def hand_out(s, *refs):
    count = len(OUTPUTS)
    arrays, packed, outs = refs[: count - 1], refs[count - 1], refs[count:]
    for array, out in zip(arrays, outs):
        out[...] = array[...]
    qs, vs, ps, us, ds, fg, fs, sg, ss = outs[count - 1 :]
    for l in range(LAYERS):
        own = l * 2 * VEC_ROWS
        rows = [(qs, 4), (vs, 5)]
        rows += [(ref, VEC_ROWS + which) for ref, which in
                 ((ps, PROJ_B), (ds, DOWN_B), (fg, GAIN1), (fs, SHIFT1), (sg, GAIN2), (ss, SHIFT2))]
        for ref, at in rows:
            ref[l : l + 1, :] = packed[own + at : own + at + 1, :]
        for i in range(s.fc // LANES):
            us[l : l + 1, i * LANES : (i + 1) * LANES] = packed[own + i : own + i + 1, :]


def build(mesh, tok, d, ff):
    s = Sizes(mesh.shape["row"], mesh.shape["col"], tok, d, ff)
    return jax.shard_map(
        functools.partial(body, s),
        mesh=mesh,
        in_specs=(P("row", "col"),) + (P(None, "row", "col"),) * 6 + (P(None, "col"),) * 9 + (P(), P("row", "col")),
        out_specs=(P("row", "col"),) * 2 + (P(None, "row", "col"),) * 6 + (P(None, "col"),) * 9,
        check_vma=False,
    )


def solution(mesh):
    return build(mesh, 256, 1024, 4096)
```

```python
import functools
from types import SimpleNamespace

import jax
import jax.numpy as jnp
from jax import lax
from jax.experimental import pallas as pl
from jax.experimental.pallas import tpu as pltpu
from jax.sharding import PartitionSpec as P

MESH = pl.DeviceIdType.MESH
LAYERS = 2
HEAD_DIM = 64
LANES = 128
F32 = jnp.float32
BF16 = jnp.bfloat16
PAIRS = ((0, 0), (1, 1), (1, 2), (2, 1), (2, 2), (2, 3), (3, 2), (3, 3))
KEYS_OF = {i: [(n, j) for n, (a, j) in enumerate(PAIRS) if a == i] for i in range(4)}
QUERIES_OF = {j: [(n, i) for n, (i, b) in enumerate(PAIRS) if b == j] for j in range(4)}

PROJ_B, DOWN_B, GAIN1, SHIFT1, GAIN2, SHIFT2 = range(6)
VEC_ROWS = 8


def dot(a, b):
    return jnp.dot(a, b, preferred_element_type=F32)


def dot_nt(a, b):
    return lax.dot_general(a, b, (((1,), (1,)), ((), ())), preferred_element_type=F32)


def dot_tn(a, b):
    return lax.dot_general(a, b, (((0,), (0,)), ((), ())), preferred_element_type=F32)


class Sizes:
    def __init__(self, nr, nc, tok, d, ff):
        self.nr, self.nc, self.tok, self.d, self.ff = nr, nc, tok, d, ff
        self.half = tok // 2
        self.t = self.half // nc
        self.dc, self.fc = d // nc, ff // nc
        self.dr, self.fr = d // nr, ff // nr
        self.nz = nr // 4
        self.nzx = nr // 2
        self.qc = tok // 4


def scratch_of(s):
    L = LAYERS
    v = SimpleNamespace()
    v.xf = ((L, 2, s.half, s.d), BF16)
    v.x1 = ((L, 2, s.half, s.d), BF16)
    v.dff = ((L, 2, s.half, s.d), BF16)
    v.drf = ((L, 2, s.half, s.d), BF16)
    v.part = ((2, s.half, s.d), BF16)
    v.got = ((2, s.nc, s.t, s.d), BF16)
    v.got_in = ((2, s.nc, s.half, s.dc), BF16)
    v.act_out = ((2, s.t, s.d), BF16)
    v.act_in = ((2, s.half, s.dc), BF16)
    v.cot = ((2, s.t, s.d), BF16)
    v.pv = ((L * VEC_ROWS, s.d), F32)
    v.kv = ((L, s.nzx, 2, s.tok, 2 * s.dc), BF16)
    v.dkv = ((4, s.nzx, 2, s.qc, 2 * s.dc), BF16)
    v.dkv_c = ((L, 4, s.nzx, s.qc, 2 * s.dc), BF16)
    v.dkv_in = ((L, 4, s.nzx, s.qc, 2 * s.dc), BF16)
    v.probs = ((L, len(PAIRS), 2 * s.qc, s.nr * s.qc), BF16)
    v.q2 = ((L, 4, 2 * s.qc, s.dc), BF16)
    v.do2 = ((4, 2 * s.qc, s.dc), BF16)
    v.delta = ((4, 2 * s.qc, 1), F32)
    v.dq2 = ((4, 2 * s.qc, s.dc), F32)
    v.att = ((L, s.tok, s.dc), F32)
    v.gate = ((L, 2, s.half, s.fc), BF16)
    v.slope = ((L, 2, s.half, s.fc), F32)
    v.de = ((2, s.half, s.fc), BF16)
    v.n1 = ((L, 2, s.t, s.d), F32)
    v.n2 = ((L, 2, s.t, s.d), F32)
    v.r1 = ((L, 2, s.t, 1), F32)
    v.r2 = ((L, 2, s.t, 1), F32)
    v.carry = ((2, s.t, s.d), F32)
    v.dqkv = ((s.tok, 3 * s.dc), BF16)
    v.wqkv = ((L, s.nzx, 2, s.dr, 3 * s.dc), BF16)
    v.wup = ((L, s.nzx, 2, s.dr, s.fc), BF16)
    v.wproj = ((L, s.dc, s.d), BF16)
    v.wdown = ((L, s.fc, s.d), BF16)
    v.wp_own = ((L, s.dr, s.dc), BF16)
    v.wd_own = ((L, s.fr, s.dc), BF16)
    v.gqkv = ((s.nzx, 2, s.dr, 3 * s.dc), BF16)
    v.gup = ((s.nzx, 2, s.dr, s.fc), BF16)
    v.gproj = ((s.dc, s.d), BF16)
    v.gdown = ((s.fc, s.d), BF16)
    v.gqkv_c = ((L, s.nzx, s.dr, 3 * s.dc), BF16)
    v.gup_c = ((L, s.nzx, s.dr, s.fc), BF16)
    v.gproj_c = ((L, s.dr, s.d), BF16)
    v.gdown_c = ((L, s.fr, s.d), BF16)
    v.gqkv_in = ((L, s.nzx, s.dr, 3 * s.dc), BF16)
    v.gup_in = ((L, s.nzx, s.dr, s.fc), BF16)
    v.gproj_in = ((L, s.dr, s.d), BF16)
    v.t_gq, v.t_gp = ((s.dr, 3 * s.dc), F32), ((s.dr, s.dc), F32)
    v.t_gu, v.t_gd = ((s.dr, s.fc), F32), ((s.fr, s.dc), F32)
    v.t_gq_out = v.t_gq_in = ((L, s.dr, 3 * s.dc), BF16)
    v.t_gp_out = v.t_gp_in = ((L, s.dr, s.dc), BF16)
    v.t_gu_out = v.t_gu_in = ((L, s.dr, s.fc), BF16)
    v.t_gd_out = v.t_gd_in = ((L, s.fr, s.dc), BF16)
    v.gdown_in = ((L, s.fr, s.d), BF16)
    v.gproj_out = ((L, s.dr, s.dc), BF16)
    v.gdown_out = ((L, s.fr, s.dc), BF16)
    v.gproj_fin = ((L, s.dr, s.dc), BF16)
    v.gdown_fin = ((L, s.fr, s.dc), BF16)
    v.vec = ((L * VEC_ROWS, s.d), F32)
    v.vec_in = ((s.nc, L * VEC_ROWS, s.dc), F32)
    v.segq = ((4, 2 * s.qc, 1), jnp.int32)
    v.segk = ((4, s.nr * s.qc), jnp.int32)
    v.own = ((L * 2 * VEC_ROWS, s.dc), F32)
    v.late = ((VEC_ROWS, s.dc), F32)
    v.late_in = ((s.nr, VEC_ROWS, s.dc), F32)
    v.own_in = ((s.nr, L * 2 * VEC_ROWS, s.dc), F32)
    return vars(v)


INPUTS = tuple(dict(x=0, cotan=0, wq=0, wk=0, wv=0, wp=0, wu=0, wd=0, qb=0, vb=0, pb=0, upb=0, db=0, g1=0, s1=0, g2=0, s2=0,
                    places=0))
OUTPUTS = tuple(dict(o_act=0, o_in=0, o_q=0, o_k=0, o_v=0, o_proj=0, o_up=0, o_down=0, o_vec=0))

(X_IN, COTAN, PVEC, ACT, VEC, OWN, WPT, WDT, GPT, GDT, PR, N1, FR, H, DF, DN, DR, DX,
 WQ, WP, WU, WD, KV0, KV1, KV2, KV3, DKV0, DKV1, DKV2, DKV3, GQ, GP, GU, GD) = range(34)
CORE, ACROSS = 1, 2
IN_STEPS = {(n, l) for n in (WP, WU, WD, KV0, KV1, KV2, KV3, GP, GU, GD) for l in range(LAYERS)} | {(WQ, 1), (GQ, 0), (GQ, 1)}
KV = {KV0: 0, KV1: 1, KV2: 2, KV3: 3}
DKV = {DKV0: 0, DKV1: 1, DKV2: 2, DKV3: 3}
KEYS = (
    [(X_IN, 0, 1), (OWN, 0, 1)] + [(n, 0, 0) for n in range(X_IN, GPT)]
    + [(n, l, 0) for n in range(GPT, PR) for l in range(LAYERS)]
    + [(n, l, a) for n in range(PR, WQ) for l in range(LAYERS) for a in range(2)]
    + [(n, l, step) for n in range(WQ, GD + 1) for l in range(LAYERS) for step in range(3)]
)
PHASE = {key: index for index, key in enumerate(KEYS)}


def kernel(s, *refs):
    names = INPUTS + OUTPUTS + tuple(scratch_of(s)) + ("send", "recv")
    m = SimpleNamespace(**dict(zip(names, refs)))
    L = LAYERS
    r, c = lax.axis_index("row"), lax.axis_index("col")
    zx, k = lax.div(r, 2), lax.rem(r, 2)
    z, x = lax.div(zx, 2), lax.rem(zx, 2)
    across = z * 2 + 1 - x
    other = zx * 2 + 1 - k
    at_home = zx == c
    chips, few = s.nzx - 1, s.nc - 1

    def remote(src, dst, phase, row, col):
        return pltpu.make_async_remote_copy(
            src_ref=src, dst_ref=dst, send_sem=m.send.at[PHASE[phase]], recv_sem=m.recv.at[PHASE[phase]],
            device_id=(row, col), device_id_type=MESH)

    def wait(sems, phase, ref):
        pltpu.make_async_copy(ref, ref, sems.at[PHASE[phase]]).wait()

    def each_col(fn):
        def step(q, carry):
            fn(lax.rem(c + q, s.nc))
            return carry
        lax.fori_loop(1, s.nc, step, 0)

    def each_row(fn):
        def step(q, carry):
            fn(lax.rem(r + q, s.nr))
            return carry
        lax.fori_loop(1, s.nr, step, 0)

    def each_chip(fn):
        def step(q, carry):
            fn(lax.rem(zx + q, s.nzx))
            return carry
        lax.fori_loop(1, s.nzx, step, 0)

    def each_z(fn):
        def step(q, carry):
            fn(lax.rem(z + q, s.nz))
            return carry
        lax.fori_loop(1, s.nz, step, 0)

    def rows(i, n):
        return pl.ds(pl.multiple_of(i * n, n), n)

    barrier = pltpu.get_barrier_semaphore()

    def greet(row, col):
        pl.semaphore_signal(barrier, inc=1, device_id=(row, col), device_id_type=MESH)

    swap_row, swap_col = c * 2 + k, zx
    each_col(lambda cc: greet(r, cc))
    each_row(lambda rr: greet(rr, c))

    @pl.when(jnp.logical_not(at_home))
    def _():
        greet(swap_row, swap_col)

    def weight(name, l):
        chips = s.nzx - (2 if (name, l) in IN_STEPS else 1)
        if name in KV:
            span = pl.ds(KV[name] * s.qc, s.qc)
            return ((lambda i, kk: m.kv.at[l, i, kk, span]), (lambda kk: m.kv.at[l, :, kk, span]),
                    m.kv.at[l, pl.ds(0, chips), 0, span] if chips else None)
        if name in (WQ, WU):
            ref = {WQ: m.wqkv, WU: m.wup}[name]
            return (lambda i, kk: ref.at[l, i, kk]), (lambda kk: ref.at[l, :, kk]), \
                ref.at[l, pl.ds(0, chips), 0] if chips else None
        ref, n = {WP: (m.wproj, s.dr), WD: (m.wdown, s.fr)}[name]
        return ((lambda i, kk: ref.at[l, rows(kk, n), rows(i, s.dc)]), (lambda kk: ref.at[l, rows(kk, n)]),
                ref.at[l, pl.ds(0, n), pl.ds(0, chips * s.dc)] if chips else None)

    def gather(name, l):
        piece = weight(name, l)[0](zx, k)
        if (name, l) not in IN_STEPS:
            each_chip(lambda i: remote(piece, piece, (name, l, 0), i * 2 + k, c).start())
            return
        remote(piece, piece, (name, l, ACROSS), across * 2 + k, c).start()
        each_z(lambda i: remote(piece, piece, (name, l, 0), (i * 2 + x) * 2 + k, c).start())

    def forward(name, l):
        piece = weight(name, l)[0](across, k)
        wait(m.recv, (name, l, ACROSS), piece)
        each_z(lambda i: remote(piece, piece, (name, l, 0), (i * 2 + x) * 2 + k, c).start())

    def pass_on(name, l):
        _, half, many = weight(name, l)
        if many is not None:
            wait(m.recv, (name, l, 0), many)
        remote(half(k), half(k), (name, l, CORE), other, c).start()

    def gathered(name, l):
        wait(m.recv, (name, l, CORE), weight(name, l)[1](1 - k))

    def sent_gather(name, l):
        piece, half, many = weight(name, l)
        if many is not None:
            wait(m.send, (name, l, 0), many)
        if (name, l) in IN_STEPS:
            wait(m.send, (name, l, ACROSS), piece(zx, k))
        wait(m.send, (name, l, CORE), half(k))

    def partial_sum(name, l):
        if name in DKV:
            a = DKV[name]
            mid, got = m.dkv_c.at[l, a], m.dkv_in.at[l, a]
            return (lambda kk: m.dkv.at[a, :, kk]), mid, (lambda i: mid.at[i]), got
        if name in (GQ, GU):
            full, mid, got = {GQ: (m.gqkv, m.gqkv_c.at[l], m.gqkv_in.at[l]),
                              GU: (m.gup, m.gup_c.at[l], m.gup_in.at[l])}[name]
            return (lambda kk: full.at[:, kk]), mid, (lambda i: mid.at[i]), got
        full, mid, got, n = {GP: (m.gproj, m.gproj_c.at[l], m.gproj_in.at[l], s.dr),
                             GD: (m.gdown, m.gdown_c.at[l], m.gdown_in.at[l], s.fr)}[name]
        return (lambda kk: full.at[rows(kk, n)]), mid, (lambda i: mid.at[:, rows(i, s.dc)]), got

    def reduce_start(name, l):
        half, mid, _, _ = partial_sum(name, l)
        remote(half(1 - k), mid, (name, l, CORE), other, c).start()

    def both(name, mid, i):
        if name in (GP, GD):
            return mid.at[:, rows(i, 2 * s.dc)]
        return mid.at[pl.ds(2 * i, 2)]

    def m_pair(name, got, i):
        if name in (GP, GD):
            return got.at[:, rows(i, 2 * s.dc)]
        return got.at[pl.ds(2 * i, 2)]

    def reduce_turn(name, l):
        _, mid, piece, got = partial_sum(name, l)
        if s.nz > 1:
            wait(m.recv, (name, l, 0), m_all(name, got))
        sums = []
        for which in (x, 1 - x):
            total = piece(z * 2 + which)[...].astype(F32)
            for q in range(1, s.nz):
                i = lax.rem(z + q, s.nz) * 2 + which
                arrived = got[:, rows(i, s.dc)] if name in (GP, GD) else got[i]
                total = total + arrived.astype(F32)
            sums.append(total)
        kept, out, back = turned(name, l)
        kept[...] = sums[0]
        out[...] = sums[1].astype(BF16)
        remote(out, back, (name, l, ACROSS), across * 2 + k, c).start()

    def turned(name, l):
        return {GQ: (m.t_gq, m.t_gq_out.at[l], m.t_gq_in.at[l]), GP: (m.t_gp, m.t_gp_out.at[l], m.t_gp_in.at[l]),
                GU: (m.t_gu, m.t_gu_out.at[l], m.t_gu_in.at[l]), GD: (m.t_gd, m.t_gd_out.at[l], m.t_gd_in.at[l])}[name]

    def m_all(name, got):
        if name in (GP, GD):
            return got.at[:, pl.ds(0, 2 * (s.nz - 1) * s.dc)]
        return got.at[pl.ds(0, 2 * (s.nz - 1))]

    def reduce_mid(name, l):
        half, mid, piece, got = partial_sum(name, l)
        wait(m.recv, (name, l, CORE), mid)
        mid[...] = (half(k)[...].astype(F32) + mid[...].astype(F32)).astype(BF16)
        if (name, l) in IN_STEPS:
            each_z(lambda i: remote(both(name, mid, i), m_pair(name, got, z), (name, l, 0), (i * 2 + x) * 2 + k, c).start())
            return
        each_chip(lambda i: remote(piece(i), got.at[zx], (name, l, 0), i * 2 + k, c).start())
        got[zx] = piece(zx)[...]

    def reduce_end(name, l):
        if (name, l) in IN_STEPS:
            kept, _, back = turned(name, l)
            wait(m.recv, (name, l, ACROSS), back)
            return kept[...] + back[...].astype(F32)
        got = partial_sum(name, l)[3]
        wait(m.recv, (name, l, 0), got.at[pl.ds(0, chips)])
        total = got[0].astype(F32)
        for i in range(1, s.nzx):
            total = total + got[i].astype(F32)
        return total

    def sent_half(name, l):
        wait(m.send, (name, l, CORE), partial_sum(name, l)[1])

    def sent_pieces(name, l):
        if (name, l) in IN_STEPS:
            if s.nz > 1:
                wait(m.send, (name, l, 0), m_all(name, partial_sum(name, l)[3]))
            wait(m.send, (name, l, ACROSS), turned(name, l)[1])
            return
        wait(m.send, (name, l, 0), partial_sum(name, l)[3].at[pl.ds(0, chips)])

    m.xf[0, :, :, rows(c, s.dc)] = m.x[...]
    m.cot[:, :, rows(c, s.dc)] = m.cotan[:, rows(c, s.t), :]
    m.pv[:, rows(c, s.dc)] = jnp.zeros((L * VEC_ROWS, s.dc), F32)
    for l in range(L):
        for which, ref in enumerate((m.pb, m.db, m.g1, m.s1, m.g2, m.s2)):
            m.pv[l * VEC_ROWS + which : l * VEC_ROWS + which + 1, rows(c, s.dc)] = ref[l : l + 1, :].astype(F32)
        for which, ref in enumerate((m.wq, m.wk, m.wv)):
            m.wqkv[l, zx, k, :, which * s.dc : (which + 1) * s.dc] = ref[l]
        m.wup[l, zx, k] = m.wu[l]

    pl.semaphore_wait(barrier, s.nc - 1 + s.nr - 1 + 1 - at_home.astype(jnp.int32))

    def send_x(a):
        each_col(lambda cc: remote(m.x.at[a], m.xf.at[0, a, :, rows(c, s.dc)], (X_IN, 0, a), r, cc).start())

    send_x(0)
    gather(WQ, 0)
    send_x(1)

    @pl.when(jnp.logical_not(at_home))
    def _():
        remote(m.wp, m.wp_own, (WPT, 0, 0), swap_row, swap_col).start()
        remote(m.wd, m.wd_own, (WDT, 0, 0), swap_row, swap_col).start()
    mine = m.pv.at[:, rows(c, s.dc)]
    each_col(lambda cc: remote(mine, mine, (PVEC, 0, 0), r, cc).start())
    square = (s.qc, s.qc)
    diagonal = lax.broadcasted_iota(jnp.int32, square, 0) == lax.broadcasted_iota(jnp.int32, square, 1)
    for i in range(4):
        numbers = m.places[i : i + 1, :]
        column = jnp.sum(jnp.where(diagonal, numbers[:, : s.qc], 0), axis=1, keepdims=True)
        m.segq[i] = jnp.concatenate([column, column], axis=0)
        m.segk[i : i + 1, :] = jnp.concatenate([numbers] * (s.nr * s.qc // numbers.shape[1]), axis=1)
    m.vec[...] = jnp.zeros(m.vec.shape, F32)
    m.own[...] = jnp.zeros(m.own.shape, F32)
    m.late[...] = jnp.zeros(m.late.shape, F32)

    def vector(l, which):
        return m.pv[l * VEC_ROWS + which : l * VEC_ROWS + which + 1, :]

    unwaited = []
    in_flight = [None, None]

    def part_free(a):
        if in_flight[a] is not None:
            wait(m.send, in_flight[a], m.got.at[a, pl.ds(0, few)])

    def share(buf, value, phase):
        buf[rows(c, s.t), :] = value
        each_col(lambda cc: remote(buf.at[rows(c, s.t)], buf.at[rows(c, s.t)], phase, r, cc).start())

    def shared(buf, phase):
        wait(m.recv, phase, buf.at[pl.ds(0, few * s.t)])
        unwaited.append((phase, buf.at[pl.ds(0, few * s.t)]))

    def scatter(a, value, phase):
        part_free(a)
        in_flight[a] = phase
        m.part[a] = value.astype(BF16)
        each_col(lambda cc: remote(m.part.at[a, rows(cc, s.t)], m.got.at[a, c], phase, r, cc).start())
        m.got[a, c] = m.part[a, rows(c, s.t), :]

    def scattered(a, phase):
        wait(m.recv, phase, m.got.at[a, pl.ds(0, few)])
        total = m.got[a, 0].astype(F32)
        for i in range(1, s.nc):
            total = total + m.got[a, i].astype(F32)
        return total

    def norm(u, l, a, gain, shift, n_ref, r_ref):
        mean = jnp.sum(u, axis=1, keepdims=True) / s.d
        var = jnp.sum(u * u, axis=1, keepdims=True) / s.d - mean * mean
        inv = lax.rsqrt(var + 1e-12)
        n = (u - mean) * inv
        n_ref[l, a] = n
        r_ref[l, a] = inv
        return n * vector(l, gain) + vector(l, shift)

    def add_row(ref, at, value):
        ref[at : at + 1, :] += jnp.sum(value, axis=0, keepdims=True)

    def norm_back(g, l, a, gain, shift, n_ref, r_ref):
        n = n_ref[l, a]
        w = g * vector(l, gain)
        first = jnp.sum(w, axis=1, keepdims=True) / s.d
        second = jnp.sum(w * n, axis=1, keepdims=True) / s.d
        add_row(m.vec, l * VEC_ROWS + gain, g * n)
        add_row(m.vec, l * VEC_ROWS + shift, g)
        return r_ref[l, a] * (w - first - n * second)

    low_lanes = lax.broadcasted_iota(jnp.int32, (s.qc, s.dc), 1) < HEAD_DIM

    def two_heads(block):
        block = block.astype(F32)
        return jnp.concatenate([jnp.where(low_lanes, block, 0.0), jnp.where(low_lanes, 0.0, block)], axis=0)

    def one_block(pair):
        return jnp.where(low_lanes, pair[: s.qc], pair[s.qc :])

    def keys(l, j, value):
        lanes = pl.ds(s.dc if value else 0, s.dc)
        return m.kv[l, :, :, pl.ds(j * s.qc, s.qc), lanes].reshape(s.nr * s.qc, s.dc)

    def swapped(l):
        m.wproj[l, rows(k, s.dr), rows(zx, s.dc)] = m.wp_own[l]
        m.wdown[l, rows(k, s.fr), rows(zx, s.dc)] = m.wd_own[l]

    pass_on(WQ, 0)

    def attend(l, i):
        queries = m.q2[l, i]
        ids = m.segq[i]
        scores = []
        for _, j in KEYS_OF[i]:
            raw = dot_nt(queries, keys(l, j, False))
            scores.append(jnp.where(ids == m.segk[j : j + 1, :], raw, -1e9))
        top = functools.reduce(jnp.maximum, [jnp.max(x, axis=1, keepdims=True) for x in scores])
        raised = [jnp.exp(x - top) for x in scores]
        inverse = 1.0 / sum(jnp.sum(x, axis=1, keepdims=True) for x in raised)
        out = jnp.zeros((2 * s.qc, s.dc), F32)
        for (n, j), x in zip(KEYS_OF[i], raised):
            prob = (x * inverse).astype(BF16)
            m.probs[l, n] = prob
            out = out + dot(prob, keys(l, j, True))
        m.att[l, i * s.qc : (i + 1) * s.qc, :] = one_block(out)

    def span(a):
        return pl.ds(a * s.half, s.half)

    for l in range(L):
        for a in range(2):
            if l:
                shared(m.xf.at[l, a], (H, l - 1, a))
            else:
                wait(m.recv, (X_IN, 0, a), m.xf.at[0, a, :, pl.ds(0, few * s.dc)])
                m.carry[a] = m.xf[0, a, rows(c, s.t), :].astype(F32)
            if a == 0:
                gathered(WQ, l)
            qkv = dot(m.xf[l, a], m.wqkv[l].reshape(s.d, 3 * s.dc))
            keep = (qkv[:, 2 * s.dc :] + m.vb[l : l + 1, :].astype(F32)).astype(BF16)
            m.kv[l, zx, k, span(a), : s.dc] = qkv[:, s.dc : 2 * s.dc].astype(BF16)
            m.kv[l, zx, k, span(a), s.dc :] = keep
            gather(KV0 + 2 * a, l)
            gather(KV1 + 2 * a, l)
            for i in range(2):
                block = (qkv[i * s.qc : (i + 1) * s.qc, : s.dc] + m.qb[l : l + 1, :].astype(F32)).astype(BF16)
                m.q2[l, 2 * a + i] = (two_heads(block) * HEAD_DIM ** (-0.5)).astype(BF16)
        if l == 0:
            @pl.when(at_home)
            def _():
                m.wp_own[...] = m.wp[...]
                m.wd_own[...] = m.wd[...]

            @pl.when(jnp.logical_not(at_home))
            def _():
                wait(m.recv, (WPT, 0, 0), m.wp_own)
                wait(m.recv, (WDT, 0, 0), m.wd_own)
            swapped(0)
            gather(WP, 0)
        for name in KV:
            forward(name, l)
        if l == 0:
            forward(WP, 0)
        for name in KV:
            pass_on(name, l)
        if l == 0:
            gather(WU, 0)
            gather(WD, 0)
            pass_on(WP, 0)
        else:
            forward(WU, 1)
            forward(WD, 1)
        gathered(KV0, l)
        attend(l, 0)
        gathered(KV1, l)
        gathered(KV2, l)
        attend(l, 1)
        gathered(KV3, l)
        gathered(WP, l)
        scatter(0, dot(m.att[l, span(0), :].astype(BF16), m.wproj[l]), (PR, l, 0))
        attend(l, 2)
        attend(l, 3)
        scatter(1, dot(m.att[l, span(1), :].astype(BF16), m.wproj[l]), (PR, l, 1))
        if l == 0:
            forward(WU, 0)
            forward(WD, 0)
            swapped(1)
        if l == 0:
            wait(m.recv, (PVEC, 0, 0), m.pv.at[:, pl.ds(0, few * s.dc)])
        for a in range(2):
            u = scattered(a, (PR, l, a)) + vector(l, PROJ_B) + m.carry[a]
            first_out = norm(u, l, a, GAIN1, SHIFT1, m.n1, m.r1)
            share(m.x1.at[l, a], first_out.astype(BF16), (N1, l, a))
            m.carry[a] = first_out
        pass_on(WU, l)
        pass_on(WD, l)
        if l == 0:
            gather(WQ, 1)
            gather(WP, 1)
        else:
            each_col(lambda cc: remote(
                m.cotan.at[:, rows(cc, s.t)], m.cot.at[:, :, rows(c, s.dc)], (COTAN, 0, 0), r, cc).start())
        gathered(WU, l)
        for a in range(2):
            shared(m.x1.at[l, a], (N1, l, a))
            pre = dot(m.x1[l, a], m.wup[l].reshape(s.d, s.fc)) + m.upb[l : l + 1, :].astype(F32)
            cdf = 0.5 * (1.0 + lax.erf(pre * 0.5**0.5))
            m.gate[l, a] = (pre * cdf).astype(BF16)
            if a == 0:
                gathered(WD, l)
            scatter(a, dot(m.gate[l, a], m.wdown[l]), (FR, l, a))
            m.slope[l, a] = cdf + pre * (jnp.exp(-0.5 * pre * pre) * 0.3989422804014327)
        if l == 0:
            forward(WQ, 1)
            forward(WP, 1)
            gather(WU, 1)
            gather(WD, 1)
        for a in range(2):
            u = scattered(a, (FR, l, a)) + vector(l, DOWN_B) + m.carry[a]
            hidden = norm(u, l, a, GAIN2, SHIFT2, m.n2, m.r2)
            if l == 0:
                share(m.xf.at[1, a], hidden.astype(BF16), (H, 0, a))
                m.carry[a] = hidden
            else:
                m.act_out[a] = hidden.astype(BF16)
        if l == 0:
            pass_on(WQ, 1)
            pass_on(WP, 1)

    def swap_back(l, name, total):
        out, fin, phase = {GP: (m.gproj_out, m.gproj_fin, (GPT, l, 0)), GD: (m.gdown_out, m.gdown_fin, (GDT, l, 0))}[name]
        out[l] = total.astype(BF16)

        @pl.when(jnp.logical_not(at_home))
        def _():
            remote(out.at[l], fin.at[l], phase, swap_row, swap_col).start()

        @pl.when(at_home)
        def _():
            fin[l] = out[l]

    def swap_end(l, name, out):
        fin, phase = {GP: (m.gproj_fin, (GPT, l, 0)), GD: (m.gdown_fin, (GDT, l, 0))}[name]

        @pl.when(jnp.logical_not(at_home))
        def _():
            wait(m.recv, phase, fin.at[l])
        out[l] = fin[l].astype(F32)

    def attend_back(l, j):
        key_grad = jnp.zeros((s.nr * s.qc, s.dc), F32)
        value_grad = jnp.zeros((s.nr * s.qc, s.dc), F32)
        for n, i in QUERIES_OF[j]:
            prob = m.probs[l, n]
            prob_grad = dot_nt(m.do2[i], keys(l, j, True))
            score_grad = (prob.astype(F32) * (prob_grad - m.delta[i])).astype(BF16)
            m.dq2[i] += dot(score_grad, keys(l, j, False))
            key_grad = key_grad + dot_tn(score_grad, m.q2[l, i])
            value_grad = value_grad + dot_tn(prob, m.do2[i])
        shape = (s.nzx, 2, s.qc, s.dc)
        m.dkv[j, :, :, :, pl.ds(0, s.dc)] = key_grad.astype(BF16).reshape(shape)
        m.dkv[j, :, :, :, pl.ds(s.dc, s.dc)] = value_grad.astype(BF16).reshape(shape)

    wait(m.recv, (COTAN, 0, 0), m.cot.at[:, :, pl.ds(0, few * s.dc)])
    for l in reversed(range(L)):
        at = l * VEC_ROWS
        own = l * 2 * VEC_ROWS
        for a in range(2):
            if l + 1 < L:
                grad = scattered(a, (DX, l + 1, a)) + m.carry[a]
            else:
                grad = m.cot[a].astype(F32)
            dz = norm_back(grad, l, a, GAIN2, SHIFT2, m.n2, m.r2)
            m.carry[a] = dz
            low = dz.astype(BF16)
            share(m.dff.at[l, a], low, (DF, l, a))
            add_row(m.vec, at + DOWN_B, low.astype(F32))
        if l + 1 == L:
            each_col(lambda cc: remote(
                m.act_out.at[:, :, rows(cc, s.dc)], m.act_in.at[:, rows(c, s.t)], (ACT, 0, 0), r, cc).start())
            m.act_in[:, rows(c, s.t), :] = m.act_out[:, :, rows(c, s.dc)]
        else:
            reduce_mid(GQ, l + 1)
            reduce_turn(GU, l + 1)
            swap_back(l + 1, GD, reduce_end(GD, l + 1))
            swap_back(l + 1, GP, reduce_end(GP, l + 1))
        for a in range(2):
            shared(m.dff.at[l, a], (DF, l, a))
            de = (dot_nt(m.dff[l, a], m.wdown[l]) * m.slope[l, a]).astype(BF16)
            m.de[a] = de
            scatter(a, dot_nt(de, m.wup[l].reshape(s.d, s.fc)), (DN, l, a))
            sums = jnp.sum(de.astype(F32), axis=0, keepdims=True)
            for i in range(s.fc // LANES):
                m.own[own + i : own + i + 1, :] += sums[:, i * LANES : (i + 1) * LANES]
        if l + 1 < L:
            reduce_turn(GQ, l + 1)
            m.o_up[l + 1] = reduce_end(GU, l + 1)
            sent_half(GD, l + 1)
            sent_half(GU, l + 1)
        m.gdown[...] = dot_tn(m.gate[l].reshape(s.tok, s.fc), m.dff[l].reshape(s.tok, s.d)).astype(BF16)
        reduce_start(GD, l)
        for a in range(2):
            grad = scattered(a, (DN, l, a)) + m.carry[a]
            du = norm_back(grad, l, a, GAIN1, SHIFT1, m.n1, m.r1)
            m.carry[a] = du
            low = du.astype(BF16)
            share(m.drf.at[l, a], low, (DR, l, a))
            add_row(m.vec, at + PROJ_B, low.astype(F32))
        m.gup[...] = dot_tn(m.x1[l].reshape(s.tok, s.d), m.de[...].reshape(s.tok, s.fc)).astype(BF16).reshape(m.gup.shape)
        reduce_start(GU, l)
        reduce_mid(GD, l)
        if l + 1 < L:
            swap_end(l + 1, GD, m.o_down)
            swap_end(l + 1, GP, m.o_proj)
            total = reduce_end(GQ, l + 1)
            for which, out in enumerate((m.o_q, m.o_k, m.o_v)):
                out[l + 1] = total[:, which * s.dc : (which + 1) * s.dc]
        if l == 0:
            each_col(lambda cc: remote(m.vec.at[:, rows(cc, s.dc)], m.vec_in.at[c], (VEC, 0, 0), r, cc).start())
            m.vec_in[c] = m.vec[:, rows(c, s.dc)]
        if l + 1 < L:
            for name in DKV:
                sent_half(name, l + 1)
        for a in range(2):
            shared(m.drf.at[l, a], (DR, l, a))
            dout = dot_nt(m.drf[l, a], m.wproj[l]).astype(BF16)
            for b in range(2):
                i = 2 * a + b
                block = two_heads(dout[b * s.qc : (b + 1) * s.qc, :])
                kept = m.att[l, i * s.qc : (i + 1) * s.qc, :]
                m.do2[i] = block.astype(BF16)
                m.delta[i] = jnp.sum(block * jnp.concatenate([kept, kept], axis=0), axis=1, keepdims=True)
                m.dq2[i] = jnp.zeros((2 * s.qc, s.dc), F32)
            if a == 0:
                attend_back(l, 0)
                reduce_start(DKV0, l)
        if l + 1 < L:
            sent_half(GP, l + 1)
        m.gproj[...] = dot_tn(m.att[l].astype(BF16), m.drf[l].reshape(s.tok, s.d)).astype(BF16)
        reduce_start(GP, l)
        attend_back(l, 1)
        reduce_start(DKV1, l)
        reduce_mid(DKV0, l)
        attend_back(l, 2)
        reduce_start(DKV2, l)
        reduce_mid(DKV1, l)
        reduce_mid(GP, l)
        attend_back(l, 3)
        reduce_start(DKV3, l)
        reduce_mid(DKV2, l)
        for i in range(4):
            m.dqkv[i * s.qc : (i + 1) * s.qc, : s.dc] = (one_block(m.dq2[i]) * HEAD_DIM ** (-0.5)).astype(BF16)
        reduce_mid(DKV3, l)
        reduce_mid(GU, l)
        reduce_turn(GD, l)
        for a in range(2):
            for j in (2 * a, 2 * a + 1):
                m.dqkv[j * s.qc : (j + 1) * s.qc, s.dc :] = reduce_end(DKV0 + j, l).astype(BF16)
            back = dot_nt(m.dqkv[span(a), :], m.wqkv[l].reshape(s.d, 3 * s.dc))
            if l:
                scatter(a, back, (DX, l, a))
            else:
                part_free(a)
                m.part[a] = back.astype(BF16)
                mine = m.part[a, rows(c, s.t), :].astype(F32) + m.carry[a]
                m.part[a, rows(c, s.t), :] = mine.astype(BF16)
                each_col(lambda cc: remote(m.part.at[a, :, rows(cc, s.dc)], m.got_in.at[a, c], (DX, 0, a), r, cc).start())
                m.got_in[a, c] = m.part[a, :, rows(c, s.dc)]
        if l + 1 < L:
            sent_half(GQ, l + 1)
        if l == 0:
            wait(m.recv, (VEC, 0, 0), m.vec_in.at[pl.ds(0, few)])
            total = m.vec_in[0]
            for i in range(1, s.nc):
                total = total + m.vec_in[i]
            for i in range(L):
                to = i * 2 * VEC_ROWS + VEC_ROWS
                m.own[to : to + VEC_ROWS, :] = total[i * VEC_ROWS : (i + 1) * VEC_ROWS]
            m.own_in[r] = m.own[...]
            each_row(lambda rr: remote(m.own, m.own_in.at[r], (OWN, 0, 0), rr, c).start())
        m.gqkv[...] = dot_tn(m.xf[l].reshape(s.tok, s.d), m.dqkv[...]).astype(BF16).reshape(m.gqkv.shape)
        reduce_start(GQ, l)
        sums = jnp.sum(m.dqkv[...].astype(F32), axis=0, keepdims=True)
        late, to = (m.own, own + 4) if l else (m.late, 0)
        late[to : to + 1, :] = sums[:, : s.dc]
        late[to + 1 : to + 2, :] = sums[:, 2 * s.dc :]
        reduce_turn(GP, l)
        if l == 0:
            reduce_turn(GU, l)
            swap_back(l, GD, reduce_end(GD, l))

    m.late_in[r] = m.late[...]
    each_row(lambda rr: remote(m.late, m.late_in.at[r], (OWN, 0, 1), rr, c).start())
    reduce_mid(GQ, 0)
    wait(m.recv, (ACT, 0, 0), m.act_in.at[:, pl.ds(0, few * s.t)])
    m.o_act[...] = m.act_in[...]
    swap_back(0, GP, reduce_end(GP, 0))
    m.o_up[0] = reduce_end(GU, 0)
    reduce_turn(GQ, 0)
    swap_end(0, GD, m.o_down)
    for a in range(2):
        wait(m.recv, (DX, 0, a), m.got_in.at[a, pl.ds(0, few)])
        total = m.got_in[a, 0].astype(F32)
        for i in range(1, s.nc):
            total = total + m.got_in[a, i].astype(F32)
        m.o_in[a] = total
    wait(m.recv, (OWN, 0, 0), m.own_in.at[pl.ds(0, s.nr - 1)])
    total = m.own_in[0]
    for i in range(1, s.nr):
        total = total + m.own_in[i]
    m.o_vec[...] = total
    wait(m.recv, (OWN, 0, 1), m.late_in.at[pl.ds(0, s.nr - 1)])
    total = m.late_in[0]
    for i in range(1, s.nr):
        total = total + m.late_in[i]
    m.o_vec[4:6, :] = total[:2]
    total = reduce_end(GQ, 0)
    for which, out in enumerate((m.o_q, m.o_k, m.o_v)):
        out[0] = total[:, which * s.dc : (which + 1) * s.dc]
    swap_end(0, GP, m.o_proj)

    for phase, ref in unwaited:
        wait(m.send, phase, ref)
    for a in range(2):
        wait(m.send, (X_IN, 0, a), m.xf.at[0, a, :, pl.ds(0, few * s.dc)])
    wait(m.send, (PVEC, 0, 0), m.pv.at[:, pl.ds(0, few * s.dc)])
    wait(m.send, (COTAN, 0, 0), m.cot.at[:, :, pl.ds(0, few * s.dc)])
    wait(m.send, (ACT, 0, 0), m.act_in.at[:, pl.ds(0, few * s.t)])
    for a in range(2):
        wait(m.send, (DX, 0, a), m.got_in.at[a, pl.ds(0, few)])
    wait(m.send, (VEC, 0, 0), m.vec_in.at[pl.ds(0, few)])
    wait(m.send, (OWN, 0, 0), m.own_in.at[pl.ds(0, s.nr - 1)])
    wait(m.send, (OWN, 0, 1), m.late_in.at[pl.ds(0, s.nr - 1)])

    @pl.when(jnp.logical_not(at_home))
    def _():
        wait(m.send, (WPT, 0, 0), m.wp_own)
        wait(m.send, (WDT, 0, 0), m.wd_own)
        for l in range(L):
            wait(m.send, (GPT, l, 0), m.gproj_fin.at[l])
            wait(m.send, (GDT, l, 0), m.gdown_fin.at[l])
    for l in range(L):
        for name in (WQ, WP, WU, WD, *KV):
            sent_gather(name, l)
        for name in (GQ, GP, GU, GD, *DKV):
            sent_pieces(name, l)
    for name in (GQ, GP, GU, GD, *DKV):
        sent_half(name, 0)


def body(s, layer_input, query_weight, key_weight, value_weight, proj_weight, up_weight, down_weight, query_shift,
         value_shift, proj_shift, up_shift, down_shift, first_gain, first_shift, second_gain, second_shift, segment_ids,
         cotangent):
    L = LAYERS
    places = jnp.tile(segment_ids[: s.tok].reshape(4, s.qc), (1, LANES // s.qc))
    shapes = scratch_of(s)
    halves = (2, s.half, s.dc)
    square = jax.ShapeDtypeStruct((L, s.dr, s.dc), F32)
    out_shape = (
        jax.ShapeDtypeStruct((2, s.half, s.dc), BF16),
        jax.ShapeDtypeStruct((2, s.half, s.dc), F32),
        square, square, square, square,
        jax.ShapeDtypeStruct((L, s.dr, s.fc), F32),
        jax.ShapeDtypeStruct((L, s.fr, s.dc), F32),
        jax.ShapeDtypeStruct((L * 2 * VEC_ROWS, s.dc), F32),
    )
    vmem = pl.BlockSpec(memory_space=pltpu.VMEM)
    results = pl.pallas_call(
        functools.partial(kernel, s),
        out_shape=out_shape,
        in_specs=[vmem] * len(INPUTS),
        out_specs=[vmem] * len(OUTPUTS),
        scratch_shapes=[pltpu.VMEM(shape, dtype) for shape, dtype in shapes.values()]
        + [pltpu.SemaphoreType.DMA((len(KEYS),))] * 2,
        compiler_params=pltpu.CompilerParams(
            collective_id=0, has_side_effects=True, vmem_limit_bytes=60 * 2**20),
        name="encoder",
    )(layer_input.reshape(halves), cotangent.reshape(halves), query_weight, key_weight, value_weight, proj_weight, up_weight,
      down_weight, query_shift, value_shift, proj_shift, up_shift, down_shift, first_gain, first_shift, second_gain,
      second_shift, places)
    narrow, wide = jax.ShapeDtypeStruct((L, s.dc), F32), jax.ShapeDtypeStruct((L, s.fc), F32)
    o_act, o_in, *others = pl.pallas_call(
        functools.partial(hand_out, s),
        out_shape=out_shape[:-1] + (narrow,) * 3 + (wide,) + (narrow,) * 5,
        in_specs=[vmem] * len(OUTPUTS),
        out_specs=[vmem] * 17,
        name="results",
    )(*results)
    return (o_act.reshape(s.tok, s.dc), o_in.reshape(s.tok, s.dc), *others)


def hand_out(s, *refs):
    count = len(OUTPUTS)
    arrays, packed, outs = refs[: count - 1], refs[count - 1], refs[count:]
    for array, out in zip(arrays, outs):
        out[...] = array[...]
    qs, vs, ps, us, ds, fg, fs, sg, ss = outs[count - 1 :]
    for l in range(LAYERS):
        own = l * 2 * VEC_ROWS
        rows = [(qs, 4), (vs, 5)]
        rows += [(ref, VEC_ROWS + which) for ref, which in
                 ((ps, PROJ_B), (ds, DOWN_B), (fg, GAIN1), (fs, SHIFT1), (sg, GAIN2), (ss, SHIFT2))]
        for ref, at in rows:
            ref[l : l + 1, :] = packed[own + at : own + at + 1, :]
        for i in range(s.fc // LANES):
            us[l : l + 1, i * LANES : (i + 1) * LANES] = packed[own + i : own + i + 1, :]


def build(mesh, tok, d, ff):
    s = Sizes(mesh.shape["row"], mesh.shape["col"], tok, d, ff)
    return jax.shard_map(
        functools.partial(body, s),
        mesh=mesh,
        in_specs=(P("row", "col"),) + (P(None, "row", "col"),) * 6 + (P(None, "col"),) * 9 + (P(), P("row", "col")),
        out_specs=(P("row", "col"),) * 2 + (P(None, "row", "col"),) * 6 + (P(None, "col"),) * 9,
        check_vma=False,
    )


def solution(mesh):
    return build(mesh, 256, 1024, 4096)
```
